32 devices in a mesh: dp: 8 (over y, x, core), inner: 4 (over z).
Axes of the slice: x: 2, y: 2, z: 4, core: 2. Of those that a mesh axis runs over, the one named last changes fastest.
Arguments:
- frames_in: bfloat16 [32, 1024, 1024], P(('dp', 'inner')), may hold values from -6 to 6
- lengths: int32 [32], P(('dp', 'inner')), may hold values from 1 to 1024, 24576 in all
- first_gain: float32 [1024], replicated, may hold values from 0.1 to 1.9
- first_shift: float32 [1024], replicated, may hold values from -3 to 3
- attend_weight: bfloat16 [1024, 3072], P('dp', 'inner'), may hold values from -0.1875 to 0.1875
- attend_bias: float32 [2, 1024], replicated, may hold values from -3 to 3
- output_weight: bfloat16 [1024, 1024], P('dp', 'inner'), may hold values from -3 to 3
- output_bias: float32 [1024], replicated, may hold values from -3 to 3
- second_gain: float32 [1024], replicated, may hold values from 0.1 to 1.9
- second_shift: float32 [1024], replicated, may hold values from -3 to 3
- up_weight: bfloat16 [1024, 4096], P('dp', 'inner'), may hold values from -0.1875 to 0.1875
- up_bias: float32 [4096], replicated, may hold values from -3 to 3
- down_weight: bfloat16 [4096, 1024], P('dp', 'inner'), may hold values from -0.125 to 0.125
- down_bias: float32 [1024], replicated, may hold values from -3 to 3
- cotangent: bfloat16 [32, 1024, 1024], P(('dp', 'inner')), may hold values from -6 to 6
Outputs:
- frames_out: bfloat16 [32, 1024, 1024], P(('dp', 'inner'))
- gradient_frames: bfloat16 [32, 1024, 1024], P(('dp', 'inner'))
- gradient_first_gain: float32 [1024], replicated
- gradient_first_shift: float32 [1024], replicated
- gradient_attend_weight: float32 [1024, 3072], P('dp', 'inner')
- gradient_attend_bias: float32 [2, 1024], replicated
- gradient_output_weight: float32 [1024, 1024], P('dp', 'inner')
- gradient_output_bias: float32 [1024], replicated
- gradient_second_gain: float32 [1024], replicated
- gradient_second_shift: float32 [1024], replicated
- gradient_up_weight: float32 [1024, 4096], P('dp', 'inner')
- gradient_up_bias: float32 [4096], replicated
- gradient_down_weight: float32 [4096, 1024], P('dp', 'inner')
- gradient_down_bias: float32 [1024], replicated
The draws below stay inside these ranges and needn't reach their ends.
Inputs may be any that keep to these rules, and one draw needn't show every extreme that they name: The longest utterance fills its slot of 1024 frames exactly, and the lengths fill three quarters of all slots.
All inputs are finite; a program needn't handle non-finite values. No bound on the sum of `lengths` on one device may be relied on, other than what follows from the above.
Results may differ from the reference program's by a relative error of at most 0.012.
Values may be sent and summed in bfloat16 or wider, within the bound.
No kernel may reach another device: no remote copies, remote signals or barrier semaphores. Data moves between devices by JAX's collectives and lax.ppermute only.
A program may use at most 320 MiB of HBM per device.

```python
import math
import jax
import jax.numpy as jnp
import numpy as np
from jax import lax

D = 1024
HEADS = 16
FF = 4096
LEN = 1024
UTTS = 32


def steps_of(key, dims, split, smallest, largest):
    factor_of = 1.0
    for axis_at, shards_of in split:
        steps = jax.random.uniform(jax.random.fold_in(jax.random.fold_in(key, 6), axis_at), (shards_of,), jnp.float32, smallest / len(split), largest / len(split))
        factor_of = factor_of * jnp.repeat(jnp.exp(steps), dims[axis_at] // shards_of).reshape((-1,) + (1,) * (len(dims) - 1 - axis_at))
    return factor_of


def length_profile(amount, total, limit, slope):
    loads = [(1 << 20) // math.isqrt(grade ** slope) + 1 for grade in range(2, amount + 1)]
    rest, counts = total - limit - (amount - 1), [1] * (amount - 1)
    while rest > 0:
        free = [i for i in range(amount - 1) if counts[i] < limit]
        pool, budget = sum([loads[i] for i in free]), rest
        for i in free:
            addition = min(limit - counts[i], max(1, budget * loads[i] // pool), rest)
            counts[i] = counts[i] + addition
            rest = rest - addition
    return np.array([limit] + counts)


def ragged(own_key, count, total, bound, skew):
    if count == 2:
        one = jax.random.randint(own_key, (), max(1, total - bound), min(bound, total - 1) + 1)
        return jnp.stack([one, total - one])
    sizes = jnp.asarray(length_profile(count, total, bound, skew), jnp.int32)
    twos = (count - 1) // 2
    source_of, taker = sizes[1:1 + 2 * twos:2], sizes[2:2 + 2 * twos:2]
    room = jnp.minimum(source_of - 1, bound - taker)
    moved = jax.random.randint(jax.random.fold_in(own_key, 1), (twos,), 0, 1 << 20) % (room + 1)
    sizes = sizes.at[1:1 + 2 * twos:2].set(source_of - moved).at[2:2 + 2 * twos:2].set(taker + moved)
    return sizes[jax.random.permutation(jax.random.fold_in(own_key, 2), count)]


def centred(key, extent, scale, reach, split=(), kind=jnp.bfloat16):
    values = scale * jax.random.normal(key, extent, jnp.float32)
    if split:
        values = values * steps_of(key, extent, split, -0.22, 0.18)
    return jnp.clip(values, -reach, reach).astype(kind)


def setup_inputs(seed: int = 0) -> dict:
    arg_keys = jax.random.split(jax.random.key(seed), 16)
    frames_in = centred(arg_keys[0], (UTTS, LEN, D), 1.0, 6.0, ((0, 32),))
    lengths = ragged(arg_keys[1], UTTS, UTTS * LEN * 3 // 4, LEN, 1).astype(jnp.int32)
    first_gain = jnp.clip(1.0 + 0.18 * jax.random.normal(arg_keys[2], (D,), jnp.float32), 0.1, 1.9)
    first_shift = centred(arg_keys[3], (D,), 0.5, 3.0, (), jnp.float32)
    attend_weight = centred(arg_keys[4], (D, 3 * D), D ** -0.5, 0.1875, ((0, 8), (1, 4)))
    attend_bias = centred(arg_keys[5], (2, D), 0.5, 3.0, (), jnp.float32)
    output_weight = centred(arg_keys[6], (D, D), (max(1, 4 * D // LEN)) ** -0.5, 3.0, ((0, 8), (1, 4)))
    output_bias = centred(arg_keys[7], (D,), 0.5, 3.0, (), jnp.float32)
    second_gain = jnp.clip(1.0 + 0.18 * jax.random.normal(arg_keys[8], (D,), jnp.float32), 0.1, 1.9)
    second_shift = centred(arg_keys[9], (D,), 0.5, 3.0, (), jnp.float32)
    up_weight = centred(arg_keys[10], (D, FF), D ** -0.5, 0.1875, ((0, 8), (1, 4)))
    up_bias = centred(arg_keys[11], (FF,), 0.5, 3.0, (), jnp.float32)
    down_weight = centred(arg_keys[12], (FF, D), (FF // 2) ** -0.5, 0.125, ((0, 8), (1, 4)))
    down_bias = centred(arg_keys[13], (D,), 0.5, 3.0, (), jnp.float32)
    cotangent = centred(arg_keys[14], (UTTS, LEN, D), 1.0, 6.0, ((0, 32),))
    return dict(frames_in=frames_in, lengths=lengths, first_gain=first_gain, first_shift=first_shift, attend_weight=attend_weight, attend_bias=attend_bias, output_weight=output_weight, output_bias=output_bias, second_gain=second_gain, second_shift=second_shift, up_weight=up_weight, up_bias=up_bias, down_weight=down_weight, down_bias=down_bias, cotangent=cotangent)


@jax.custom_vjp
def low(v):
    return lax.optimization_barrier(v.astype(jnp.bfloat16)).astype(jnp.float32)

@jax.custom_vjp
def low_back(v):
    return v

def low_keep(v):
    return (low(v), None)

def low_pass(kept, grad):
    return (grad,)

def back_keep(v):
    return (v, None)

def back_low(kept, grad):
    return (low(grad),)
low.defvjp(low_keep, low_pass)
low_back.defvjp(back_keep, back_low)
highest = lax.Precision.HIGHEST

def layer_norm(tokens, norm_gain, norm_shift):
    center = tokens - lax.optimization_barrier(jnp.mean(tokens, axis=-1, keepdims=True))
    spread = lax.optimization_barrier(jnp.mean(center * center, axis=-1, keepdims=True))
    return center * lax.rsqrt(spread + 1e-05) * norm_gain + norm_shift

def attend(queries, key_rows, value_rows, length):
    frame_count = queries.shape[0]
    block_rows = min(512, frame_count)
    head_dim = queries.shape[1] // HEADS
    scaling = head_dim ** (-0.5)
    key_heads = key_rows.reshape(frame_count, HEADS, head_dim)
    value_heads = value_rows.reshape(frame_count, HEADS, head_dim)
    key_place = jnp.arange(frame_count, dtype=jnp.int32)

    def one_block(first_row):
        query_block = lax.dynamic_slice_in_dim(queries, first_row, block_rows, 0).reshape(block_rows, HEADS, head_dim)
        scores = jnp.einsum('qhd,khd->hqk', query_block, key_heads, precision=highest) * scaling
        scores = low_back(scores)
        query_place = first_row + jnp.arange(block_rows, dtype=jnp.int32)
        allowed = (key_place[None, :] <= query_place[:, None]) & (key_place[None, :] < length)
        scores = jnp.where(allowed[None], scores, -1e+30)
        highest_score = lax.optimization_barrier(jnp.max(scores, axis=-1, keepdims=True))
        weights = jnp.exp(scores - highest_score)
        chances = low(weights / lax.optimization_barrier(jnp.sum(weights, axis=-1, keepdims=True)))
        mixture = jnp.einsum('hqk,khd->qhd', chances, value_heads, precision=highest)
        return mixture.reshape(block_rows, HEADS * head_dim)
    starts = jnp.arange(frame_count // block_rows, dtype=jnp.int32) * block_rows
    blocks = lax.map(jax.checkpoint(one_block), starts)
    return blocks.reshape(frame_count, HEADS * head_dim)

def forward(tokens, length, params):
    first_gain, first_shift, attend_weight, attend_bias, output_weight, output_bias, second_gain, second_shift, up_weight, up_bias, down_weight, down_bias = params
    model_width = tokens.shape[1]
    normed = low(layer_norm(tokens, first_gain, first_shift))
    bias_row = jnp.concatenate([attend_bias[0], jnp.zeros_like(attend_bias[0]), attend_bias[1]])
    project = low(low_back(jnp.dot(normed, attend_weight, precision=highest) + bias_row))
    mixture = attend(project[:, :model_width], project[:, model_width:2 * model_width], project[:, 2 * model_width:], length)
    mixture = low(low_back(mixture))
    branch = low_back(jnp.dot(mixture, output_weight, precision=highest) + output_bias)
    middle = tokens + branch
    normed_two = low(layer_norm(middle, second_gain, second_shift))
    hidden = low_back(jnp.dot(normed_two, up_weight, precision=highest) + up_bias)
    active = low(jax.nn.gelu(hidden, approximate=False))
    result = low_back(jnp.dot(active, down_weight, precision=highest) + down_bias)
    return middle + result

def reference(frames_in, lengths, first_gain, first_shift, attend_weight, attend_bias, output_weight, output_bias, second_gain, second_shift, up_weight, up_bias, down_weight, down_bias, cotangent):
    params = tuple((member.astype(jnp.float32) for member in (first_gain, first_shift, attend_weight, attend_bias, output_weight, output_bias, second_gain, second_shift, up_weight, up_bias, down_weight, down_bias)))
    tokens_all = frames_in.astype(jnp.float32)
    upstream_all = cotangent.astype(jnp.float32)

    def one_utterance(totals, current):
        tokens, length, upstream = current
        live = jnp.arange(tokens.shape[0], dtype=jnp.int32) < length
        upstream = jnp.where(live[:, None], upstream, jnp.float32(0.0))
        result, pullback = jax.vjp(lambda row_data, weights: forward(row_data, length, weights), tokens, params)
        grad_tokens, grad_params = pullback(upstream)
        totals = jax.tree.map(jnp.add, totals, grad_params)
        return (totals, (result.astype(jnp.bfloat16), grad_tokens.astype(jnp.bfloat16)))
    zeros = jax.tree.map(jnp.zeros_like, params)
    totals, (frames_out, gradient_frames) = lax.scan(one_utterance, zeros, (tokens_all, lengths, upstream_all))
    return (frames_out, gradient_frames, totals[0], totals[1], totals[2], totals[3], totals[4], totals[5], totals[6], totals[7], totals[8], totals[9], totals[10], totals[11])
```

```python
import functools

import jax
import jax.numpy as jnp
from jax import lax
from jax.experimental import pallas as pl
from jax.experimental.pallas import tpu as pltpu
from jax.sharding import PartitionSpec as P

HEADS = 16
HEAD = 64
TILE = 1024
ROWS = 256
LOG2E = 1.4426950408889634
MASKED = -1e30
SCALE = HEAD ** (-0.5)
BF = jnp.bfloat16
F32 = jnp.float32
LIMIT = 60 * 2**20


def dot(left, right, on_left, on_right):
    return lax.dot_general(
        left, right, (((on_left,), (on_right,)), ((), ())), preferred_element_type=F32
    )


def normalise(values):
    center = values - jnp.mean(values, axis=-1, keepdims=True)
    spread = jnp.mean(center * center, axis=-1, keepdims=True)
    scale = lax.rsqrt(spread + 1e-05)
    return center * scale, scale


def params(name_limit=LIMIT):
    return pltpu.CompilerParams(vmem_limit_bytes=name_limit)


def estimate(flops, moved, exps=0):
    return pl.CostEstimate(flops=int(flops), bytes_accessed=int(moved), transcendentals=int(exps))


ANY = pl.BlockSpec(memory_space=pl.ANY)
SMEM = pl.BlockSpec(memory_space=pltpu.SMEM)


def whole(*shape):
    return pl.BlockSpec(shape, lambda *_: (0,) * len(shape))


def vec(size):
    return jax.ShapeDtypeStruct((1, size), F32)


PIECES = 8
SLOTS = 4
T_ROW = 0
T_COL = 8
T_SLOT_IN = 12
T_SLOT_OUT = 16
T_PAIR = 20
T_OUT = 24
T_PLACE = 32
T_CORE = 40
T_SIZE = 48


def make_table(spread):
    if not spread:
        order = list(range(4))
        entries = [0] * T_SIZE
        entries[T_PAIR : T_PAIR + 4] = order
        return jnp.array(entries, jnp.int32)
    row = lax.axis_index("dp").astype(jnp.int32)
    column = lax.axis_index("inner").astype(jnp.int32)
    core = row & 1
    near = jnp.where(core == 0, 2, 4)
    far = 6 - near
    entries = [
        row,
        row ^ near,
        row ^ far,
        row ^ 6,
        row ^ 1,
        row ^ 1 ^ far,
        row ^ 1 ^ near,
        row ^ 7,
    ]
    entries += [(column - slot) & 3 for slot in range(4)]
    entries += [(column - block) & 3 for block in range(4)]
    entries += [(block - column) & 3 for block in range(4)]
    pair = row >> 1
    entries += [pair, pair ^ (near >> 1), pair ^ (far >> 1), pair ^ 3]
    for half in range(2):
        a, b = (far, near) if half == 0 else (near, far)
        own = row ^ half
        entries += [own ^ 6, own ^ a, own ^ b, own]
    for half in range(2):
        first = far if half == 0 else near
        for block in range(4):
            relative = (pair ^ block) << 1
            entries.append(
                jnp.where(
                    relative == 6,
                    0,
                    jnp.where(relative == 0, 3, jnp.where(relative == first, 1, 2)),
                )
            )
    entries += [core]
    entries += [jnp.int32(0)] * (T_SIZE - len(entries))
    return jnp.stack([jnp.asarray(entry, jnp.int32) for entry in entries])


def aligned(index, size):
    return pl.ds(pl.multiple_of(index * size, size), size)


def load_columns(pieces, tab, block, target, sems, width, first=0):
    if len(pieces) == 1:
        copies = [
            pltpu.make_async_copy(pieces[0].at[:, aligned(block, width)], target, sems.at[0])
        ]
        return copies
    slot = tab[T_SLOT_IN + block]
    rows = pieces[0].shape[1]
    return [
        pltpu.make_async_copy(
            pieces[p].at[slot, :, pl.ds(first, width)],
            target.at[aligned(tab[T_ROW + p], rows), :],
            sems.at[p],
        )
        for p in range(PIECES)
    ]


def load_rows(pieces, tab, step, target, sems):
    if len(pieces) == 1:
        return [
            pltpu.make_async_copy(
                pieces[0].at[aligned(tab[T_PAIR + step], TILE), :], target, sems.at[0]
            )
        ]
    rows, width = pieces[0].shape[1:]
    partner = (4, 6, 5, 7)[step]
    copies = []
    for n, p in enumerate((step, partner)):
        half = tab[T_ROW + p] & 1
        for slot in range(SLOTS):
            copies.append(
                pltpu.make_async_copy(
                    pieces[p].at[slot],
                    target.at[aligned(half, rows), aligned(tab[T_COL + slot], width)],
                    sems.at[n * SLOTS + slot],
                )
            )
    return copies


def load_all(pieces, tab, target, sems, width, first=0):
    if len(pieces) == 1:
        return [pltpu.make_async_copy(pieces[0], target, sems.at[0])]
    rows = pieces[0].shape[1]
    return [
        pltpu.make_async_copy(
            pieces[p].at[slot, :, pl.ds(first, width)],
            target.at[aligned(tab[T_ROW + p], rows), aligned(tab[T_COL + slot], width)],
            sems.at[p * SLOTS + slot],
        )
        for p in range(PIECES)
        for slot in range(SLOTS)
    ]


def store_column_block(outs, tab, block, source, sems, width, first=0):
    if len(outs) == 1:
        return [pltpu.make_async_copy(source, outs[0].at[:, aligned(block, width)], sems.at[0])]
    rows = outs[0].shape[2]
    slot = tab[T_SLOT_OUT + block]
    return [
        pltpu.make_async_copy(
            source.at[aligned(tab[T_OUT + half * 4 + place], rows), :],
            outs[half].at[place, slot, :, pl.ds(first, width)],
            sems.at[half * 4 + place],
        )
        for half in range(2)
        for place in range(4)
    ]


def store_row_pair(outs, tab, pair, source, sems):
    if len(outs) == 1:
        return [pltpu.make_async_copy(source, outs[0].at[aligned(pair, TILE), :], sems.at[0])]
    rows, width = outs[0].shape[2:]
    copies = []
    for half in range(2):
        local = tab[T_CORE] ^ half
        for block in range(4):
            copies.append(
                pltpu.make_async_copy(
                    source.at[aligned(local, rows), pl.ds(block * width, width)],
                    outs[half].at[tab[T_PLACE + half * 4 + pair], tab[T_SLOT_OUT + block]],
                    sems.at[half * 4 + block],
                )
            )
    return copies


def start(copies):
    for copy in copies:
        copy.start()


def wait(copies):
    for copy in copies:
        copy.wait()


def gradient_shapes(spread, rows, columns, dp, inner):
    if spread:
        return [jax.ShapeDtypeStruct((4, 4, rows // dp, columns // inner), BF)] * 2
    return [jax.ShapeDtypeStruct((rows, columns), BF)]


def project_kernel(count, tab, frames, gain, shift, bias, *rest):
    pieces = rest[:count]
    normed, project, tokens, weight, sems, token_sem = rest[count:]
    step = pl.program_id(0)
    steps = pl.num_programs(0)
    width = project.shape[0]

    def fetch(block):
        slot = lax.rem(block, 2)
        return load_columns(pieces, tab, block, weight.at[slot], sems.at[slot], width)

    @pl.when(step == 0)
    def _():
        copy = pltpu.make_async_copy(frames, tokens, token_sem)
        copy.start()
        start(fetch(step))
        copy.wait()
        for first in range(0, tokens.shape[0], ROWS):
            rows = pl.ds(first, ROWS)
            unit, _ = normalise(tokens[rows, :].astype(F32))
            normed[rows, :] = (unit * gain[...] + shift[...]).astype(BF)

    @pl.when(step + 1 < steps)
    def _():
        start(fetch(step + 1))

    wait(fetch(step))
    column = jnp.transpose(jnp.broadcast_to(bias[...], (128, width)))[:, :1]
    project[...] = (dot(weight[lax.rem(step, 2)], normed[...], 0, 1) + column).astype(BF)


def project_call(tab, frames, gain, shift, bias, pieces):
    frames_count, model = frames.shape
    width = 3 * model // 4
    return pl.pallas_call(
        functools.partial(project_kernel, len(pieces)),
        grid=(4,),
        in_specs=[SMEM, ANY, whole(1, model), whole(1, model)]
        + [pl.BlockSpec((1, width), lambda i: (0, i))]
        + [ANY] * len(pieces),
        out_specs=[whole(frames_count, model), pl.BlockSpec((width, frames_count), lambda i: (i, 0))],
        out_shape=[
            jax.ShapeDtypeStruct((frames_count, model), BF),
            jax.ShapeDtypeStruct((3 * model, frames_count), BF),
        ],
        scratch_shapes=[
            pltpu.VMEM((frames_count, model), BF),
            pltpu.VMEM((2, model, width), BF),
            pltpu.SemaphoreType.DMA((2, 8)),
            pltpu.SemaphoreType.DMA,
        ],
        compiler_params=params(),
        cost_estimate=estimate(6 * frames_count * model * model, 16e6),
        name="project",
    )(tab, frames, gain, shift, bias, *pieces)


def causal_bias(block):
    key = lax.broadcasted_iota(jnp.int32, (block, block), 0)
    query = lax.broadcasted_iota(jnp.int32, (block, block), 1)
    return jnp.where(key <= query, 0.0, MASKED)


def extend_rows(length, extent):
    first = lax.broadcasted_iota(jnp.int32, (16, extent), 0) == 0
    past = lax.broadcasted_iota(jnp.int32, (16, extent), 1) >= length
    key_rows = jnp.where(first & past, MASKED, 0.0).astype(BF)
    query_rows = jnp.where(first, 1.0, 0.0).astype(BF)
    return key_rows, query_rows


def attention_kernel(
    group, block, lengths, query, key, value, mixture, totals, keys, queries, causal
):
    extent = query.shape[1]

    @pl.when(pl.program_id(0) == 0)
    def _():
        causal[...] = causal_bias(block)

    key_rows, query_rows = extend_rows(lengths[0], extent)
    for head in range(group):
        part = pl.ds(HEAD * head, HEAD)
        keys[head, :HEAD, :] = key[part, :]
        keys[head, HEAD:, :] = key_rows
        queries[head, :HEAD, :] = query[part, :]
        queries[head, HEAD:, :] = query_rows
    for head in range(group):
        part = pl.ds(HEAD * head, HEAD)
        for tile in range(extent // block):
            place = pl.ds(tile * block, block)
            own = queries[head, :, place]
            scores = []
            for other in range(tile + 1):
                score = dot(keys[head, :, pl.ds(other * block, block)], own, 0, 0)
                scores.append(score + causal[...] if other == tile else score)
            highest = scores[0].max(0, keepdims=True)
            for score in scores[1:]:
                highest = jnp.maximum(highest, score.max(0, keepdims=True))
            offset = highest * (SCALE * LOG2E)
            summed = jnp.zeros((1, block), F32)
            total = jnp.zeros((HEAD, block), F32)
            for other, score in enumerate(scores):
                weight = jnp.exp2(score * (SCALE * LOG2E) - offset)
                summed = summed + weight.sum(0, keepdims=True)
                total = total + dot(value[part, pl.ds(other * block, block)], weight.astype(BF), 1, 0)
            mixture[part, place] = (total * (1.0 / summed)).astype(BF)
            totals[0, pl.ds(head, 1), place] = offset + jnp.log2(summed)


def attention_call(lengths, project):
    extent = project.shape[1]
    group, block = 2, min(512, extent)
    size, steps = HEAD * group, HEADS // group

    def part(section):
        return pl.BlockSpec((size, extent), lambda i: (i + section * steps, 0))

    pairs = extent * extent * 5 // 8
    return pl.pallas_call(
        functools.partial(attention_kernel, group, block),
        grid=(steps,),
        in_specs=[SMEM, part(0), part(1), part(2)],
        out_specs=[part(0), pl.BlockSpec((1, group, extent), lambda i: (i, 0, 0))],
        out_shape=[
            jax.ShapeDtypeStruct((HEADS * HEAD, extent), BF),
            jax.ShapeDtypeStruct((steps, group, extent), F32),
        ],
        scratch_shapes=[
            pltpu.VMEM((group, HEAD + 16, extent), BF),
            pltpu.VMEM((group, HEAD + 16, extent), BF),
            pltpu.VMEM((block, block), F32),
        ],
        compiler_params=params(),
        cost_estimate=estimate(16 * HEADS * pairs * HEAD, 8e6, HEADS * pairs),
        name="attention",
    )(lengths, project, project, project)


def gelu_parts(hidden):
    chance = 0.5 + 0.5 * lax.erf(hidden * 0.7071067811865476)
    density = jnp.exp2(hidden * hidden * (-0.5 * LOG2E)) * 0.3989422804014327
    return hidden * chance, chance + hidden * density


def up_kernel(counts, tab, lengths, mixture, frames, cotangent, *rest):
    count_out, count_up, count_grad = counts
    out_bias, gain, shift, up_bias = rest[:4]
    out_pieces = rest[4 : 4 + count_out]
    rest = rest[4 + count_out :]
    up_pieces = rest[:count_up]
    rest = rest[count_up:]
    middle, normed, active, slope, down_bias = rest[:5]
    grads = rest[5 : 5 + count_grad]
    (
        mixed,
        out_weight,
        tokens,
        result,
        weight,
        staged,
        sems_in,
        sems_out,
        sems_up,
        sems_grad,
    ) = rest[5 + count_grad :]
    step = pl.program_id(0)
    steps = pl.num_programs(0)
    extent = tokens.shape[0]

    def fetch(block):
        slot = lax.rem(block, 2)
        return load_columns(up_pieces, tab, block, weight.at[slot], sems_up.at[slot], TILE)

    def send(pair):
        slot = lax.rem(pair, 2)
        return store_row_pair(grads, tab, pair, staged.at[slot], sems_grad.at[slot])

    @pl.when(step == 0)
    def _():
        width = mixed.shape[0] // 4
        copies = [pltpu.make_async_copy(mixture, mixed, sems_in.at[0])]
        copies += [pltpu.make_async_copy(frames, tokens, sems_in.at[1])]
        outs = load_all(out_pieces, tab, out_weight, sems_out, width, TILE)
        last = pltpu.make_async_copy(cotangent, result, sems_in.at[2])
        start(copies + outs)
        start(fetch(step))
        last.start()
        wait(copies + outs)
        for first in range(0, extent, ROWS):
            rows = pl.ds(first, ROWS)
            branch = dot(mixed[:, rows], out_weight[...], 0, 0) + out_bias[...]
            total = tokens[rows, :].astype(F32) + branch
            middle[rows, :] = total
            unit, _ = normalise(total)
            normed[rows, :] = (unit * gain[...] + shift[...]).astype(BF)
        last.wait()
        place = lax.broadcasted_iota(jnp.int32, (extent, 1), 0)
        masked = jnp.where(place < lengths[0], result[...].astype(F32), 0.0)
        result[...] = masked.astype(BF)
        down_bias[...] = masked.sum(0, keepdims=True)

    @pl.when(step + 1 < steps)
    def _():
        start(fetch(step + 1))

    wait(fetch(step))
    now = lax.rem(step, 2)
    for first in range(0, extent, ROWS):
        rows = pl.ds(first, ROWS)
        hidden = dot(normed[rows, :], weight[now], 1, 0) + up_bias[...]
        value, grade = gelu_parts(hidden)
        active[rows, :] = value.astype(BF)
        slope[rows, :] = grade.astype(BF)

    @pl.when(step >= 2)
    def _():
        wait(send(step - 2))

    staged[now] = dot(active[...], result[...], 0, 0).astype(BF)
    start(send(step))

    @pl.when(step == steps - 1)
    def _():
        wait(send(step - 1))
        wait(send(step))


def up_call(tab, lengths, mixture, frames, cotangent, vectors, out_pieces, up_pieces, spread, sizes):
    model, extent = mixture.shape
    hidden = 4 * model
    grads = gradient_shapes(spread, hidden, model, *sizes)
    steps = hidden // TILE
    return pl.pallas_call(
        functools.partial(up_kernel, (len(out_pieces), len(up_pieces), len(grads))),
        grid=(steps,),
        in_specs=[SMEM, SMEM, ANY, ANY, ANY]
        + [whole(1, model)] * 3
        + [pl.BlockSpec((1, TILE), lambda i: (0, i))]
        + [ANY] * (len(out_pieces) + len(up_pieces)),
        out_specs=[
            whole(extent, model),
            whole(extent, model),
            pl.BlockSpec((extent, TILE), lambda i: (0, i)),
            pl.BlockSpec((extent, TILE), lambda i: (0, i)),
            whole(1, model),
        ]
        + [ANY] * len(grads),
        out_shape=[
            jax.ShapeDtypeStruct((extent, model), F32),
            jax.ShapeDtypeStruct((extent, model), BF),
            jax.ShapeDtypeStruct((extent, hidden), BF),
            jax.ShapeDtypeStruct((extent, hidden), BF),
            vec(model),
        ]
        + grads,
        scratch_shapes=[
            pltpu.VMEM((model, extent), BF),
            pltpu.VMEM((model, model), BF),
            pltpu.VMEM((extent, model), BF),
            pltpu.VMEM((extent, model), BF),
            pltpu.VMEM((2, model, TILE), BF),
            pltpu.VMEM((2, TILE, model), BF),
            pltpu.SemaphoreType.DMA((3,)),
            pltpu.SemaphoreType.DMA((32,)),
            pltpu.SemaphoreType.DMA((2, 8)),
            pltpu.SemaphoreType.DMA((2, 8)),
        ],
        compiler_params=params(),
        cost_estimate=estimate(18 * extent * model * model, 50e6, extent * hidden),
        name="up",
    )(tab, lengths, mixture, frames, cotangent, *vectors, *out_pieces, *up_pieces)


def back_kernel(counts, tab, lengths, mixture, middle, normed, cotangent, slope, *rest):
    count_out, count_up, count_down, count_grad = counts
    gain = rest[0]
    rest = rest[1:]
    out_pieces, rest = rest[:count_out], rest[count_out:]
    up_pieces, rest = rest[:count_up], rest[count_up:]
    down_pieces, rest = rest[:count_down], rest[count_down:]
    d_middle, d_mixture, up_bias, gain_grad, shift_grad, out_bias = rest[:6]
    rest = rest[6:]
    grads, rest = rest[:count_grad], rest[count_grad:]
    (
        mixed,
        out_weight,
        total,
        unit_rows,
        result,
        down,
        up,
        d_hidden,
        d_normed,
        staged,
        sems_in,
        sems_out,
        sems_down,
        sems_up,
        sems_grad,
    ) = rest
    spread = len(grads[0].shape) == 4
    if spread:
        up_grads = out_grads = grads
    else:
        up_grads, out_grads = grads[:1], grads[1:]
    step = pl.program_id(0)
    steps = pl.num_programs(0)
    extent, model = result.shape
    width = model // 4

    def fetch(index):
        slot = index % 2
        copies = load_rows(down_pieces, tab, index, down.at[slot], sems_down.at[slot])
        block = tab[T_PAIR + index]
        copies += load_columns(up_pieces, tab, block, up.at[slot], sems_up.at[slot], TILE)
        return copies

    def send(index):
        slot = index % 2
        block = tab[T_PAIR + index]
        return store_column_block(
            up_grads, tab, block, staged.at[slot], sems_grad.at[slot], TILE
        )

    def send_out(block):
        return store_column_block(
            out_grads,
            tab,
            block,
            staged.at[0, :, pl.ds(block * width, width)],
            sems_out.at[pl.ds(block * 8, 8)],
            width,
            TILE if spread else 0,
        )

    def early(n):
        pair = ((cotangent, result), (normed, unit_rows))[n]
        return pltpu.make_async_copy(*pair, sems_in.at[n])

    def late():
        return [
            pltpu.make_async_copy(middle, total, sems_in.at[2]),
            pltpu.make_async_copy(mixture, mixed, sems_in.at[3]),
        ] + load_all(out_pieces, tab, out_weight, sems_out, width, TILE)

    def body(index):
        slot = index % 2
        if index == 0:
            early(0).start()
            start(fetch(0))
            early(1).start()
            early(0).wait()
            place = lax.broadcasted_iota(jnp.int32, (extent, 1), 0)
            masked = jnp.where(place < lengths[0], result[...].astype(F32), 0.0)
            result[...] = masked.astype(BF)
        if index == 2:
            start(late())
        if index + 1 < 4:
            start(fetch(index + 1))
        wait(fetch(index))
        sums = jnp.zeros((1, TILE), F32)
        for first in range(0, extent, ROWS):
            rows = pl.ds(first, ROWS)
            d_active = dot(result[rows, :], down[slot], 1, 1)
            piece = (d_active * slope[rows, :].astype(F32)).astype(BF)
            d_hidden[rows, :] = piece
            sums = sums + piece.astype(F32).sum(0, keepdims=True)
        up_bias[...] = sums
        if index == 0:
            early(1).wait()
        if index >= 2:
            wait(send(index - 2))
        staged[slot] = dot(unit_rows[...], d_hidden[...], 0, 0).astype(BF)
        start(send(index))
        part = dot(d_hidden[...], up[slot], 1, 1)
        if index == 0:
            d_normed[...] = part
        else:
            d_normed[...] += part

    for index in range(4):
        pl.when(step == index)(functools.partial(body, index))

    @pl.when(step == steps - 1)
    def _():
        wait(late())
        gains = jnp.zeros((1, model), F32)
        shifts = jnp.zeros((1, model), F32)
        biases = jnp.zeros((1, model), F32)
        for first in range(0, extent, ROWS):
            rows = pl.ds(first, ROWS)
            unit, scale = normalise(total[rows, :])
            grade = d_normed[rows, :]
            gains = gains + (grade * unit).sum(0, keepdims=True)
            shifts = shifts + grade.sum(0, keepdims=True)
            grade = grade * gain[...]
            level = jnp.mean(grade, axis=-1, keepdims=True)
            tilt = jnp.mean(grade * unit, axis=-1, keepdims=True)
            d_total = result[rows, :].astype(F32) + scale * (grade - level - unit * tilt)
            d_middle[rows, :] = d_total
            branch = d_total.astype(BF)
            unit_rows[rows, :] = branch
            biases = biases + branch.astype(F32).sum(0, keepdims=True)
        gain_grad[...] = gains
        shift_grad[...] = shifts
        out_bias[...] = biases
        wait(send(2))
        staged[0] = dot(mixed[...], unit_rows[...], 1, 0).astype(BF)
        for block in range(4):
            start(send_out(block))
        d_mixture[...] = dot(out_weight[...], unit_rows[...], 1, 1).astype(BF)
        wait(send(3))
        for block in range(4):
            wait(send_out(block))


def back_call(
    tab, lengths, mixture, middle, normed, cotangent, slope, gain, pieces, spread, sizes
):
    out_pieces, up_pieces, down_pieces = pieces
    model, extent = mixture.shape
    hidden = slope.shape[1]
    if spread:
        grads = gradient_shapes(spread, model, hidden + model, *sizes)
    else:
        grads = gradient_shapes(spread, model, hidden, *sizes)
        grads += gradient_shapes(spread, model, model, *sizes)
    steps = hidden // TILE
    grid = pltpu.PrefetchScalarGridSpec(
        num_scalar_prefetch=1,
        grid=(steps,),
        in_specs=[SMEM, ANY, ANY, ANY, ANY]
        + [pl.BlockSpec((extent, TILE), lambda i, tab: (0, tab[T_PAIR + i]))]
        + [whole(1, model)]
        + [ANY] * (len(out_pieces) + len(up_pieces) + len(down_pieces)),
        out_specs=[
            whole(extent, model),
            whole(model, extent),
            pl.BlockSpec((1, TILE), lambda i, tab: (0, tab[T_PAIR + i])),
            whole(1, model),
            whole(1, model),
            whole(1, model),
        ]
        + [ANY] * len(grads),
        scratch_shapes=[
            pltpu.VMEM((model, extent), BF),
            pltpu.VMEM((model, model), BF),
            pltpu.VMEM((extent, model), F32),
            pltpu.VMEM((extent, model), BF),
            pltpu.VMEM((extent, model), BF),
            pltpu.VMEM((2, TILE, model), BF),
            pltpu.VMEM((2, model, TILE), BF),
            pltpu.VMEM((extent, TILE), BF),
            pltpu.VMEM((extent, model), F32),
            pltpu.VMEM((2, model, TILE), BF),
            pltpu.SemaphoreType.DMA((4,)),
            pltpu.SemaphoreType.DMA((32,)),
            pltpu.SemaphoreType.DMA((2, 8)),
            pltpu.SemaphoreType.DMA((2, 8)),
            pltpu.SemaphoreType.DMA((2, 8)),
        ],
    )
    return pl.pallas_call(
        functools.partial(
            back_kernel, (len(out_pieces), len(up_pieces), len(down_pieces), len(grads))
        ),
        grid_spec=grid,
        out_shape=[
            jax.ShapeDtypeStruct((extent, model), F32),
            jax.ShapeDtypeStruct((model, extent), BF),
            vec(hidden),
            vec(model),
            vec(model),
            vec(model),
        ]
        + grads,
        compiler_params=params(),
        cost_estimate=estimate(28 * extent * model * model, 60e6),
        name="back",
    )(
        tab,
        lengths,
        mixture,
        middle,
        normed,
        cotangent,
        slope,
        gain,
        *out_pieces,
        *up_pieces,
        *down_pieces,
    )


def attention_back_kernel(
    group,
    block,
    lengths,
    query,
    key,
    value,
    mixture,
    d_mixture,
    totals,
    d_project,
    keys,
    queries,
    causal,
    d_keys,
    d_values,
):
    extent = query.shape[1]

    @pl.when(pl.program_id(0) == 0)
    def _():
        causal[...] = causal_bias(block)

    key_rows, query_rows = extend_rows(lengths[0], extent)
    for head in range(group):
        part = pl.ds(HEAD * head, HEAD)
        keys[head, :HEAD, :] = key[part, :]
        keys[head, HEAD:, :] = key_rows
        queries[head, :HEAD, :] = query[part, :]
        queries[head, HEAD:, :] = query_rows
    for head in range(group):
        part = pl.ds(HEAD * head, HEAD)
        for tile in range(extent // block):
            place = pl.ds(tile * block, block)
            own = queries[head, :, place]
            grade = d_mixture[part, place]
            center = (grade.astype(F32) * mixture[part, place].astype(F32)).sum(0, keepdims=True)
            total = totals[0, pl.ds(head, 1), place]
            d_query = jnp.zeros((HEAD, block), F32)
            for other in range(tile + 1):
                span = pl.ds(other * block, block)
                score = dot(keys[head, :, span], own, 0, 0)
                if other == tile:
                    score = score + causal[...]
                weight = jnp.exp2(score * (SCALE * LOG2E) - total)
                d_weight = dot(value[part, span], grade, 0, 0)
                d_score = (weight * (d_weight - center)).astype(BF)
                d_value = dot(grade, weight.astype(BF), 1, 1)
                d_key = dot(query[part, place], d_score, 1, 1)
                d_query = d_query + dot(key[part, span], d_score, 1, 0)
                if other == tile:
                    d_values[:, span] = d_value
                    d_keys[:, span] = d_key
                else:
                    d_values[:, span] += d_value
                    d_keys[:, span] += d_key
            d_project[0, part, place] = (d_query * SCALE).astype(BF)
        d_project[1, part, :] = (d_keys[...] * SCALE).astype(BF)
        d_project[2, part, :] = d_values[...].astype(BF)


def attention_back_call(lengths, project, mixture, d_mixture, totals):
    extent = project.shape[1]
    group, block = 2, min(512, extent)
    size, steps = HEAD * group, HEADS // group

    def part(section):
        return pl.BlockSpec((size, extent), lambda i: (i + section * steps, 0))

    pairs = extent * extent * 5 // 8
    return pl.pallas_call(
        functools.partial(attention_back_kernel, group, block),
        grid=(steps,),
        in_specs=[SMEM, part(0), part(1), part(2), part(0), part(0)]
        + [pl.BlockSpec((1, group, extent), lambda i: (i, 0, 0))],
        out_specs=pl.BlockSpec((3, size, extent), lambda i: (0, i, 0)),
        out_shape=jax.ShapeDtypeStruct((3, HEADS * HEAD, extent), BF),
        scratch_shapes=[
            pltpu.VMEM((group, HEAD + 16, extent), BF),
            pltpu.VMEM((group, HEAD + 16, extent), BF),
            pltpu.VMEM((block, block), F32),
            pltpu.VMEM((HEAD, extent), F32),
            pltpu.VMEM((HEAD, extent), F32),
        ],
        compiler_params=params(),
        cost_estimate=estimate(30 * HEADS * pairs * HEAD, 16e6, HEADS * pairs),
        name="attention_back",
    )(lengths, project, project, project, mixture, d_mixture, totals)


def first_kernel(counts, tab, d_project, normed, frames, d_middle, gain, *rest):
    count_in, count_grad = counts
    pieces, rest = rest[:count_in], rest[count_in:]
    d_frames, bias_grad, gain_grad, shift_grad = rest[:4]
    grads, rest = rest[4 : 4 + count_grad], rest[4 + count_grad :]
    weight, total, staged, d_normed, sems, sem_total, sems_grad = rest
    step = pl.program_id(0)
    steps = pl.num_programs(0)
    extent, model = normed.shape
    width = d_project.shape[0]

    def fetch(block):
        slot = lax.rem(block, 2)
        return load_columns(pieces, tab, block, weight.at[slot], sems.at[slot], width)

    def send(block):
        slot = lax.rem(block, 2)
        return store_column_block(grads, tab, block, staged.at[slot], sems_grad.at[slot], width)

    def late():
        return pltpu.make_async_copy(d_middle, total, sem_total)

    @pl.when(step == 0)
    def _():
        start(fetch(step))
        late().start()

    @pl.when(step + 1 < steps)
    def _():
        start(fetch(step + 1))

    @pl.when(step >= 2)
    def _():
        wait(send(step - 2))

    now = lax.rem(step, 2)
    staged[now] = dot(normed[...], d_project[...], 0, 1).astype(BF)
    start(send(step))
    bias_grad[...] = dot(jnp.ones((8, extent), BF), d_project[...], 1, 1)[:1, :]
    wait(fetch(step))
    part = dot(d_project[...], weight[now], 0, 1)

    @pl.when(step == 0)
    def _():
        d_normed[...] = part

    @pl.when(step > 0)
    def _():
        d_normed[...] += part

    @pl.when(step == steps - 1)
    def _():
        late().wait()
        gains = jnp.zeros((1, model), F32)
        shifts = jnp.zeros((1, model), F32)
        for first in range(0, extent, ROWS):
            rows = pl.ds(first, ROWS)
            unit, scale = normalise(frames[rows, :].astype(F32))
            grade = d_normed[rows, :]
            gains = gains + (grade * unit).sum(0, keepdims=True)
            shifts = shifts + grade.sum(0, keepdims=True)
            grade = grade * gain[...]
            level = jnp.mean(grade, axis=-1, keepdims=True)
            tilt = jnp.mean(grade * unit, axis=-1, keepdims=True)
            d_frames[rows, :] = (total[rows, :] + scale * (grade - level - unit * tilt)).astype(BF)
        gain_grad[...] = gains
        shift_grad[...] = shifts
        wait(send(step - 1))
        wait(send(step))


def first_call(tab, d_project, normed, frames, d_middle, gain, pieces, spread, sizes):
    extent, model = frames.shape
    width = 3 * model // 4
    grads = gradient_shapes(spread, model, 3 * model, *sizes)
    return pl.pallas_call(
        functools.partial(first_kernel, (len(pieces), len(grads))),
        grid=(4,),
        in_specs=[SMEM, pl.BlockSpec((width, extent), lambda i: (i, 0))]
        + [whole(extent, model), whole(extent, model), ANY, whole(1, model)]
        + [ANY] * len(pieces),
        out_specs=[
            whole(extent, model),
            pl.BlockSpec((1, width), lambda i: (0, i)),
            whole(1, model),
            whole(1, model),
        ]
        + [ANY] * len(grads),
        out_shape=[
            jax.ShapeDtypeStruct((extent, model), BF),
            vec(3 * model),
            vec(model),
            vec(model),
        ]
        + grads,
        scratch_shapes=[
            pltpu.VMEM((2, model, width), BF),
            pltpu.VMEM((extent, model), F32),
            pltpu.VMEM((2, model, width), BF),
            pltpu.VMEM((extent, model), F32),
            pltpu.SemaphoreType.DMA((2, 8)),
            pltpu.SemaphoreType.DMA,
            pltpu.SemaphoreType.DMA((2, 8)),
        ],
        compiler_params=params(),
        cost_estimate=estimate(12 * extent * model * model, 32e6),
        name="first",
    )(tab, d_project, normed, frames, d_middle, gain, *pieces)


def down_kernel(count, tab, active, middle, bias, *rest):
    pieces = rest[:count]
    frames_out, weight, total, sems = rest[count:]
    step = pl.program_id(0)
    steps = pl.num_programs(0)

    def fetch(index):
        slot = index % 2
        return load_rows(pieces, tab, index, weight.at[slot], sems.at[slot])

    def body(index):
        if index == 0:
            start(fetch(0))
        if index + 1 < 4:
            start(fetch(index + 1))
        wait(fetch(index))
        part = dot(active[...], weight[index % 2], 1, 0)
        if index == 0:
            total[...] = part
        elif index < 3:
            total[...] += part
        else:
            frames_out[...] = (total[...] + part + (middle[...] + bias[...])).astype(BF)

    for index in range(4):
        pl.when(step == index)(functools.partial(body, index))


def down_call(tab, active, middle, bias, pieces):
    extent, hidden = active.shape
    model = middle.shape[1]
    grid = pltpu.PrefetchScalarGridSpec(
        num_scalar_prefetch=1,
        grid=(hidden // TILE,),
        in_specs=[pl.BlockSpec((extent, TILE), lambda i, tab: (0, tab[T_PAIR + i]))]
        + [whole(extent, model), whole(1, model)]
        + [ANY] * len(pieces),
        out_specs=whole(extent, model),
        scratch_shapes=[
            pltpu.VMEM((2, TILE, model), BF),
            pltpu.VMEM((extent, model), F32),
            pltpu.SemaphoreType.DMA((2, 8)),
        ],
    )
    return pl.pallas_call(
        functools.partial(down_kernel, len(pieces)),
        grid_spec=grid,
        out_shape=jax.ShapeDtypeStruct((extent, model), BF),
        compiler_params=params(),
        cost_estimate=estimate(8 * extent * model * model, 24e6),
        name="down",
    )(tab, active, middle, bias, *pieces)


def gather_plain(weight):
    wide = lax.all_gather(weight, "inner", axis=1, tiled=True)
    return [lax.all_gather(wide, "dp", axis=0, tiled=True)]


def scatter_plain(grads):
    wide = lax.psum_scatter(grads[0], "dp", scatter_dimension=0, tiled=True)
    return lax.psum_scatter(wide, "inner", scatter_dimension=1, tiled=True).astype(F32)


def shards(
    spread,
    sizes,
    frames_in,
    lengths,
    first_gain,
    first_shift,
    attend_weight,
    attend_bias,
    output_weight,
    output_bias,
    second_gain,
    second_shift,
    up_weight,
    up_bias,
    down_weight,
    down_bias,
    cotangent,
):
    _, extent, model = frames_in.shape
    frames = frames_in.reshape(extent, model)
    upstream = cotangent.reshape(extent, model)
    tab = make_table(spread)

    def row(vector):
        return vector.reshape(1, -1)

    attend_pieces = gather_plain(attend_weight)
    out_pieces = gather_plain(output_weight)
    up_pieces = gather_plain(up_weight)
    down_pieces = gather_plain(down_weight)
    bias_row = jnp.concatenate([attend_bias[0], jnp.zeros_like(attend_bias[0]), attend_bias[1]])
    normed, project = project_call(
        tab, frames, row(first_gain), row(first_shift), row(bias_row), attend_pieces
    )
    mixture, totals = attention_call(lengths, project)
    vectors = (row(output_bias), row(second_gain), row(second_shift), row(up_bias))
    middle, normed_two, active, slope, grad_down_bias, *down_grads = up_call(
        tab,
        lengths,
        mixture,
        frames,
        upstream,
        vectors,
        out_pieces,
        up_pieces,
        spread,
        sizes,
    )
    (
        d_middle,
        d_mixture,
        grad_up_bias,
        grad_second_gain,
        grad_second_shift,
        grad_output_bias,
        *back_grads,
    ) = back_call(
        tab,
        lengths,
        mixture,
        middle,
        normed_two,
        upstream,
        slope,
        row(second_gain),
        (out_pieces, up_pieces, down_pieces),
        spread,
        sizes,
    )
    d_project = attention_back_call(lengths, project, mixture, d_mixture, totals)
    d_frames, grad_bias, grad_first_gain, grad_first_shift, *attend_grads = first_call(
        tab,
        d_project.reshape(3 * model, extent),
        normed,
        frames,
        d_middle,
        row(first_gain),
        attend_pieces,
        spread,
        sizes,
    )
    frames_out = down_call(tab, active, middle, row(down_bias), down_pieces)
    down_owned = scatter_plain(down_grads)
    up_owned = scatter_plain(back_grads[:1])
    output_owned = scatter_plain(back_grads[1:])
    attend_owned = scatter_plain(attend_grads)
    small = lax.psum(
        jnp.concatenate(
            [
                grad_first_gain,
                grad_first_shift,
                grad_bias[:, :model],
                grad_bias[:, 2 * model :],
                grad_output_bias,
                grad_second_gain,
                grad_second_shift,
                grad_down_bias,
                grad_up_bias,
            ],
            axis=1,
        ),
        ("dp", "inner"),
    ).reshape(-1)

    def take(first, count=1):
        return small[first * model : (first + count) * model]

    return (
        frames_out.reshape(frames_in.shape),
        d_frames.reshape(frames_in.shape),
        take(0),
        take(1),
        attend_owned,
        take(2, 2).reshape(2, model),
        output_owned,
        take(4),
        take(5),
        take(6),
        up_owned,
        take(8, 4),
        down_owned,
        take(7),
    )


def solution(mesh):
    sizes = (mesh.shape["dp"], mesh.shape["inner"])
    spread = False
    return jax.shard_map(
        functools.partial(shards, spread, sizes),
        mesh=mesh,
        in_specs=(
            P(("dp", "inner"), None, None),
            P(("dp", "inner")),
            P(),
            P(),
            P("dp", "inner"),
            P(),
            P("dp", "inner"),
            P(),
            P(),
            P(),
            P("dp", "inner"),
            P(),
            P("dp", "inner"),
            P(),
            P(("dp", "inner"), None, None),
        ),
        out_specs=(
            P(("dp", "inner"), None, None),
            P(("dp", "inner"), None, None),
            P(),
            P(),
            P("dp", "inner"),
            P(),
            P("dp", "inner"),
            P(),
            P(),
            P(),
            P("dp", "inner"),
            P(),
            P("dp", "inner"),
            P(),
        ),
        check_vma=False,
    )
```

```python
import functools

import jax
import jax.numpy as jnp
from jax import lax
from jax.experimental import pallas as pl
from jax.experimental.pallas import tpu as pltpu
from jax.sharding import PartitionSpec as P

HEADS = 16
HEAD = 64
TILE = 1024
ROWS = 256
LOG2E = 1.4426950408889634
MASKED = -1e30
SCALE = HEAD ** (-0.5)
BF = jnp.bfloat16
F32 = jnp.float32
LIMIT = 60 * 2**20


def dot(left, right, on_left, on_right):
    return lax.dot_general(
        left, right, (((on_left,), (on_right,)), ((), ())), preferred_element_type=F32
    )


def normalise(values):
    center = values - jnp.mean(values, axis=-1, keepdims=True)
    spread = jnp.mean(center * center, axis=-1, keepdims=True)
    scale = lax.rsqrt(spread + 1e-05)
    return center * scale, scale


def params(name_limit=LIMIT):
    return pltpu.CompilerParams(vmem_limit_bytes=name_limit)


def estimate(flops, moved, exps=0):
    return pl.CostEstimate(
        flops=int(8 * flops), bytes_accessed=int(8 * moved), transcendentals=int(8 * exps)
    )


ANY = pl.BlockSpec(memory_space=pl.ANY)
SMEM = pl.BlockSpec(memory_space=pltpu.SMEM)


def whole(*shape):
    return pl.BlockSpec(shape, lambda *_: (0,) * len(shape))


def vec(size):
    return jax.ShapeDtypeStruct((1, size), F32)


PIECES = 8
SLOTS = 4
T_ROW = 0
T_COL = 8
T_SLOT_IN = 12
T_SLOT_OUT = 16
T_PAIR = 20
T_OUT = 24
T_PLACE = 32
T_CORE = 40
T_SIZE = 48


def make_table(spread, relative):
    if not spread:
        order = list(range(4))
        entries = [0] * T_SIZE
        entries[T_PAIR : T_PAIR + 4] = order
        entries[T_COL : T_COL + 4] = order
        return jnp.array(entries, jnp.int32)
    row = lax.axis_index("dp").astype(jnp.int32)
    column = lax.axis_index("inner").astype(jnp.int32)
    core = row & 1
    near = jnp.where(core == 0, 2, 4)
    far = 6 - near
    entries = [
        row,
        row ^ near,
        row ^ far,
        row ^ 6,
        row ^ 1,
        row ^ 1 ^ far,
        row ^ 1 ^ near,
        row ^ 7,
    ]
    if relative:
        entries += [(column - block) & 3 for block in range(4)] * 2
    else:
        entries += [0, 1, 2, 3] * 2
    entries += [(block - column) & 3 for block in range(4)]
    pair = row >> 1
    entries += [pair, pair ^ (near >> 1), pair ^ (far >> 1), pair ^ 3]
    for half in range(2):
        a, b = (far, near) if half == 0 else (near, far)
        own = row ^ half
        entries += [own ^ 6, own ^ a, own ^ b, own]
    for half in range(2):
        first = far if half == 0 else near
        for block in range(4):
            relative = (pair ^ block) << 1
            entries.append(
                jnp.where(
                    relative == 6,
                    0,
                    jnp.where(relative == 0, 3, jnp.where(relative == first, 1, 2)),
                )
            )
    entries += [core]
    entries += [jnp.int32(0)] * (T_SIZE - len(entries))
    return jnp.stack([jnp.asarray(entry, jnp.int32) for entry in entries])


def aligned(index, size):
    return pl.ds(pl.multiple_of(index * size, size), size)


def load_slot(pieces, tab, step, target, sems, width):
    if len(pieces) == 1:
        return load_columns(pieces, tab, tab[T_COL + step], target, sems, width)
    rows = pieces[0].shape[-2]
    copies = []
    for p in range(PIECES):
        source = pieces[p] if step == 0 else pieces[PIECES + p].at[step - 1]
        place = target.at[aligned(tab[T_ROW + p], rows), :]
        copies.append(pltpu.make_async_copy(source, place, sems.at[p]))
    return copies


def load_columns(pieces, tab, block, target, sems, width, first=0):
    if len(pieces) == 1:
        copies = [
            pltpu.make_async_copy(pieces[0].at[:, aligned(block, width)], target, sems.at[0])
        ]
        return copies
    slot = tab[T_SLOT_IN + block]
    rows = pieces[0].shape[1]
    return [
        pltpu.make_async_copy(
            pieces[p].at[slot, :, pl.ds(first, width)],
            target.at[aligned(tab[T_ROW + p], rows), :],
            sems.at[p],
        )
        for p in range(PIECES)
    ]


def load_rows(pieces, tab, step, target, sems):
    if len(pieces) == 1 and len(pieces[0].shape) == 2:
        return [
            pltpu.make_async_copy(
                pieces[0].at[aligned(tab[T_PAIR + step], TILE), :], target, sems.at[0]
            )
        ]
    rows, width = pieces[0].shape[-2:]
    if len(pieces) == 1:
        return [
            pltpu.make_async_copy(
                pieces[0].at[2 * tab[T_PAIR + step] + half, block],
                target.at[pl.ds(half * rows, rows), pl.ds(block * width, width)],
                sems.at[half * SLOTS + block],
            )
            for half in range(2)
            for block in range(4)
        ]
    partner = (4, 6, 5, 7)[step]
    copies = []
    for n, p in enumerate((step, partner)):
        half = tab[T_ROW + p] & 1
        for slot in range(SLOTS):
            copies.append(
                pltpu.make_async_copy(
                    pieces[p].at[slot],
                    target.at[aligned(half, rows), aligned(tab[T_COL + slot], width)],
                    sems.at[n * SLOTS + slot],
                )
            )
    return copies


def load_all(pieces, tab, target, sems, width, first=0):
    if len(pieces) == 1:
        return [pltpu.make_async_copy(pieces[0], target, sems.at[0])]
    rows = pieces[0].shape[1]
    return [
        pltpu.make_async_copy(
            pieces[p].at[slot, :, pl.ds(first, width)],
            target.at[aligned(tab[T_ROW + p], rows), aligned(tab[T_COL + slot], width)],
            sems.at[p * SLOTS + slot],
        )
        for p in range(PIECES)
        for slot in range(SLOTS)
    ]


def store_column_block(outs, tab, block, source, sems, width, first=0):
    if len(outs) == 1:
        return [pltpu.make_async_copy(source, outs[0].at[:, aligned(block, width)], sems.at[0])]
    rows = outs[0].shape[2]
    slot = tab[T_SLOT_OUT + block]
    return [
        pltpu.make_async_copy(
            source.at[aligned(tab[T_OUT + half * 4 + place], rows), :],
            outs[half].at[place, slot, :, pl.ds(first, width)],
            sems.at[half * 4 + place],
        )
        for half in range(2)
        for place in range(4)
    ]


def store_row_pair(outs, tab, pair, source, sems):
    if len(outs) == 1:
        return [pltpu.make_async_copy(source, outs[0].at[aligned(pair, TILE), :], sems.at[0])]
    rows, width = outs[0].shape[2:]
    copies = []
    for half in range(2):
        local = tab[T_CORE] ^ half
        for block in range(4):
            copies.append(
                pltpu.make_async_copy(
                    source.at[aligned(local, rows), pl.ds(block * width, width)],
                    outs[half].at[tab[T_PLACE + half * 4 + pair], tab[T_SLOT_OUT + block]],
                    sems.at[half * 4 + block],
                )
            )
    return copies


def chunks(extent, size, body, init=0):
    for first in range(0, extent, size):
        init = body(pl.ds(first, size), init)
    return init


def start(copies):
    for copy in copies:
        copy.start()


def wait(copies):
    for copy in copies:
        copy.wait()


def gradient_shapes(spread, rows, columns, dp, inner):
    if spread:
        return [jax.ShapeDtypeStruct((4, 4, rows // dp, columns // inner), BF)] * 2
    return [jax.ShapeDtypeStruct((rows, columns), BF)]


def project_kernel(count, tab, frames, gain, shift, bias, *rest):
    pieces = rest[:count]
    normed, project, tokens, weight, sems, token_sem = rest[count:]
    step = pl.program_id(0)
    steps = pl.num_programs(0)
    width = project.shape[0]

    def fetch(index):
        slot = index % 2
        return load_slot(pieces, tab, index, weight.at[slot], sems.at[slot], width)

    @pl.when(step == 0)
    def _():
        copy = pltpu.make_async_copy(frames, tokens, token_sem)
        copy.start()
        start(fetch(0))
        copy.wait()

        def norm(rows, carry):
            unit, _ = normalise(tokens[rows, :].astype(F32))
            normed[rows, :] = (unit * gain[...] + shift[...]).astype(BF)
            return carry

        chunks(tokens.shape[0], ROWS, norm)

    def arrive(index):
        if index + 1 < 4:
            start(fetch(index + 1))
        wait(fetch(index))

    for index in range(4):
        pl.when(step == index)(functools.partial(arrive, index))

    column = jnp.transpose(jnp.broadcast_to(bias[...], (128, width)))[:, :1]
    project[...] = (dot(weight[lax.rem(step, 2)], normed[...], 0, 1) + column).astype(BF)


def project_call(tab, frames, gain, shift, bias, pieces):
    frames_count, model = frames.shape
    width = 3 * model // 4
    grid = pltpu.PrefetchScalarGridSpec(
        num_scalar_prefetch=1,
        grid=(4,),
        in_specs=[ANY, whole(1, model), whole(1, model)]
        + [pl.BlockSpec((1, width), lambda i, tab: (0, tab[T_COL + i]))]
        + [ANY] * len(pieces),
        out_specs=[
            whole(frames_count, model),
            pl.BlockSpec((width, frames_count), lambda i, tab: (tab[T_COL + i], 0)),
        ],
        scratch_shapes=[
            pltpu.VMEM((frames_count, model), BF),
            pltpu.VMEM((2, model, width), BF),
            pltpu.SemaphoreType.DMA((2, 8)),
            pltpu.SemaphoreType.DMA,
        ],
    )
    return pl.pallas_call(
        functools.partial(project_kernel, len(pieces)),
        grid_spec=grid,
        out_shape=[
            jax.ShapeDtypeStruct((frames_count, model), BF),
            jax.ShapeDtypeStruct((3 * model, frames_count), BF),
        ],
        compiler_params=params(),
        cost_estimate=estimate(6 * frames_count * model * model, 16e6),
        name="project",
    )(tab, frames, gain, shift, bias, *pieces)


def causal_bias(block):
    key = lax.broadcasted_iota(jnp.int32, (block, block), 0)
    query = lax.broadcasted_iota(jnp.int32, (block, block), 1)
    return jnp.where(key <= query, 0.0, MASKED)


def extend_rows(length, extent):
    first = lax.broadcasted_iota(jnp.int32, (16, extent), 0) == 0
    past = lax.broadcasted_iota(jnp.int32, (16, extent), 1) >= length
    key_rows = jnp.where(first & past, MASKED, 0.0).astype(BF)
    query_rows = jnp.where(first, 1.0, 0.0).astype(BF)
    return key_rows, query_rows


def attention_kernel(group, block, lengths, query, key, value, *rest):
    mixture, totals, keys, queries, causal = rest[-5:]
    extent = query.shape[1]

    @pl.when(pl.program_id(0) == 0)
    def _():
        causal[...] = causal_bias(block)

    key_rows, query_rows = extend_rows(lengths[0], extent)
    for head in range(group):
        part = pl.ds(HEAD * head, HEAD)
        keys[head, :HEAD, :] = key[part, :]
        keys[head, HEAD:, :] = key_rows
        queries[head, :HEAD, :] = query[part, :]
        queries[head, HEAD:, :] = query_rows
    for head in range(group):
        part = pl.ds(HEAD * head, HEAD)
        for tile in range(extent // block):
            place = pl.ds(tile * block, block)
            own = queries[head, :, place]
            scores = []
            for other in range(tile + 1):
                score = dot(keys[head, :, pl.ds(other * block, block)], own, 0, 0)
                scores.append(score + causal[...] if other == tile else score)
            highest = scores[0].max(0, keepdims=True)
            for score in scores[1:]:
                highest = jnp.maximum(highest, score.max(0, keepdims=True))
            offset = highest * (SCALE * LOG2E)
            summed = jnp.zeros((1, block), F32)
            total = jnp.zeros((HEAD, block), F32)
            for other, score in enumerate(scores):
                weight = jnp.exp2(score * (SCALE * LOG2E) - offset)
                summed = summed + weight.sum(0, keepdims=True)
                total = total + dot(value[part, pl.ds(other * block, block)], weight.astype(BF), 1, 0)
            mixture[part, place] = (total * (1.0 / summed)).astype(BF)
            totals[0, pl.ds(head, 1), place] = offset + jnp.log2(summed)


def attention_call(lengths, project, part_of=(0, 1), earlier=()):
    extent = project.shape[1]
    group, block = 2, min(512, extent)
    size, groups = HEAD * group, HEADS // group
    steps = groups // part_of[1]
    base = steps * part_of[0]

    def part(section):
        return pl.BlockSpec((size, extent), lambda i: (i + base + section * groups, 0))

    pairs = extent * extent * 5 // 8
    return pl.pallas_call(
        functools.partial(attention_kernel, group, block),
        grid=(steps,),
        in_specs=[SMEM, part(0), part(1), part(2)] + [ANY] * len(earlier),
        out_specs=[part(0), pl.BlockSpec((1, group, extent), lambda i: (i + base, 0, 0))],
        out_shape=[
            jax.ShapeDtypeStruct((HEADS * HEAD, extent), BF),
            jax.ShapeDtypeStruct((groups, group, extent), F32),
        ],
        input_output_aliases={4 + n: n for n in range(len(earlier))},
        scratch_shapes=[
            pltpu.VMEM((group, HEAD + 16, extent), BF),
            pltpu.VMEM((group, HEAD + 16, extent), BF),
            pltpu.VMEM((block, block), F32),
        ],
        compiler_params=params(),
        cost_estimate=estimate(16 * HEADS * pairs * HEAD / part_of[1], 8e6),
        name="attention",
    )(lengths, project, project, project, *earlier)


def gelu_parts(hidden):
    chance = 0.5 + 0.5 * lax.erf(hidden * 0.7071067811865476)
    density = jnp.exp2(hidden * hidden * (-0.5 * LOG2E)) * 0.3989422804014327
    return hidden * chance, chance + hidden * density


def out_kernel(
    count, tab, lengths, mixture, frames, cotangent, out_bias, gain, shift, *rest
):
    pieces = rest[:count]
    middle, normed, result, down_bias, out_weight, sems = rest[count:]
    step = pl.program_id(0)
    model = mixture.shape[0]

    size = frames.shape[0]

    def fetch():
        return load_all(pieces, tab, out_weight, sems, model // 4, TILE)

    @pl.when(step == 0)
    def _():
        start(fetch())
        down_bias[...] = jnp.zeros_like(down_bias)

    def mask(rows, sums):
        place = step * size + rows.start + lax.broadcasted_iota(jnp.int32, (ROWS, 1), 0)
        masked = jnp.where(place < lengths[0], cotangent[rows, :].astype(F32), 0.0)
        result[rows, :] = masked.astype(BF)
        return sums + masked.sum(0, keepdims=True)

    down_bias[...] += chunks(size, ROWS, mask, jnp.zeros((1, model), F32))

    @pl.when(step == 0)
    def _():
        wait(fetch())

    def branch(rows, carry):
        total = dot(mixture[:, rows], out_weight[...], 0, 0) + out_bias[...]
        total = frames[rows, :].astype(F32) + total
        middle[rows, :] = total
        unit, _ = normalise(total)
        normed[rows, :] = (unit * gain[...] + shift[...]).astype(BF)
        return carry

    chunks(size, ROWS, branch)


def out_call(tab, lengths, mixture, frames, cotangent, vectors, pieces):
    model, extent = mixture.shape
    size = min(512, extent)
    block = pl.BlockSpec((size, model), lambda i: (i, 0))
    return pl.pallas_call(
        functools.partial(out_kernel, len(pieces)),
        grid=(extent // size,),
        in_specs=[SMEM, SMEM]
        + [pl.BlockSpec((model, size), lambda i: (0, i)), block, block]
        + [whole(1, model)] * 3
        + [ANY] * len(pieces),
        out_specs=[block, block, block, whole(1, model)],
        out_shape=[
            jax.ShapeDtypeStruct((extent, model), F32),
            jax.ShapeDtypeStruct((extent, model), BF),
            jax.ShapeDtypeStruct((extent, model), BF),
            vec(model),
        ],
        scratch_shapes=[pltpu.VMEM((model, model), BF), pltpu.SemaphoreType.DMA((32,))],
        compiler_params=params(),
        cost_estimate=estimate(1, 1),
        name="out",
    )(tab, lengths, mixture, frames, cotangent, *vectors, *pieces)


def up_kernel(counts, tab, normed, result, up_bias, *rest):
    count_up, count_grad = counts
    up_pieces, rest = rest[:count_up], rest[count_up:]
    active, slope = rest[:2]
    grads, rest = rest[2 : 2 + count_grad], rest[2 + count_grad :]
    weight, staged, sems_up, sems_grad = rest
    step = pl.program_id(0)
    steps = pl.num_programs(0)
    extent = normed.shape[0]

    def fetch(block):
        slot = lax.rem(block, 2)
        return load_columns(up_pieces, tab, block, weight.at[slot], sems_up.at[slot], TILE)

    def send(pair):
        slot = lax.rem(pair, 2)
        return store_row_pair(grads, tab, pair, staged.at[slot], sems_grad.at[slot])

    @pl.when(step == 0)
    def _():
        start(fetch(step))

    @pl.when(step + 1 < steps)
    def _():
        start(fetch(step + 1))

    wait(fetch(step))
    now = lax.rem(step, 2)

    def widen(rows, carry):
        hidden = dot(normed[rows, :], weight[now], 1, 0) + up_bias[...]
        value, grade = gelu_parts(hidden)
        active[rows, :] = value.astype(BF)
        slope[rows, :] = grade.astype(BF)
        return carry

    chunks(extent, ROWS, widen)

    @pl.when(step >= 2)
    def _():
        wait(send(step - 2))

    def weigh(columns, carry):
        staged[now, columns, :] = dot(active[:, columns], result[...], 0, 0).astype(BF)
        return carry

    chunks(TILE, ROWS, weigh)
    start(send(step))

    @pl.when(step == steps - 1)
    def _():
        wait(send(step - 1))
        wait(send(step))


def up_call(tab, normed, result, up_bias, up_pieces, spread, sizes):
    extent, model = normed.shape
    hidden = 4 * model
    grads = gradient_shapes(spread, hidden, model, *sizes)
    steps = hidden // TILE
    return pl.pallas_call(
        functools.partial(up_kernel, (len(up_pieces), len(grads))),
        grid=(steps,),
        in_specs=[SMEM, whole(extent, model), whole(extent, model)]
        + [pl.BlockSpec((1, TILE), lambda i: (0, i))]
        + [ANY] * len(up_pieces),
        out_specs=[
            pl.BlockSpec((extent, TILE), lambda i: (0, i)),
            pl.BlockSpec((extent, TILE), lambda i: (0, i)),
        ]
        + [ANY] * len(grads),
        out_shape=[
            jax.ShapeDtypeStruct((extent, hidden), BF),
            jax.ShapeDtypeStruct((extent, hidden), BF),
        ]
        + grads,
        scratch_shapes=[
            pltpu.VMEM((2, model, TILE), BF),
            pltpu.VMEM((2, TILE, model), BF),
            pltpu.SemaphoreType.DMA((2, 8)),
            pltpu.SemaphoreType.DMA((2, 8)),
        ],
        compiler_params=params(),
        cost_estimate=estimate(16 * extent * model * model, 50e6, extent * hidden),
        name="up",
    )(tab, normed, result, up_bias, *up_pieces)


def back_kernel(counts, tab, mixture, middle, normed, d_result, slope, *rest):
    count_out, count_up, count_down, count_grad = counts
    gain = rest[0]
    rest = rest[1:]
    out_pieces, rest = rest[:count_out], rest[count_out:]
    up_pieces, rest = rest[:count_up], rest[count_up:]
    down_pieces, rest = rest[:count_down], rest[count_down:]
    d_middle, d_mixture, up_bias, gain_grad, shift_grad, out_bias = rest[:6]
    rest = rest[6:]
    grads, rest = rest[:count_grad], rest[count_grad:]
    (
        mixed,
        out_weight,
        total,
        unit_rows,
        result,
        down,
        up,
        d_hidden,
        d_normed,
        staged,
        sems_in,
        sems_out,
        sems_down,
        sems_up,
        sems_grad,
    ) = rest
    spread = len(grads[0].shape) == 4
    if spread:
        up_grads = out_grads = grads
    else:
        up_grads, out_grads = grads[:1], grads[1:]
    step = pl.program_id(0)
    steps = pl.num_programs(0)
    extent, model = result.shape
    width = model // 4

    def fetch(index):
        slot = index % 2
        copies = load_rows(down_pieces, tab, index, down.at[slot], sems_down.at[slot])
        block = tab[T_PAIR + index]
        copies += load_columns(up_pieces, tab, block, up.at[slot], sems_up.at[slot], TILE)
        return copies

    def send(index):
        slot = index % 2
        block = tab[T_PAIR + index]
        return store_column_block(
            up_grads, tab, block, staged.at[slot], sems_grad.at[slot], TILE
        )

    def send_out(block):
        return store_column_block(
            out_grads,
            tab,
            block,
            staged.at[0, :, pl.ds(block * width, width)],
            sems_out.at[pl.ds(block * 8, 8)],
            width,
            TILE if spread else 0,
        )

    def early(n):
        pair = ((d_result, result), (normed, unit_rows))[n]
        return pltpu.make_async_copy(*pair, sems_in.at[n])

    def late():
        return [
            pltpu.make_async_copy(middle, total, sems_in.at[2]),
            pltpu.make_async_copy(mixture, mixed, sems_in.at[3]),
        ] + load_all(out_pieces, tab, out_weight, sems_out, width, TILE)

    now = lax.rem(step, 2)

    @pl.when(step == 0)
    def _():
        early(0).start()
        start(fetch(0))
        early(1).start()
        early(0).wait()
        d_normed[...] = jnp.zeros_like(d_normed)

    def arrive(index):
        if index == 2:
            start(late())
        if index + 1 < 4:
            start(fetch(index + 1))
        wait(fetch(index))
        if index >= 2:
            wait(send(index - 2))

    for index in range(4):
        pl.when(step == index)(functools.partial(arrive, index))

    def shrink(rows, sums):
        d_active = dot(result[rows, :], down[now], 1, 1)
        piece = (d_active * slope[rows, :].astype(F32)).astype(BF)
        d_hidden[rows, :] = piece
        return sums + piece.astype(F32).sum(0, keepdims=True)

    up_bias[...] = chunks(extent, ROWS, shrink, jnp.zeros((1, TILE), F32))

    @pl.when(step == 0)
    def _():
        early(1).wait()

    def weigh(columns, carry):
        staged[now, columns, :] = dot(unit_rows[:, columns], d_hidden[...], 0, 0).astype(BF)
        return carry

    chunks(model, ROWS, weigh)
    for index in range(4):
        pl.when(step == index)(lambda index=index: start(send(index)))

    def widen(rows, carry):
        d_normed[rows, :] += dot(d_hidden[rows, :], up[now], 1, 1)
        return carry

    chunks(extent, ROWS, widen)

    @pl.when(step == steps - 1)
    def _():
        wait(late())
        none = jnp.zeros((1, model), F32)

        def norm(rows, sums):
            unit, scale = normalise(total[rows, :])
            grade = d_normed[rows, :]
            gains = sums[0] + (grade * unit).sum(0, keepdims=True)
            shifts = sums[1] + grade.sum(0, keepdims=True)
            grade = grade * gain[...]
            level = jnp.mean(grade, axis=-1, keepdims=True)
            tilt = jnp.mean(grade * unit, axis=-1, keepdims=True)
            d_total = result[rows, :].astype(F32) + scale * (grade - level - unit * tilt)
            d_middle[rows, :] = d_total
            branch = d_total.astype(BF)
            unit_rows[rows, :] = branch
            return gains, shifts, sums[2] + branch.astype(F32).sum(0, keepdims=True)

        sums = chunks(extent, ROWS, norm, (none, none, none))
        gain_grad[...], shift_grad[...], out_bias[...] = sums
        wait(send(2))

        def weigh_out(rows, carry):
            staged[0, rows, :] = dot(mixed[rows, :], unit_rows[...], 1, 0).astype(BF)
            return carry

        chunks(model, ROWS, weigh_out)
        for block in range(4):
            start(send_out(block))

        def turn(rows, carry):
            d_mixture[rows, :] = dot(out_weight[rows, :], unit_rows[...], 1, 1).astype(BF)
            return carry

        chunks(model, ROWS, turn)
        wait(send(3))
        for block in range(4):
            wait(send_out(block))


def back_call(tab, mixture, middle, normed, d_result, slope, gain, pieces, spread, sizes):
    out_pieces, up_pieces, down_pieces = pieces
    model, extent = mixture.shape
    hidden = slope.shape[1]
    if spread:
        grads = gradient_shapes(spread, model, hidden + model, *sizes)
    else:
        grads = gradient_shapes(spread, model, hidden, *sizes)
        grads += gradient_shapes(spread, model, model, *sizes)
    steps = hidden // TILE
    grid = pltpu.PrefetchScalarGridSpec(
        num_scalar_prefetch=1,
        grid=(steps,),
        in_specs=[ANY, ANY, ANY, ANY]
        + [pl.BlockSpec((extent, TILE), lambda i, tab: (0, tab[T_PAIR + i]))]
        + [whole(1, model)]
        + [ANY] * (len(out_pieces) + len(up_pieces) + len(down_pieces)),
        out_specs=[
            whole(extent, model),
            whole(model, extent),
            pl.BlockSpec((1, TILE), lambda i, tab: (0, tab[T_PAIR + i])),
            whole(1, model),
            whole(1, model),
            whole(1, model),
        ]
        + [ANY] * len(grads),
        scratch_shapes=[
            pltpu.VMEM((model, extent), BF),
            pltpu.VMEM((model, model), BF),
            pltpu.VMEM((extent, model), F32),
            pltpu.VMEM((extent, model), BF),
            pltpu.VMEM((extent, model), BF),
            pltpu.VMEM((2, TILE, model), BF),
            pltpu.VMEM((2, model, TILE), BF),
            pltpu.VMEM((extent, TILE), BF),
            pltpu.VMEM((extent, model), F32),
            pltpu.VMEM((2, model, TILE), BF),
            pltpu.SemaphoreType.DMA((4,)),
            pltpu.SemaphoreType.DMA((32,)),
            pltpu.SemaphoreType.DMA((2, 8)),
            pltpu.SemaphoreType.DMA((2, 8)),
            pltpu.SemaphoreType.DMA((2, 8)),
        ],
    )
    return pl.pallas_call(
        functools.partial(
            back_kernel, (len(out_pieces), len(up_pieces), len(down_pieces), len(grads))
        ),
        grid_spec=grid,
        out_shape=[
            jax.ShapeDtypeStruct((extent, model), F32),
            jax.ShapeDtypeStruct((model, extent), BF),
            vec(hidden),
            vec(model),
            vec(model),
            vec(model),
        ]
        + grads,
        compiler_params=params(),
        cost_estimate=estimate(28 * extent * model * model, 60e6),
        name="back",
    )(
        tab,
        mixture,
        middle,
        normed,
        d_result,
        slope,
        gain,
        *out_pieces,
        *up_pieces,
        *down_pieces,
    )


def attention_back_kernel(
    group,
    block,
    lengths,
    query,
    key,
    value,
    mixture,
    d_mixture,
    totals,
    *rest,
):
    d_project, keys, queries, causal, d_keys, d_values = rest[-6:]
    extent = query.shape[1]

    @pl.when(pl.program_id(0) == 0)
    def _():
        causal[...] = causal_bias(block)

    key_rows, query_rows = extend_rows(lengths[0], extent)
    for head in range(group):
        part = pl.ds(HEAD * head, HEAD)
        keys[head, :HEAD, :] = key[part, :]
        keys[head, HEAD:, :] = key_rows
        queries[head, :HEAD, :] = query[part, :]
        queries[head, HEAD:, :] = query_rows
    for head in range(group):
        part = pl.ds(HEAD * head, HEAD)
        for tile in range(extent // block):
            place = pl.ds(tile * block, block)
            own = queries[head, :, place]
            grade = d_mixture[part, place]
            center = (grade.astype(F32) * mixture[part, place].astype(F32)).sum(0, keepdims=True)
            total = totals[0, pl.ds(head, 1), place]
            d_query = jnp.zeros((HEAD, block), F32)
            for other in range(tile + 1):
                span = pl.ds(other * block, block)
                score = dot(keys[head, :, span], own, 0, 0)
                if other == tile:
                    score = score + causal[...]
                weight = jnp.exp2(score * (SCALE * LOG2E) - total)
                d_weight = dot(value[part, span], grade, 0, 0)
                d_score = (weight * (d_weight - center)).astype(BF)
                d_value = dot(grade, weight.astype(BF), 1, 1)
                d_key = dot(query[part, place], d_score, 1, 1)
                d_query = d_query + dot(key[part, span], d_score, 1, 0)
                if other == tile:
                    d_values[:, span] = d_value
                    d_keys[:, span] = d_key
                else:
                    d_values[:, span] += d_value
                    d_keys[:, span] += d_key
            d_project[0, part, place] = (d_query * SCALE).astype(BF)
        d_project[1, part, :] = (d_keys[...] * SCALE).astype(BF)
        d_project[2, part, :] = d_values[...].astype(BF)


def attention_back_call(
    lengths, project, mixture, d_mixture, totals, part_of=(0, 1), earlier=()
):
    extent = project.shape[1]
    group, block = 2, min(512, extent)
    size, groups = HEAD * group, HEADS // group
    steps = groups // part_of[1]
    base = steps * part_of[0]

    def part(section):
        return pl.BlockSpec((size, extent), lambda i: (i + base + section * groups, 0))

    pairs = extent * extent * 5 // 8
    return pl.pallas_call(
        functools.partial(attention_back_kernel, group, block),
        grid=(steps,),
        in_specs=[SMEM, part(0), part(1), part(2), part(0), part(0)]
        + [pl.BlockSpec((1, group, extent), lambda i: (i + base, 0, 0))]
        + [ANY] * len(earlier),
        out_specs=pl.BlockSpec((3, size, extent), lambda i: (0, i + base, 0)),
        out_shape=jax.ShapeDtypeStruct((3, HEADS * HEAD, extent), BF),
        input_output_aliases={7: 0} if earlier else {},
        scratch_shapes=[
            pltpu.VMEM((group, HEAD + 16, extent), BF),
            pltpu.VMEM((group, HEAD + 16, extent), BF),
            pltpu.VMEM((block, block), F32),
            pltpu.VMEM((HEAD, extent), F32),
            pltpu.VMEM((HEAD, extent), F32),
        ],
        compiler_params=params(),
        cost_estimate=estimate(30 * HEADS * pairs * HEAD / part_of[1], 16e6),
        name="attention_back",
    )(lengths, project, project, project, mixture, d_mixture, totals, *earlier)


def attend_grad_kernel(count_grad, tab, d_project, normed, *rest):
    bias_grad = rest[0]
    grads, rest = rest[1 : 1 + count_grad], rest[1 + count_grad :]
    staged, sems_grad = rest
    step = pl.program_id(0)
    steps = pl.num_programs(0)
    extent, model = normed.shape
    width = d_project.shape[0]

    def send(block):
        slot = lax.rem(block, 2)
        return store_column_block(grads, tab, block, staged.at[slot], sems_grad.at[slot], width)

    @pl.when(step >= 2)
    def _():
        wait(send(step - 2))

    now = lax.rem(step, 2)

    def weigh(columns, carry):
        staged[now, columns, :] = dot(normed[:, columns], d_project[...], 0, 1).astype(BF)
        return carry

    chunks(model, ROWS, weigh)
    start(send(step))
    bias_grad[...] = dot(jnp.ones((8, extent), BF), d_project[...], 1, 1)[:1, :]

    @pl.when(step == steps - 1)
    def _():
        wait(send(step - 1))
        wait(send(step))


def attend_grad_call(tab, d_project, normed, spread, sizes):
    extent, model = normed.shape
    width = 3 * model // 4
    grads = gradient_shapes(spread, model, 3 * model, *sizes)
    return pl.pallas_call(
        functools.partial(attend_grad_kernel, len(grads)),
        grid=(4,),
        in_specs=[SMEM, pl.BlockSpec((width, extent), lambda i: (i, 0)), whole(extent, model)],
        out_specs=[pl.BlockSpec((1, width), lambda i: (0, i))] + [ANY] * len(grads),
        out_shape=[vec(3 * model)] + grads,
        scratch_shapes=[
            pltpu.VMEM((2, model, width), BF),
            pltpu.SemaphoreType.DMA((2, 8)),
        ],
        compiler_params=params(),
        cost_estimate=estimate(6 * extent * model * model, 14e6),
        name="attend_grad",
    )(tab, d_project, normed)


def first_kernel(count_in, tab, d_project, frames, d_middle, gain, *rest):
    pieces, rest = rest[:count_in], rest[count_in:]
    d_frames, gain_grad, shift_grad, weight, total, d_normed, sems, sem_total = rest
    step = pl.program_id(0)
    steps = pl.num_programs(0)
    extent, model = frames.shape
    width = d_project.shape[0]

    def fetch(index):
        slot = index % 2
        return load_slot(pieces, tab, index, weight.at[slot], sems.at[slot], width)

    def late():
        return pltpu.make_async_copy(d_middle, total, sem_total)

    @pl.when(step == 0)
    def _():
        start(fetch(0))
        late().start()
        d_normed[...] = jnp.zeros_like(d_normed)

    def arrive(index):
        if index + 1 < 4:
            start(fetch(index + 1))
        wait(fetch(index))

    for index in range(4):
        pl.when(step == index)(functools.partial(arrive, index))
    now = lax.rem(step, 2)

    def widen(rows, carry):
        d_normed[rows, :] += dot(d_project[:, rows], weight[now], 0, 1)
        return carry

    chunks(extent, ROWS, widen)

    @pl.when(step == steps - 1)
    def _():
        late().wait()
        none = jnp.zeros((1, model), F32)

        def norm(rows, sums):
            unit, scale = normalise(frames[rows, :].astype(F32))
            grade = d_normed[rows, :]
            gains = sums[0] + (grade * unit).sum(0, keepdims=True)
            shifts = sums[1] + grade.sum(0, keepdims=True)
            grade = grade * gain[...]
            level = jnp.mean(grade, axis=-1, keepdims=True)
            tilt = jnp.mean(grade * unit, axis=-1, keepdims=True)
            d_frames[rows, :] = (total[rows, :] + scale * (grade - level - unit * tilt)).astype(BF)
            return gains, shifts

        gains, shifts = chunks(extent, ROWS, norm, (none, none))
        gain_grad[...] = gains
        shift_grad[...] = shifts


def first_call(tab, d_project, frames, d_middle, gain, pieces):
    extent, model = frames.shape
    width = 3 * model // 4
    grid = pltpu.PrefetchScalarGridSpec(
        num_scalar_prefetch=1,
        grid=(4,),
        in_specs=[pl.BlockSpec((width, extent), lambda i, tab: (tab[T_COL + i], 0))]
        + [whole(extent, model), ANY, whole(1, model)]
        + [ANY] * len(pieces),
        out_specs=[whole(extent, model), whole(1, model), whole(1, model)],
        scratch_shapes=[
            pltpu.VMEM((2, model, width), BF),
            pltpu.VMEM((extent, model), F32),
            pltpu.VMEM((extent, model), F32),
            pltpu.SemaphoreType.DMA((2, 8)),
            pltpu.SemaphoreType.DMA,
        ],
    )
    return pl.pallas_call(
        functools.partial(first_kernel, len(pieces)),
        grid_spec=grid,
        out_shape=[jax.ShapeDtypeStruct((extent, model), BF), vec(model), vec(model)],
        compiler_params=params(),
        cost_estimate=estimate(6 * extent * model * model, 24e6),
        name="first",
    )(tab, d_project, frames, d_middle, gain, *pieces)


def down_kernel(count, base, ending, tab, active, middle, bias, *rest):
    pieces = rest[:count]
    frames_out, weight, total, sems = rest[count:]
    step = pl.program_id(0)
    steps = pl.num_programs(0)

    def fetch(index):
        slot = (index - base) % 2
        return load_rows(pieces, tab, index, weight.at[slot], sems.at[slot])

    def arrive(index):
        if index == base:
            start(fetch(index))
        if index + 1 < ending:
            start(fetch(index + 1))
        wait(fetch(index))

    for index in range(base, ending):
        pl.when(step == index - base)(functools.partial(arrive, index))

    @pl.when(step == 0)
    def _():
        total[...] = middle[...] + bias[...] if base == 0 else middle[...]

    def widen(rows, carry):
        total[rows, :] += dot(active[rows, :], weight[lax.rem(step, 2)], 1, 0)
        return carry

    chunks(total.shape[0], ROWS, widen)

    @pl.when(step == steps - 1)
    def _():
        frames_out[...] = total[...].astype(frames_out.dtype)


def down_call(tab, active, middle, bias, pieces, part_of=(0, 1)):
    extent, hidden = active.shape
    model = middle.shape[1]
    steps = hidden // TILE // part_of[1]
    base = steps * part_of[0]
    last = part_of[0] + 1 == part_of[1]
    grid = pltpu.PrefetchScalarGridSpec(
        num_scalar_prefetch=1,
        grid=(steps,),
        in_specs=[pl.BlockSpec((extent, TILE), lambda i, tab: (0, tab[T_PAIR + base + i]))]
        + [whole(extent, model), whole(1, model)]
        + [ANY] * len(pieces),
        out_specs=whole(extent, model),
        scratch_shapes=[
            pltpu.VMEM((2, TILE, model), BF),
            pltpu.VMEM((extent, model), F32),
            pltpu.SemaphoreType.DMA((2, 8)),
        ],
    )
    return pl.pallas_call(
        functools.partial(down_kernel, len(pieces), base, base + steps),
        grid_spec=grid,
        out_shape=jax.ShapeDtypeStruct((extent, model), BF if last else F32),
        compiler_params=params(),
        cost_estimate=estimate(8 * extent * model * model, 24e6),
        name="down",
    )(tab, active, middle, bias, *pieces)


def gather_plain(weight):
    wide = lax.all_gather(weight, "inner", axis=1, tiled=True)
    return [lax.all_gather(wide, "dp", axis=0, tiled=True)]


def scatter_plain(grads):
    wide = lax.psum_scatter(grads[0], "dp", scatter_dimension=0, tiled=True)
    return lax.psum_scatter(wide, "inner", scatter_dimension=1, tiled=True).astype(F32)


CORE, NEAR, FAR = 0, 1, 2


def swap(value, way):
    flips = {CORE: (1, 1), NEAR: (2, 4), FAR: (4, 2)}[way]
    return lax.ppermute(value, "dp", [(d, d ^ flips[d & 1]) for d in range(8)])


def shift(value, amount):
    return lax.ppermute(value, "inner", [(i, (i + amount) & 3) for i in range(4)])


def after(value, *done):
    return lax.optimization_barrier((value, done))[0]


def stack_spread(block):
    return jnp.stack([block] + [shift(block, amount) for amount in (1, 2, 3)])


def added(*values):
    total = values[0].astype(F32)
    for value in values[1:]:
        total = total + value.astype(F32)
    return total


def sum_parts(keep, core, link, last):
    blocks = [added(keep[3, k], core[3, k], link[1, k], last[k]) for k in range(4)]
    return [blocks[0]] + [block.astype(BF) for block in blocks[1:]]


def shift_parts(parts):
    return [shift(parts[k], k) for k in (1, 2, 3)]


def exchange(values, axis, size):
    return [values] + [
        lax.ppermute(values, axis, [(i, i ^ flip) for i in range(size)])
        for flip in range(1, size)
    ]


def tree_sum(terms):
    while len(terms) > 1:
        terms = [terms[i] + terms[i + 1] for i in range(0, len(terms), 2)]
    return terms[0]


def shards(
    spread,
    sizes,
    frames_in,
    lengths,
    first_gain,
    first_shift,
    attend_weight,
    attend_bias,
    output_weight,
    output_bias,
    second_gain,
    second_shift,
    up_weight,
    up_bias,
    down_weight,
    down_bias,
    cotangent,
):
    _, extent, model = frames_in.shape
    frames = frames_in.reshape(extent, model)
    upstream = cotangent.reshape(extent, model)
    tab = make_table(spread, True)
    tab_plain = make_table(spread, False)

    def row(vector):
        return vector.reshape(1, -1)

    if not spread:
        attend_pieces = gather_plain(attend_weight)
        out_pieces = gather_plain(output_weight)
        up_pieces = gather_plain(up_weight)
        down_pieces = gather_plain(down_weight)
    else:
        others = [shift(attend_weight, amount) for amount in (1, 2, 3)]
        near, far = swap(attend_weight, NEAR), swap(attend_weight, FAR)
        others = jnp.stack(others)
        far, near = after((far, near), near, far)
        diagonal = swap(near, FAR)
        attend_pieces = [attend_weight, near, far, diagonal]
        attend_pieces += [swap(piece, CORE) for piece in attend_pieces]
        others = after(others, diagonal)
        near, far = swap(others, NEAR), swap(others, FAR)
        up_block = after(jnp.concatenate([up_weight, output_weight], axis=1), others)
        up_own = lax.all_gather(up_block, "inner")
        near, far = after((near, far), near, far)
        diagonal = swap(near, FAR)
        others = [others, near, far, diagonal]
        attend_pieces += others + [swap(piece, CORE) for piece in others]
        up_own = after(up_own, diagonal)
        up_near, up_far = swap(up_own, NEAR), swap(up_own, FAR)
        down_own = lax.all_gather(after(down_weight, up_own), "inner")
    bias_row = jnp.concatenate([attend_bias[0], jnp.zeros_like(attend_bias[0]), attend_bias[1]])
    normed, project = project_call(
        tab,
        after(frames, up_own) if spread else frames,
        row(first_gain),
        row(first_shift),
        row(bias_row),
        attend_pieces,
    )
    if spread:
        mixture, totals = attention_call(lengths, after(project, up_own), (0, 2))
        up_near, up_far = after((up_near, up_far), totals)
        up_diagonal = swap(up_near, FAR)
        ahead = [swap(piece, CORE) for piece in (after(up_own, totals), up_near, up_far)]
        down_own = after(down_own, up_near, up_far)
        down_near, down_far = swap(down_own, NEAR), swap(down_own, FAR)
        mixture, totals = attention_call(
            lengths, after(project, up_near, up_far, down_own), (1, 2), (mixture, totals)
        )
        up_pieces = [up_own, up_near, up_far, up_diagonal]
        up_pieces += ahead + [swap(after(up_diagonal, totals), CORE)]
        out_pieces = up_pieces
    else:
        mixture, totals = attention_call(lengths, project)
    vectors = (row(output_bias), row(second_gain), row(second_shift))
    middle, normed_two, d_result, grad_down_bias = out_call(
        tab_plain, lengths, mixture, frames, upstream, vectors, out_pieces
    )
    if spread:
        down_near, down_far = after((down_near, down_far), normed_two)
        down_diagonal = swap(down_near, FAR)
        ahead = [swap(piece, CORE) for piece in (after(down_own, totals), down_near, down_far)]
        normed_two = after(normed_two, down_near, down_far)
    active, slope, *down_grads = up_call(
        tab_plain, normed_two, d_result, row(up_bias), up_pieces, False, sizes
    )
    if spread:
        down_pieces = [down_own, down_near, down_far, down_diagonal]
        down_pieces += ahead + [swap(after(down_diagonal, slope), CORE)]
        down_wide = lax.psum_scatter(down_grads[0], "dp", scatter_dimension=0, tiled=True)
    else:
        down_owned = scatter_plain(down_grads)
    (
        d_middle,
        d_mixture,
        grad_up_bias,
        grad_second_gain,
        grad_second_shift,
        grad_output_bias,
        *back_grads,
    ) = back_call(
        tab_plain,
        mixture,
        middle,
        normed_two,
        d_result,
        slope,
        row(second_gain),
        (out_pieces, up_pieces, down_pieces),
        spread,
        sizes,
    )
    early = jnp.concatenate(
        [grad_output_bias, grad_second_gain, grad_second_shift, grad_down_bias, grad_up_bias],
        axis=1,
    )
    if spread:
        back_keep, back_send = back_grads
        back_core = swap(back_send, CORE)
        d_project = attention_back_call(lengths, project, mixture, d_mixture, totals, (0, 2))
        back_core, down_wide = after((back_core, down_wide), d_project)
        back_first = added(back_keep[:2], back_core[:2]).astype(BF)
        back_link = swap(back_first, FAR)
        down_owned = lax.psum_scatter(down_wide, "inner", scatter_dimension=1, tiled=True)
        d_project = attention_back_call(
            lengths,
            project,
            mixture,
            after(d_mixture, back_first, down_wide),
            totals,
            (1, 2),
            (d_project,),
        )
        d_rows = d_project.reshape(3 * model, extent)
        grad_bias, attend_keep, attend_send = attend_grad_call(tab, d_rows, normed, spread, sizes)
        attend_core = swap(attend_send, CORE)
        back_link = after(back_link, grad_bias)
        back_second = added(back_keep[2], back_core[2], back_link[0]).astype(BF)
        back_last = swap(back_second, NEAR)
        attend_core = after(attend_core, back_second)
        attend_first = added(attend_keep[:2], attend_core[:2]).astype(BF)
        attend_link = swap(attend_first, FAR)
        d_frames, grad_first_gain, grad_first_shift = first_call(
            tab,
            after(d_rows, attend_first),
            frames,
            d_middle,
            row(first_gain),
            attend_pieces,
        )
        late = [grad_first_gain, grad_first_shift, grad_bias[:, :model], grad_bias[:, 2 * model :]]
        small = jnp.concatenate(late + [early], axis=1)
        back_last, attend_link, down_owned = after((back_last, attend_link, down_owned), d_frames)
        attend_second = added(attend_keep[2], attend_core[2], attend_link[0]).astype(BF)
        attend_last = swap(attend_second, NEAR)
        back_last = after(back_last, attend_second)
        back_parts = sum_parts(back_keep, back_core, back_link, back_last)
        back_others = shift_parts(back_parts)
        small_terms = exchange(small, "inner", 4)
        active, middle = after((active, middle), attend_second, back_parts, small, down_owned)
        frames_out = down_call(tab_plain, active, middle, row(down_bias), down_pieces)
        attend_last, back_others, small_terms = after(
            (attend_last, back_others, small_terms), frames_out
        )
        back_owned = added(back_parts[0], *back_others)
        small = tree_sum(small_terms)
        attend_parts = sum_parts(attend_keep, attend_core, attend_link, attend_last)
        attend_parts, small = after((attend_parts, small), back_owned, small, attend_parts)
        others = shift_parts(attend_parts)
        small_terms = exchange(small, "dp", 8)
        attend_owned = added(attend_parts[0], *others)
        small = tree_sum(small_terms).reshape(-1)
        down_owned = down_owned.astype(F32)
        up_owned, output_owned = back_owned[:, :TILE], back_owned[:, TILE:]
    else:
        d_project = attention_back_call(lengths, project, mixture, d_mixture, totals)
        d_rows = d_project.reshape(3 * model, extent)
        grad_bias, *attend_grads = attend_grad_call(tab, d_rows, normed, spread, sizes)
        d_frames, grad_first_gain, grad_first_shift = first_call(
            tab, d_rows, frames, d_middle, row(first_gain), attend_pieces
        )
        frames_out = down_call(tab_plain, active, middle, row(down_bias), down_pieces)
        up_owned = scatter_plain(back_grads[:1])
        output_owned = scatter_plain(back_grads[1:])
        attend_owned = scatter_plain(attend_grads)
        late = [grad_first_gain, grad_first_shift, grad_bias[:, :model], grad_bias[:, 2 * model :]]
        small = lax.psum(jnp.concatenate(late + [early], axis=1), ("dp", "inner")).reshape(-1)

    def take(first, count=1):
        return small[first * model : (first + count) * model]

    return (
        frames_out.reshape(frames_in.shape),
        d_frames.reshape(frames_in.shape),
        take(0),
        take(1),
        attend_owned,
        take(2, 2).reshape(2, model),
        output_owned,
        take(4),
        take(5),
        take(6),
        up_owned,
        take(8, 4),
        down_owned,
        take(7),
    )


def solution(mesh):
    sizes = (mesh.shape["dp"], mesh.shape["inner"])
    spread = sizes == (8, 4)
    return jax.shard_map(
        functools.partial(shards, spread, sizes),
        mesh=mesh,
        in_specs=(
            P(("dp", "inner"), None, None),
            P(("dp", "inner")),
            P(),
            P(),
            P("dp", "inner"),
            P(),
            P("dp", "inner"),
            P(),
            P(),
            P(),
            P("dp", "inner"),
            P(),
            P("dp", "inner"),
            P(),
            P(("dp", "inner"), None, None),
        ),
        out_specs=(
            P(("dp", "inner"), None, None),
            P(("dp", "inner"), None, None),
            P(),
            P(),
            P("dp", "inner"),
            P(),
            P("dp", "inner"),
            P(),
            P(),
            P(),
            P("dp", "inner"),
            P(),
            P("dp", "inner"),
            P(),
        ),
        check_vma=False,
    )
```

```python
import functools

import jax
import jax.numpy as jnp
from jax import lax
from jax.experimental import pallas as pl
from jax.experimental.pallas import tpu as pltpu
from jax.sharding import PartitionSpec as P

HEADS = 16
HEAD = 64
TILE = 1024
ROWS = 256
LOG2E = 1.4426950408889634
MASKED = -1e30
SCALE = HEAD ** (-0.5)
BF = jnp.bfloat16
F32 = jnp.float32
LIMIT = 60 * 2**20


def dot(left, right, on_left, on_right):
    return lax.dot_general(
        left, right, (((on_left,), (on_right,)), ((), ())), preferred_element_type=F32
    )


def normalise(values):
    center = values - jnp.mean(values, axis=-1, keepdims=True)
    spread = jnp.mean(center * center, axis=-1, keepdims=True)
    scale = lax.rsqrt(spread + 1e-05)
    return center * scale, scale


def params(name_limit=LIMIT):
    return pltpu.CompilerParams(vmem_limit_bytes=name_limit)


def estimate(flops, moved, exps=0):
    return pl.CostEstimate(
        flops=int(8 * flops), bytes_accessed=int(8 * moved), transcendentals=int(8 * exps)
    )


ANY = pl.BlockSpec(memory_space=pl.ANY)
SMEM = pl.BlockSpec(memory_space=pltpu.SMEM)


def whole(*shape):
    return pl.BlockSpec(shape, lambda *_: (0,) * len(shape))


def vec(size):
    return jax.ShapeDtypeStruct((1, size), F32)


PIECES = 8
SLOTS = 4
T_ROW = 0
T_COL = 8
T_SLOT_IN = 12
T_SLOT_OUT = 16
T_PAIR = 20
T_OUT = 24
T_PLACE = 32
T_CORE = 40
T_SIZE = 48


def make_table(spread, relative):
    if not spread:
        order = list(range(4))
        entries = [0] * T_SIZE
        entries[T_PAIR : T_PAIR + 4] = order
        entries[T_COL : T_COL + 4] = order
        return jnp.array(entries, jnp.int32)
    row = lax.axis_index("dp").astype(jnp.int32)
    column = lax.axis_index("inner").astype(jnp.int32)
    core = row & 1
    near = jnp.where(core == 0, 2, 4)
    far = 6 - near
    entries = [
        row,
        row ^ near,
        row ^ far,
        row ^ 6,
        row ^ 1,
        row ^ 1 ^ far,
        row ^ 1 ^ near,
        row ^ 7,
    ]
    if relative:
        entries += [(column - block) & 3 for block in range(4)] * 2
    else:
        entries += [0, 1, 2, 3] * 2
    entries += [(block - column) & 3 for block in range(4)]
    pair = row >> 1
    entries += [pair, pair ^ (near >> 1), pair ^ (far >> 1), pair ^ 3]
    for half in range(2):
        a, b = (far, near) if half == 0 else (near, far)
        own = row ^ half
        entries += [own ^ 6, own ^ a, own ^ b, own]
    for half in range(2):
        first = far if half == 0 else near
        for block in range(4):
            relative = (pair ^ block) << 1
            entries.append(
                jnp.where(
                    relative == 6,
                    0,
                    jnp.where(relative == 0, 3, jnp.where(relative == first, 1, 2)),
                )
            )
    entries += [core]
    entries += [jnp.int32(0)] * (T_SIZE - len(entries))
    return jnp.stack([jnp.asarray(entry, jnp.int32) for entry in entries])


def aligned(index, size):
    return pl.ds(pl.multiple_of(index * size, size), size)


def load_slot(pieces, tab, step, target, sems, width):
    if len(pieces) == 1:
        return load_columns(pieces, tab, tab[T_COL + step], target, sems, width)
    rows = pieces[0].shape[-2]
    copies = []
    for p in range(PIECES):
        source = pieces[p] if step == 0 else pieces[PIECES + p].at[step - 1]
        place = target.at[aligned(tab[T_ROW + p], rows), :]
        copies.append(pltpu.make_async_copy(source, place, sems.at[p]))
    return copies


def load_columns(pieces, tab, block, target, sems, width, first=0):
    if len(pieces) == 1:
        copies = [
            pltpu.make_async_copy(pieces[0].at[:, aligned(block, width)], target, sems.at[0])
        ]
        return copies
    slot = tab[T_SLOT_IN + block]
    rows = pieces[0].shape[1]
    return [
        pltpu.make_async_copy(
            pieces[p].at[slot, :, pl.ds(first, width)],
            target.at[aligned(tab[T_ROW + p], rows), :],
            sems.at[p],
        )
        for p in range(PIECES)
    ]


def load_rows(pieces, tab, step, target, sems):
    if len(pieces) == 1 and len(pieces[0].shape) == 2:
        return [
            pltpu.make_async_copy(
                pieces[0].at[aligned(tab[T_PAIR + step], TILE), :], target, sems.at[0]
            )
        ]
    rows, width = pieces[0].shape[-2:]
    if len(pieces) == 1:
        return [
            pltpu.make_async_copy(
                pieces[0].at[2 * tab[T_PAIR + step] + half, block],
                target.at[pl.ds(half * rows, rows), pl.ds(block * width, width)],
                sems.at[half * SLOTS + block],
            )
            for half in range(2)
            for block in range(4)
        ]
    partner = (4, 6, 5, 7)[step]
    copies = []
    for n, p in enumerate((step, partner)):
        half = tab[T_ROW + p] & 1
        for slot in range(SLOTS):
            copies.append(
                pltpu.make_async_copy(
                    pieces[p].at[slot],
                    target.at[aligned(half, rows), aligned(tab[T_COL + slot], width)],
                    sems.at[n * SLOTS + slot],
                )
            )
    return copies


def load_all(pieces, tab, target, sems, width, first=0):
    if len(pieces) == 1:
        return [pltpu.make_async_copy(pieces[0], target, sems.at[0])]
    rows = pieces[0].shape[1]
    return [
        pltpu.make_async_copy(
            pieces[p].at[slot, :, pl.ds(first, width)],
            target.at[aligned(tab[T_ROW + p], rows), aligned(tab[T_COL + slot], width)],
            sems.at[p * SLOTS + slot],
        )
        for p in range(PIECES)
        for slot in range(SLOTS)
    ]


def store_column_block(outs, tab, block, source, sems, width, first=0):
    if len(outs) == 1:
        return [pltpu.make_async_copy(source, outs[0].at[:, aligned(block, width)], sems.at[0])]
    rows = outs[0].shape[2]
    slot = tab[T_SLOT_OUT + block]
    return [
        pltpu.make_async_copy(
            source.at[aligned(tab[T_OUT + half * 4 + place], rows), :],
            outs[half].at[place, slot, :, pl.ds(first, width)],
            sems.at[half * 4 + place],
        )
        for half in range(2)
        for place in range(4)
    ]


def store_row_pair(outs, tab, pair, source, sems):
    if len(outs) == 1:
        return [pltpu.make_async_copy(source, outs[0].at[aligned(pair, TILE), :], sems.at[0])]
    rows, width = outs[0].shape[2:]
    copies = []
    for half in range(2):
        local = tab[T_CORE] ^ half
        for block in range(4):
            copies.append(
                pltpu.make_async_copy(
                    source.at[aligned(local, rows), pl.ds(block * width, width)],
                    outs[half].at[tab[T_PLACE + half * 4 + pair], tab[T_SLOT_OUT + block]],
                    sems.at[half * 4 + block],
                )
            )
    return copies


def chunks(extent, size, body, init=0):
    for first in range(0, extent, size):
        init = body(pl.ds(first, size), init)
    return init


def start(copies):
    for copy in copies:
        copy.start()


def wait(copies):
    for copy in copies:
        copy.wait()


def gradient_shapes(spread, rows, columns, dp, inner):
    if spread:
        return [jax.ShapeDtypeStruct((4, 4, rows // dp, columns // inner), BF)] * 2
    return [jax.ShapeDtypeStruct((rows, columns), BF)]


def project_kernel(count, tab, tokens, gain, shift, bias, *rest):
    pieces = rest[:count]
    normed, project, weight, sems = rest[count:]
    step = pl.program_id(0)
    width = project.shape[0]

    def fetch(index):
        slot = index % 2
        return load_slot(pieces, tab, index, weight.at[slot], sems.at[slot], width)

    @pl.when(step == 0)
    def _():
        start(fetch(0))

        def norm(rows, carry):
            unit, _ = normalise(tokens[rows, :].astype(F32))
            normed[rows, :] = (unit * gain[...] + shift[...]).astype(BF)
            return carry

        chunks(tokens.shape[0], ROWS, norm)

    def arrive(index):
        if index + 1 < 4:
            start(fetch(index + 1))
        wait(fetch(index))

    for index in range(4):
        pl.when(step == index)(functools.partial(arrive, index))

    column = jnp.transpose(jnp.broadcast_to(bias[...], (128, width)))[:, :1]

    project[...] = (dot(weight[lax.rem(step, 2)], normed[...], 0, 1) + column).astype(BF)


def project_call(tab, tokens, gain, shift, bias, pieces):
    extent, model = tokens.shape
    width = 3 * model // 4
    grid = pltpu.PrefetchScalarGridSpec(
        num_scalar_prefetch=1,
        grid=(4,),
        in_specs=[whole(extent, model), whole(1, model), whole(1, model)]
        + [pl.BlockSpec((1, width), lambda i, tab: (0, tab[T_COL + i]))]
        + [ANY] * len(pieces),
        out_specs=[
            whole(extent, model),
            pl.BlockSpec((width, extent), lambda i, tab: (tab[T_COL + i], 0)),
        ],
        scratch_shapes=[
            pltpu.VMEM((2, model, width), BF),
            pltpu.SemaphoreType.DMA((2, 8)),
        ],
    )
    return pl.pallas_call(
        functools.partial(project_kernel, len(pieces)),
        grid_spec=grid,
        out_shape=[
            jax.ShapeDtypeStruct((extent, model), BF),
            jax.ShapeDtypeStruct((3 * model, extent), BF),
        ],
        compiler_params=params(),
        cost_estimate=estimate(6 * extent * model * model, 16e6),
        name="project",
    )(tab, tokens, gain, shift, bias, *pieces)


def causal_bias(block):
    key = lax.broadcasted_iota(jnp.int32, (block, block), 0)
    query = lax.broadcasted_iota(jnp.int32, (block, block), 1)
    return jnp.where(key <= query, 0.0, MASKED)


def extend_rows(length, extent):
    first = lax.broadcasted_iota(jnp.int32, (16, extent), 0) == 0
    past = lax.broadcasted_iota(jnp.int32, (16, extent), 1) >= length
    key_rows = jnp.where(first & past, MASKED, 0.0).astype(BF)
    query_rows = jnp.where(first, 1.0, 0.0).astype(BF)
    return key_rows, query_rows


def attention_kernel(group, block, lengths, query, key, value, *rest):
    mixture, totals, keys, queries, causal = rest[-5:]
    extent = query.shape[1]

    @pl.when(pl.program_id(0) == 0)
    def _():
        causal[...] = causal_bias(block)

    key_rows, query_rows = extend_rows(lengths[0], extent)
    for head in range(group):
        part = pl.ds(HEAD * head, HEAD)
        keys[head, :HEAD, :] = key[part, :]
        keys[head, HEAD:, :] = key_rows
        queries[head, :HEAD, :] = query[part, :]
        queries[head, HEAD:, :] = query_rows
    for head in range(group):
        part = pl.ds(HEAD * head, HEAD)
        for tile in range(extent // block):
            place = pl.ds(tile * block, block)
            own = queries[head, :, place]
            scores = []
            for other in range(tile + 1):
                score = dot(keys[head, :, pl.ds(other * block, block)], own, 0, 0)
                scores.append(score + causal[...] if other == tile else score)
            highest = scores[0].max(0, keepdims=True)
            for score in scores[1:]:
                highest = jnp.maximum(highest, score.max(0, keepdims=True))
            offset = highest * (SCALE * LOG2E)
            summed = jnp.zeros((1, block), F32)
            total = jnp.zeros((HEAD, block), F32)
            for other, score in enumerate(scores):
                weight = jnp.exp2(score * (SCALE * LOG2E) - offset)
                summed = summed + weight.sum(0, keepdims=True)
                total = total + dot(value[part, pl.ds(other * block, block)], weight.astype(BF), 1, 0)
            mixture[part, place] = (total * (1.0 / summed)).astype(BF)
            totals[0, pl.ds(head, 1), place] = offset + jnp.log2(summed)


def attention_call(lengths, project, part_of=(0, 1), earlier=()):
    extent = project.shape[1]
    group, block = 2, min(512, extent)
    size, groups = HEAD * group, HEADS // group
    steps = groups // part_of[1]
    base = steps * part_of[0]

    def part(section):
        return pl.BlockSpec((size, extent), lambda i: (i + base + section * groups, 0))

    pairs = extent * extent * 5 // 8
    return pl.pallas_call(
        functools.partial(attention_kernel, group, block),
        grid=(steps,),
        in_specs=[SMEM, part(0), part(1), part(2)] + [ANY] * len(earlier),
        out_specs=[part(0), pl.BlockSpec((1, group, extent), lambda i: (i + base, 0, 0))],
        out_shape=[
            jax.ShapeDtypeStruct((HEADS * HEAD, extent), BF),
            jax.ShapeDtypeStruct((groups, group, extent), F32),
        ],
        input_output_aliases={4 + n: n for n in range(len(earlier))},
        scratch_shapes=[
            pltpu.VMEM((group, HEAD + 16, extent), BF),
            pltpu.VMEM((group, HEAD + 16, extent), BF),
            pltpu.VMEM((block, block), F32),
        ],
        compiler_params=params(),
        cost_estimate=estimate(16 * HEADS * pairs * HEAD / part_of[1], 8e6),
        name="attention",
    )(lengths, project, project, project, *earlier)


def gelu_parts(hidden):
    chance = 0.5 + 0.5 * lax.erf(hidden * 0.7071067811865476)
    density = jnp.exp2(hidden * hidden * (-0.5 * LOG2E)) * 0.3989422804014327
    return hidden * chance, chance + hidden * density


def out_kernel(
    count, tab, lengths, mixture, frames, cotangent, out_bias, gain, shift, *rest
):
    pieces = rest[:count]
    middle, normed, result, down_bias, out_weight, sems = rest[count:]
    step = pl.program_id(0)
    model = mixture.shape[0]

    size = frames.shape[0]

    def fetch():
        return load_all(pieces, tab, out_weight, sems, model // 4, TILE)

    @pl.when(step == 0)
    def _():
        start(fetch())
        down_bias[...] = jnp.zeros_like(down_bias)

    def mask(rows, sums):
        place = step * size + rows.start + lax.broadcasted_iota(jnp.int32, (ROWS, 1), 0)
        masked = jnp.where(place < lengths[0], cotangent[rows, :].astype(F32), 0.0)
        result[rows, :] = masked.astype(BF)
        return sums + masked.sum(0, keepdims=True)

    down_bias[...] += chunks(size, ROWS, mask, jnp.zeros((1, model), F32))

    @pl.when(step == 0)
    def _():
        wait(fetch())

    def branch(rows, carry):
        total = dot(mixture[:, rows], out_weight[...], 0, 0) + out_bias[...]
        total = frames[rows, :].astype(F32) + total
        middle[rows, :] = total
        unit, _ = normalise(total)
        normed[rows, :] = (unit * gain[...] + shift[...]).astype(BF)
        return carry

    chunks(size, ROWS, branch)


def out_call(tab, lengths, mixture, frames, cotangent, vectors, pieces):
    model, extent = mixture.shape
    size = min(512, extent)
    block = pl.BlockSpec((size, model), lambda i: (i, 0))
    return pl.pallas_call(
        functools.partial(out_kernel, len(pieces)),
        grid=(extent // size,),
        in_specs=[SMEM, SMEM]
        + [pl.BlockSpec((model, size), lambda i: (0, i)), block, block]
        + [whole(1, model)] * 3
        + [ANY] * len(pieces),
        out_specs=[block, block, block, whole(1, model)],
        out_shape=[
            jax.ShapeDtypeStruct((extent, model), F32),
            jax.ShapeDtypeStruct((extent, model), BF),
            jax.ShapeDtypeStruct((extent, model), BF),
            vec(model),
        ],
        scratch_shapes=[pltpu.VMEM((model, model), BF), pltpu.SemaphoreType.DMA((32,))],
        compiler_params=params(),
        cost_estimate=estimate(1, 1),
        name="out",
    )(tab, lengths, mixture, frames, cotangent, *vectors, *pieces)


def up_kernel(counts, base, tab, normed, result, up_bias, *rest):
    count_up, count_earlier, count_grad = counts
    up_pieces, rest = rest[:count_up], rest[count_up + count_earlier :]
    active, slope = rest[:2]
    grads, rest = rest[2 : 2 + count_grad], rest[2 + count_grad :]
    weight, staged, sems_up, sems_grad = rest
    step = pl.program_id(0)
    steps = pl.num_programs(0)
    extent = normed.shape[0]

    def fetch(index):
        slot = lax.rem(index, 2)
        return load_columns(
            up_pieces, tab, base + index, weight.at[slot], sems_up.at[slot], TILE
        )

    def send(index):
        slot = lax.rem(index, 2)
        return store_row_pair(grads, tab, base + index, staged.at[slot], sems_grad.at[slot])

    @pl.when(step == 0)
    def _():
        start(fetch(step))

    @pl.when(step + 1 < steps)
    def _():
        start(fetch(step + 1))

    wait(fetch(step))
    now = lax.rem(step, 2)

    def widen(rows, carry):
        hidden = dot(normed[rows, :], weight[now], 1, 0) + up_bias[...]
        value, grade = gelu_parts(hidden)
        active[rows, :] = value.astype(BF)
        slope[rows, :] = grade.astype(BF)
        return carry

    chunks(extent, ROWS, widen)

    @pl.when(step >= 2)
    def _():
        wait(send(step - 2))

    def weigh(columns, carry):
        staged[now, columns, :] = dot(active[:, columns], result[...], 0, 0).astype(BF)
        return carry

    chunks(TILE, ROWS, weigh)
    start(send(step))

    @pl.when(step == steps - 1)
    def _():
        wait(send(step - 1))
        wait(send(step))


def up_call(tab, normed, result, up_bias, up_pieces, spread, sizes, part_of=(0, 1), earlier=()):
    extent, model = normed.shape
    hidden = 4 * model
    grads = gradient_shapes(spread, hidden, model, *sizes)
    steps = hidden // TILE // part_of[1]
    base = steps * part_of[0]
    tile = pl.BlockSpec((extent, TILE), lambda i: (0, base + i))
    aliases = {4 + len(up_pieces) + n: n for n in range(len(earlier))}
    return pl.pallas_call(
        functools.partial(up_kernel, (len(up_pieces), len(earlier), len(grads)), base),
        grid=(steps,),
        in_specs=[SMEM, whole(extent, model), whole(extent, model)]
        + [pl.BlockSpec((1, TILE), lambda i: (0, base + i))]
        + [ANY] * (len(up_pieces) + len(earlier)),
        out_specs=[tile, tile] + [ANY] * len(grads),
        out_shape=[
            jax.ShapeDtypeStruct((extent, hidden), BF),
            jax.ShapeDtypeStruct((extent, hidden), BF),
        ]
        + grads,
        input_output_aliases=aliases,
        scratch_shapes=[
            pltpu.VMEM((2, model, TILE), BF),
            pltpu.VMEM((2, TILE, model), BF),
            pltpu.SemaphoreType.DMA((2, 8)),
            pltpu.SemaphoreType.DMA((2, 8)),
        ],
        compiler_params=params(),
        cost_estimate=estimate(16 * extent * model * model / part_of[1], 50e6, extent * hidden),
        name="up",
    )(tab, normed, result, up_bias, *up_pieces, *earlier)


def back_kernel(counts, tab, mixture, middle, normed, d_result, slope, *rest):
    count_out, count_up, count_down, count_grad = counts
    gain = rest[0]
    rest = rest[1:]
    out_pieces, rest = rest[:count_out], rest[count_out:]
    up_pieces, rest = rest[:count_up], rest[count_up:]
    down_pieces, rest = rest[:count_down], rest[count_down:]
    d_middle, d_mixture, up_bias, gain_grad, shift_grad, out_bias = rest[:6]
    rest = rest[6:]
    grads, rest = rest[:count_grad], rest[count_grad:]
    (
        mixed,
        out_weight,
        total,
        unit_rows,
        result,
        down,
        up,
        d_hidden,
        d_normed,
        staged,
        sems_in,
        sems_out,
        sems_down,
        sems_up,
        sems_grad,
    ) = rest
    spread = len(grads[0].shape) == 4
    if spread:
        up_grads = out_grads = grads
    else:
        up_grads, out_grads = grads[:1], grads[1:]
    step = pl.program_id(0)
    steps = pl.num_programs(0)
    extent, model = result.shape
    width = model // 4

    def fetch(index):
        slot = index % 2
        copies = load_rows(down_pieces, tab, index, down.at[slot], sems_down.at[slot])
        block = tab[T_PAIR + index]
        copies += load_columns(up_pieces, tab, block, up.at[slot], sems_up.at[slot], TILE)
        return copies

    def send(index):
        slot = index % 2
        block = tab[T_PAIR + index]
        return store_column_block(
            up_grads, tab, block, staged.at[slot], sems_grad.at[slot], TILE
        )

    def send_out(block):
        return store_column_block(
            out_grads,
            tab,
            block,
            staged.at[0, :, pl.ds(block * width, width)],
            sems_out.at[pl.ds(block * 8, 8)],
            width,
            TILE if spread else 0,
        )

    def early(n):
        pair = ((d_result, result), (normed, unit_rows))[n]
        return pltpu.make_async_copy(*pair, sems_in.at[n])

    def late():
        return [
            pltpu.make_async_copy(middle, total, sems_in.at[2]),
            pltpu.make_async_copy(mixture, mixed, sems_in.at[3]),
        ] + load_all(out_pieces, tab, out_weight, sems_out, width, TILE)

    now = lax.rem(step, 2)

    @pl.when(step == 0)
    def _():
        early(0).start()
        start(fetch(0))
        early(1).start()
        early(0).wait()
        d_normed[...] = jnp.zeros_like(d_normed)

    def arrive(index):
        if index == 2:
            start(late())
        if index + 1 < 4:
            start(fetch(index + 1))
        wait(fetch(index))
        if index >= 2:
            wait(send(index - 2))

    for index in range(4):
        pl.when(step == index)(functools.partial(arrive, index))

    def shrink(rows, sums):
        d_active = dot(result[rows, :], down[now], 1, 1)
        piece = (d_active * slope[rows, :].astype(F32)).astype(BF)
        d_hidden[rows, :] = piece
        return sums + piece.astype(F32).sum(0, keepdims=True)

    up_bias[...] = chunks(extent, ROWS, shrink, jnp.zeros((1, TILE), F32))

    @pl.when(step == 0)
    def _():
        early(1).wait()

    def weigh(columns, carry):
        staged[now, columns, :] = dot(unit_rows[:, columns], d_hidden[...], 0, 0).astype(BF)
        return carry

    chunks(model, ROWS, weigh)
    for index in range(4):
        pl.when(step == index)(lambda index=index: start(send(index)))

    def widen(rows, carry):
        d_normed[rows, :] += dot(d_hidden[rows, :], up[now], 1, 1)
        return carry

    @pl.when(step < steps - 1)
    def _():
        chunks(extent, ROWS, widen)

    @pl.when(step == steps - 1)
    def _():
        wait(late())
        none = jnp.zeros((1, model), F32)

        def norm(rows, sums):
            grade = d_normed[rows, :] + dot(d_hidden[rows, :], up[now], 1, 1)
            unit, scale = normalise(total[rows, :])
            gains = sums[0] + (grade * unit).sum(0, keepdims=True)
            shifts = sums[1] + grade.sum(0, keepdims=True)
            grade = grade * gain[...]
            level = jnp.mean(grade, axis=-1, keepdims=True)
            tilt = jnp.mean(grade * unit, axis=-1, keepdims=True)
            d_total = result[rows, :].astype(F32) + scale * (grade - level - unit * tilt)
            d_middle[rows, :] = d_total
            branch = d_total.astype(BF)
            unit_rows[rows, :] = branch
            return gains, shifts, sums[2] + branch.astype(F32).sum(0, keepdims=True)

        sums = chunks(extent, ROWS, norm, (none, none, none))
        gain_grad[...], shift_grad[...], out_bias[...] = sums
        wait(send(2))

        def weigh_out(rows, carry):
            staged[0, rows, :] = dot(mixed[rows, :], unit_rows[...], 1, 0).astype(BF)
            return carry

        chunks(model, ROWS, weigh_out)
        for block in range(4):
            start(send_out(block))

        def turn(rows, carry):
            d_mixture[rows, :] = dot(out_weight[rows, :], unit_rows[...], 1, 1).astype(BF)
            return carry

        chunks(model, ROWS, turn)
        wait(send(3))
        for block in range(4):
            wait(send_out(block))


def back_call(tab, mixture, middle, normed, d_result, slope, gain, pieces, spread, sizes):
    out_pieces, up_pieces, down_pieces = pieces
    model, extent = mixture.shape
    hidden = slope.shape[1]
    if spread:
        grads = gradient_shapes(spread, model, hidden + model, *sizes)
    else:
        grads = gradient_shapes(spread, model, hidden, *sizes)
        grads += gradient_shapes(spread, model, model, *sizes)
    steps = hidden // TILE
    grid = pltpu.PrefetchScalarGridSpec(
        num_scalar_prefetch=1,
        grid=(steps,),
        in_specs=[ANY, ANY, ANY, ANY]
        + [pl.BlockSpec((extent, TILE), lambda i, tab: (0, tab[T_PAIR + i]))]
        + [whole(1, model)]
        + [ANY] * (len(out_pieces) + len(up_pieces) + len(down_pieces)),
        out_specs=[
            whole(extent, model),
            whole(model, extent),
            pl.BlockSpec((1, TILE), lambda i, tab: (0, tab[T_PAIR + i])),
            whole(1, model),
            whole(1, model),
            whole(1, model),
        ]
        + [ANY] * len(grads),
        scratch_shapes=[
            pltpu.VMEM((model, extent), BF),
            pltpu.VMEM((model, model), BF),
            pltpu.VMEM((extent, model), F32),
            pltpu.VMEM((extent, model), BF),
            pltpu.VMEM((extent, model), BF),
            pltpu.VMEM((2, TILE, model), BF),
            pltpu.VMEM((2, model, TILE), BF),
            pltpu.VMEM((extent, TILE), BF),
            pltpu.VMEM((extent, model), F32),
            pltpu.VMEM((2, model, TILE), BF),
            pltpu.SemaphoreType.DMA((4,)),
            pltpu.SemaphoreType.DMA((32,)),
            pltpu.SemaphoreType.DMA((2, 8)),
            pltpu.SemaphoreType.DMA((2, 8)),
            pltpu.SemaphoreType.DMA((2, 8)),
        ],
    )
    return pl.pallas_call(
        functools.partial(
            back_kernel, (len(out_pieces), len(up_pieces), len(down_pieces), len(grads))
        ),
        grid_spec=grid,
        out_shape=[
            jax.ShapeDtypeStruct((extent, model), F32),
            jax.ShapeDtypeStruct((model, extent), BF),
            vec(hidden),
            vec(model),
            vec(model),
            vec(model),
        ]
        + grads,
        compiler_params=params(),
        cost_estimate=estimate(28 * extent * model * model, 60e6),
        name="back",
    )(
        tab,
        mixture,
        middle,
        normed,
        d_result,
        slope,
        gain,
        *out_pieces,
        *up_pieces,
        *down_pieces,
    )


def attention_back_kernel(
    group,
    block,
    lengths,
    query,
    key,
    value,
    mixture,
    d_mixture,
    totals,
    *rest,
):
    d_project, keys, queries, causal, d_keys, d_values = rest[-6:]
    extent = query.shape[1]

    @pl.when(pl.program_id(0) == 0)
    def _():
        causal[...] = causal_bias(block)

    key_rows, query_rows = extend_rows(lengths[0], extent)
    for head in range(group):
        part = pl.ds(HEAD * head, HEAD)
        keys[head, :HEAD, :] = key[part, :]
        keys[head, HEAD:, :] = key_rows
        queries[head, :HEAD, :] = query[part, :]
        queries[head, HEAD:, :] = query_rows
    for head in range(group):
        part = pl.ds(HEAD * head, HEAD)
        for tile in range(extent // block):
            place = pl.ds(tile * block, block)
            own = queries[head, :, place]
            grade = d_mixture[part, place]
            center = (grade.astype(F32) * mixture[part, place].astype(F32)).sum(0, keepdims=True)
            total = totals[0, pl.ds(head, 1), place]
            d_query = jnp.zeros((HEAD, block), F32)
            for other in range(tile + 1):
                span = pl.ds(other * block, block)
                score = dot(keys[head, :, span], own, 0, 0)
                if other == tile:
                    score = score + causal[...]
                weight = jnp.exp2(score * (SCALE * LOG2E) - total)
                d_weight = dot(value[part, span], grade, 0, 0)
                d_score = (weight * (d_weight - center)).astype(BF)
                d_value = dot(grade, weight.astype(BF), 1, 1)
                d_key = dot(query[part, place], d_score, 1, 1)
                d_query = d_query + dot(key[part, span], d_score, 1, 0)
                if other == tile:
                    d_values[:, span] = d_value
                    d_keys[:, span] = d_key
                else:
                    d_values[:, span] += d_value
                    d_keys[:, span] += d_key
            d_project[0, part, place] = (d_query * SCALE).astype(BF)
        d_project[1, part, :] = (d_keys[...] * SCALE).astype(BF)
        d_project[2, part, :] = d_values[...].astype(BF)


def attention_back_call(
    lengths, project, mixture, d_mixture, totals, base=0, ending=HEADS // 2, earlier=()
):
    extent = project.shape[1]
    group, block = 2, min(512, extent)
    size, groups = HEAD * group, HEADS // group
    steps = ending - base

    def part(section):
        return pl.BlockSpec((size, extent), lambda i: (i + base + section * groups, 0))

    pairs = extent * extent * 5 // 8
    return pl.pallas_call(
        functools.partial(attention_back_kernel, group, block),
        grid=(steps,),
        in_specs=[SMEM, part(0), part(1), part(2), part(0), part(0)]
        + [pl.BlockSpec((1, group, extent), lambda i: (i + base, 0, 0))]
        + [ANY] * len(earlier),
        out_specs=pl.BlockSpec((3, size, extent), lambda i: (0, i + base, 0)),
        out_shape=jax.ShapeDtypeStruct((3, HEADS * HEAD, extent), BF),
        input_output_aliases={7: 0} if earlier else {},
        scratch_shapes=[
            pltpu.VMEM((group, HEAD + 16, extent), BF),
            pltpu.VMEM((group, HEAD + 16, extent), BF),
            pltpu.VMEM((block, block), F32),
            pltpu.VMEM((HEAD, extent), F32),
            pltpu.VMEM((HEAD, extent), F32),
        ],
        compiler_params=params(),
        cost_estimate=estimate(4 * HEADS * pairs * HEAD * steps / groups, 1e6),
        name="attention_back",
    )(lengths, project, project, project, mixture, d_mixture, totals, *earlier)


def attend_grad_kernel(count_grad, tab, d_project, normed, *rest):
    bias_grad = rest[0]
    grads, rest = rest[1 : 1 + count_grad], rest[1 + count_grad :]
    staged, sems_grad = rest
    step = pl.program_id(0)
    steps = pl.num_programs(0)
    extent, model = normed.shape
    width = d_project.shape[0]

    def send(block):
        slot = lax.rem(block, 2)
        return store_column_block(grads, tab, block, staged.at[slot], sems_grad.at[slot], width)

    @pl.when(step >= 2)
    def _():
        wait(send(step - 2))

    now = lax.rem(step, 2)

    def weigh(columns, carry):
        staged[now, columns, :] = dot(normed[:, columns], d_project[...], 0, 1).astype(BF)
        return carry

    chunks(model, ROWS, weigh)
    start(send(step))
    bias_grad[...] = dot(jnp.ones((8, extent), BF), d_project[...], 1, 1)[:1, :]

    @pl.when(step == steps - 1)
    def _():
        wait(send(step - 1))
        wait(send(step))


def attend_grad_call(tab, d_project, normed, spread, sizes):
    extent, model = normed.shape
    width = 3 * model // 4
    grads = gradient_shapes(spread, model, 3 * model, *sizes)
    return pl.pallas_call(
        functools.partial(attend_grad_kernel, len(grads)),
        grid=(4,),
        in_specs=[SMEM, pl.BlockSpec((width, extent), lambda i: (i, 0)), whole(extent, model)],
        out_specs=[pl.BlockSpec((1, width), lambda i: (0, i))] + [ANY] * len(grads),
        out_shape=[vec(3 * model)] + grads,
        scratch_shapes=[
            pltpu.VMEM((2, model, width), BF),
            pltpu.SemaphoreType.DMA((2, 8)),
        ],
        compiler_params=params(),
        cost_estimate=estimate(6 * extent * model * model, 14e6),
        name="attend_grad",
    )(tab, d_project, normed)


def first_kernel(count_in, tab, d_project, frames, d_middle, gain, *rest):
    pieces, rest = rest[:count_in], rest[count_in:]
    bias_grad, *early = rest[:6]
    d_frames, small, weight, total, d_normed, sems, sem_total = rest[6:]
    step = pl.program_id(0)
    steps = pl.num_programs(0)
    extent, model = frames.shape
    width = d_project.shape[0]

    def fetch(index):
        slot = index % 2
        return load_slot(pieces, tab, index, weight.at[slot], sems.at[slot], width)

    def late():
        return pltpu.make_async_copy(d_middle, total, sem_total)

    @pl.when(step == 0)
    def _():
        start(fetch(0))
        late().start()
        d_normed[...] = jnp.zeros_like(d_normed)

    def arrive(index):
        if index + 1 < 4:
            start(fetch(index + 1))
        wait(fetch(index))

    for index in range(4):
        pl.when(step == index)(functools.partial(arrive, index))
    now = lax.rem(step, 2)

    def widen(rows, carry):
        d_normed[rows, :] += dot(d_project[:, rows], weight[now], 0, 1)
        return carry

    @pl.when(step < steps - 1)
    def _():
        chunks(extent, ROWS, widen)

    @pl.when(step == steps - 1)
    def _():
        late().wait()
        none = jnp.zeros((1, model), F32)

        def norm(rows, sums):
            grade = d_normed[rows, :] + dot(d_project[:, rows], weight[now], 0, 1)
            unit, scale = normalise(frames[rows, :].astype(F32))
            gains = sums[0] + (grade * unit).sum(0, keepdims=True)
            shifts = sums[1] + grade.sum(0, keepdims=True)
            grade = grade * gain[...]
            level = jnp.mean(grade, axis=-1, keepdims=True)
            tilt = jnp.mean(grade * unit, axis=-1, keepdims=True)
            d_frames[rows, :] = (total[rows, :] + scale * (grade - level - unit * tilt)).astype(BF)
            return gains, shifts

        gains, shifts = chunks(extent, ROWS, norm, (none, none))
        bias = bias_grad[...]
        vectors = [gains, shifts, bias[:, :model], bias[:, 2 * model :]]
        vectors += [vector[...] for vector in early]
        place = 0
        for vector in vectors:
            for column in range(0, vector.shape[1], 128):
                small[place : place + 1, :] = vector[:, column : column + 128]
                place += 1


def small_kernel(*refs):
    *terms, a, b, c, d, e, f, g, h = refs
    terms = [term[...] for term in terms]
    total = tree_sum(terms)
    place = 0
    for out in (a, b, c, d, e, f, g, h):
        out[...] = total[place : place + out.shape[0], :]
        place += out.shape[0]


def small_call(terms):
    unit = terms[0].shape[0] // 12
    sizes = [unit, unit, 2 * unit, unit, unit, unit, unit, 4 * unit]
    return pl.pallas_call(
        small_kernel,
        out_shape=[jax.ShapeDtypeStruct((size, 128), F32) for size in sizes],
        name="small",
    )(*terms)


def first_call(tab, d_project, frames, d_middle, gain, pieces, vectors):
    extent, model = frames.shape
    width = 3 * model // 4
    count = model + sum(vector.shape[1] for vector in vectors)
    grid = pltpu.PrefetchScalarGridSpec(
        num_scalar_prefetch=1,
        grid=(4,),
        in_specs=[pl.BlockSpec((width, extent), lambda i, tab: (tab[T_COL + i], 0))]
        + [whole(extent, model), ANY, whole(1, model)]
        + [ANY] * len(pieces)
        + [whole(*vector.shape) for vector in vectors],
        out_specs=[whole(extent, model), whole(count // 128, 128)],
        scratch_shapes=[
            pltpu.VMEM((2, model, width), BF),
            pltpu.VMEM((extent, model), F32),
            pltpu.VMEM((extent, model), F32),
            pltpu.SemaphoreType.DMA((2, 8)),
            pltpu.SemaphoreType.DMA,
        ],
    )
    return pl.pallas_call(
        functools.partial(first_kernel, len(pieces)),
        grid_spec=grid,
        out_shape=[
            jax.ShapeDtypeStruct((extent, model), BF),
            jax.ShapeDtypeStruct((count // 128, 128), F32),
        ],
        compiler_params=params(),
        cost_estimate=estimate(6 * extent * model * model, 24e6),
        name="first",
    )(tab, d_project, frames, d_middle, gain, *pieces, *vectors)


def down_kernel(count, base, ending, tab, active, middle, bias, *rest):
    pieces = rest[:count]
    frames_out, weight, total, sems = rest[count:]
    step = pl.program_id(0)
    steps = pl.num_programs(0)

    def fetch(index):
        slot = (index - base) % 2
        return load_rows(pieces, tab, index, weight.at[slot], sems.at[slot])

    def arrive(index):
        if index == base:
            start(fetch(index))
        if index + 1 < ending:
            start(fetch(index + 1))
        wait(fetch(index))

    for index in range(base, ending):
        pl.when(step == index - base)(functools.partial(arrive, index))

    @pl.when(step == 0)
    def _():
        total[...] = middle[...] + bias[...] if base == 0 else middle[...]

    def widen(rows, carry):
        total[rows, :] += dot(active[rows, :], weight[lax.rem(step, 2)], 1, 0)
        return carry

    chunks(total.shape[0], ROWS, widen)

    @pl.when(step == steps - 1)
    def _():
        frames_out[...] = total[...].astype(frames_out.dtype)


def down_call(tab, active, middle, bias, pieces, part_of=(0, 1)):
    extent, hidden = active.shape
    model = middle.shape[1]
    steps = hidden // TILE // part_of[1]
    base = steps * part_of[0]
    last = part_of[0] + 1 == part_of[1]
    grid = pltpu.PrefetchScalarGridSpec(
        num_scalar_prefetch=1,
        grid=(steps,),
        in_specs=[pl.BlockSpec((extent, TILE), lambda i, tab: (0, tab[T_PAIR + base + i]))]
        + [whole(extent, model), whole(1, model)]
        + [ANY] * len(pieces),
        out_specs=whole(extent, model),
        scratch_shapes=[
            pltpu.VMEM((2, TILE, model), BF),
            pltpu.VMEM((extent, model), F32),
            pltpu.SemaphoreType.DMA((2, 8)),
        ],
    )
    return pl.pallas_call(
        functools.partial(down_kernel, len(pieces), base, base + steps),
        grid_spec=grid,
        out_shape=jax.ShapeDtypeStruct((extent, model), BF if last else F32),
        compiler_params=params(),
        cost_estimate=estimate(8 * extent * model * model, 24e6),
        name="down",
    )(tab, active, middle, bias, *pieces)


def gather_plain(weight):
    wide = lax.all_gather(weight, "inner", axis=1, tiled=True)
    return [lax.all_gather(wide, "dp", axis=0, tiled=True)]


def scatter_plain(grads):
    wide = lax.psum_scatter(grads[0], "dp", scatter_dimension=0, tiled=True)
    return lax.psum_scatter(wide, "inner", scatter_dimension=1, tiled=True).astype(F32)


CORE, NEAR, FAR = 0, 1, 2


def swap(value, way):
    flips = {CORE: (1, 1), NEAR: (2, 4), FAR: (4, 2)}[way]
    return lax.ppermute(value, "dp", [(d, d ^ flips[d & 1]) for d in range(8)])


def shift(value, amount):
    return lax.ppermute(value, "inner", [(i, (i + amount) & 3) for i in range(4)])


def after(value, *done):
    return lax.optimization_barrier((value, done))[0]


def stack_spread(block):
    return jnp.stack([block] + [shift(block, amount) for amount in (1, 2, 3)])


def added(*values):
    total = values[0].astype(F32)
    for value in values[1:]:
        total = total + value.astype(F32)
    return total


def add_kernel(count, *refs):
    total = added(*[ref[...] for ref in refs[:count]])
    outs = refs[count:]
    if len(outs) == 1:
        outs[0][...] = total.reshape(outs[0].shape).astype(BF)
        return
    for index, out in enumerate(outs):

        @pl.when(pl.program_id(0) == index)
        def _(out=out):
            out[...] = total.reshape(out.shape).astype(out.dtype)


def add_call(terms, outs, grid):
    rows, columns = terms[0][0].shape[-2:]
    specs = []
    for term, place in terms:
        if term.ndim == 3:
            specs.append(pl.BlockSpec((1, rows, columns), lambda *at: (at[-1], 0, 0)))
        elif place is None:
            specs.append(pl.BlockSpec((1, 1, rows, columns), lambda p, k: (p, k, 0, 0)))
        else:
            specs.append(
                pl.BlockSpec((1, 1, rows, columns), lambda k, place=place: (place, k, 0, 0))
            )
    if len(outs) == 1:
        lead = (1,) * len(grid)
        out_specs = [pl.BlockSpec(lead + (rows, columns), lambda *at: at + (0, 0))]
    else:
        out_specs = [whole(rows, columns)] * len(outs)

    def kernel(*refs):
        ins = [
            ref.at[0] if len(ref.shape) == 3 else ref.at[0, 0] for ref in refs[: len(terms)]
        ]
        add_kernel(len(terms), *ins, *refs[len(terms) :])

    return pl.pallas_call(
        kernel,
        grid=grid,
        in_specs=specs,
        out_specs=out_specs,
        out_shape=outs,
        compiler_params=params(),
        cost_estimate=estimate(1e10, 1e7),
        name="add",
    )(*[term for term, _ in terms])


def add_first(keep, core):
    return added(keep[:2], core[:2]).astype(BF)


def add_second(keep, core, link):
    return added(keep[2], core[2], link[0]).astype(BF)


def add_third(keep, core, link, last):
    blocks = [added(keep[3, k], core[3, k], link[1, k], last[k]) for k in range(4)]
    return [blocks[0]] + [block.astype(BF) for block in blocks[1:]]


def add_third_kernel(keep, core, link, last):
    shapes = [jax.ShapeDtypeStruct(keep.shape[2:], F32)]
    shapes += [jax.ShapeDtypeStruct(keep.shape[2:], BF)] * 3
    return add_call([(keep, 3), (core, 3), (link, 1), (last, None)], shapes, (4,))


def shift_parts(parts):
    return [shift(parts[k], k) for k in (1, 2, 3)]


def exchange(values, axis, size):
    return [values] + [
        lax.ppermute(values, axis, [(i, i ^ flip) for i in range(size)])
        for flip in range(1, size)
    ]


def tree_sum(terms):
    while len(terms) > 1:
        terms = [terms[i] + terms[i + 1] for i in range(0, len(terms), 2)]
    return terms[0]


def shards(
    spread,
    sizes,
    frames_in,
    lengths,
    first_gain,
    first_shift,
    attend_weight,
    attend_bias,
    output_weight,
    output_bias,
    second_gain,
    second_shift,
    up_weight,
    up_bias,
    down_weight,
    down_bias,
    cotangent,
):
    _, extent, model = frames_in.shape
    frames = frames_in.reshape(extent, model)
    upstream = cotangent.reshape(extent, model)
    tab = make_table(spread, True)
    tab_plain = make_table(spread, False)

    def row(vector):
        return vector.reshape(1, -1)

    if not spread:
        attend_pieces = gather_plain(attend_weight)
        out_pieces = gather_plain(output_weight)
        up_pieces = gather_plain(up_weight)
        down_pieces = gather_plain(down_weight)
    else:
        others = [shift(attend_weight, amount) for amount in (1, 2, 3)]
        near, far = swap(attend_weight, NEAR), swap(attend_weight, FAR)
        others = jnp.stack(others)
        far, near = after((far, near), near, far)
        diagonal = swap(near, FAR)
        attend_pieces = [attend_weight, near, far, diagonal]
        attend_pieces += [swap(piece, CORE) for piece in attend_pieces]
        others = after(others, diagonal)
        near, far = swap(others, NEAR), swap(others, FAR)
        up_block = after(jnp.concatenate([up_weight, output_weight], axis=1), others)
        up_own = lax.all_gather(up_block, "inner")
        near, far = after((near, far), near, far)
        diagonal = swap(near, FAR)
        others = [others, near, far, diagonal]
        attend_pieces += others + [swap(piece, CORE) for piece in others]
        up_own = after(up_own, diagonal)
        up_near, up_far = swap(up_own, NEAR), swap(up_own, FAR)
        down_own = lax.all_gather(after(down_weight, up_own), "inner")
    bias_row = jnp.concatenate([attend_bias[0], jnp.zeros_like(attend_bias[0]), attend_bias[1]])
    vectors = (row(first_gain), row(first_shift), row(bias_row))
    tokens = after(frames, up_own) if spread else frames
    normed, project = project_call(tab, tokens, *vectors, attend_pieces)
    if spread:
        mixture, totals = attention_call(lengths, after(project, up_own), (0, 2))
        up_near, up_far = after((up_near, up_far), totals)
        up_diagonal = swap(up_near, FAR)
        ahead = [swap(piece, CORE) for piece in (after(up_own, totals), up_near, up_far)]
        mixture, totals = attention_call(
            lengths, after(project, up_near, up_far), (1, 2), (mixture, totals)
        )
        up_pieces = [up_own, up_near, up_far, up_diagonal]
        up_pieces += ahead + [swap(after(up_diagonal, totals), CORE)]
        out_pieces = up_pieces
    else:
        mixture, totals = attention_call(lengths, project)
    vectors = (row(output_bias), row(second_gain), row(second_shift))
    middle, normed_two, d_result, grad_down_bias = out_call(
        tab_plain, lengths, mixture, frames, upstream, vectors, out_pieces
    )
    if spread:
        down_own = after(down_own, normed_two)
        down_near, down_far = swap(down_own, NEAR), swap(down_own, FAR)
        *halves, half_grad = up_call(
            tab_plain, normed_two, d_result, row(up_bias), up_pieces, False, sizes, (0, 2)
        )
        down_near, down_far = after((down_near, down_far), halves)
        down_diagonal = swap(down_near, FAR)
        ahead = [swap(piece, CORE) for piece in (after(down_own, totals), down_near, down_far)]
        active, slope, *down_grads = up_call(
            tab_plain,
            after(normed_two, down_near, down_far),
            d_result,
            row(up_bias),
            up_pieces,
            False,
            sizes,
            (1, 2),
            (*halves, half_grad),
        )
    else:
        active, slope, *down_grads = up_call(
            tab_plain, normed_two, d_result, row(up_bias), up_pieces, False, sizes
        )
    if spread:
        down_pieces = [down_own, down_near, down_far, down_diagonal]
        down_pieces += ahead + [swap(after(down_diagonal, slope), CORE)]
        down_wide = lax.psum_scatter(down_grads[0], "dp", scatter_dimension=0, tiled=True)
    else:
        down_owned = scatter_plain(down_grads)
    (
        d_middle,
        d_mixture,
        grad_up_bias,
        grad_second_gain,
        grad_second_shift,
        grad_output_bias,
        *back_grads,
    ) = back_call(
        tab_plain,
        mixture,
        middle,
        normed_two,
        d_result,
        slope,
        row(second_gain),
        (out_pieces, up_pieces, down_pieces),
        spread,
        sizes,
    )
    early = [grad_output_bias, grad_second_gain, grad_second_shift, grad_down_bias, grad_up_bias]
    if spread:
        back_keep, back_send = back_grads
        back_core = swap(back_send, CORE)
        d_project = attention_back_call(lengths, project, mixture, d_mixture, totals, 0, 2)
        back_core = after(back_core, d_project)
        back_first = add_first(back_keep, back_core)
        back_link = swap(back_first, FAR)
        d_mixture = after(d_mixture, back_first)
        d_project = attention_back_call(
            lengths, project, mixture, d_mixture, totals, 2, HEADS // 2, (d_project,)
        )
        back_link, down_wide = after((back_link, down_wide), d_project)
        down_owned = lax.psum_scatter(down_wide, "inner", scatter_dimension=1, tiled=True)
        back_second = add_second(back_keep, back_core, back_link)
        back_last = swap(back_second, NEAR)
        d_rows = after(d_project, back_second, down_wide).reshape(3 * model, extent)
        grad_bias, attend_keep, attend_send = attend_grad_call(tab, d_rows, normed, spread, sizes)
        attend_core = swap(attend_send, CORE)
        back_last = after(back_last, grad_bias)
        back_parts = add_third_kernel(back_keep, back_core, back_link, back_last)
        back_others = shift_parts(back_parts)
        attend_core = after(attend_core, back_parts)
        attend_first = add_first(attend_keep, attend_core)
        attend_link = swap(attend_first, FAR)
        d_frames, small = first_call(
            tab,
            after(d_rows, attend_first),
            frames,
            d_middle,
            row(first_gain),
            attend_pieces,
            [grad_bias] + early,
        )
        attend_link, down_owned = after((attend_link, down_owned), d_frames)
        attend_second = add_second(attend_keep, attend_core, attend_link)
        attend_last = swap(attend_second, NEAR)
        small_terms = exchange(small, "inner", 4)
        active, middle = after((active, middle), attend_second, down_owned)
        frames_out = down_call(tab_plain, active, middle, row(down_bias), down_pieces)
        attend_last, back_others, small_terms = after(
            (attend_last, back_others, small_terms), frames_out
        )
        back_owned = added(back_parts[0], *back_others)
        small = tree_sum(small_terms)
        attend_parts = add_third(attend_keep, attend_core, attend_link, attend_last)
        attend_parts, small = after((attend_parts, small), back_owned, small, attend_parts)
        others = shift_parts(attend_parts)
        small_terms = exchange(small, "dp", 8)
        attend_owned = added(attend_parts[0], *others)
        small = small_call(after(small_terms, attend_owned))
        down_owned = down_owned.astype(F32)
        up_owned, output_owned = back_owned[:, :TILE], back_owned[:, TILE:]
    else:
        d_project = attention_back_call(lengths, project, mixture, d_mixture, totals)
        d_rows = d_project.reshape(3 * model, extent)
        grad_bias, *attend_grads = attend_grad_call(tab, d_rows, normed, spread, sizes)
        d_frames, small = first_call(
            tab,
            d_rows,
            frames,
            d_middle,
            row(first_gain),
            attend_pieces,
            [grad_bias] + early,
        )
        frames_out = down_call(tab_plain, active, middle, row(down_bias), down_pieces)
        up_owned = scatter_plain(back_grads[:1])
        output_owned = scatter_plain(back_grads[1:])
        attend_owned = scatter_plain(attend_grads)
        small = small_call([lax.psum(small, ("dp", "inner"))])
    small = [vector.reshape(-1) for vector in small]

    return (
        frames_out.reshape(frames_in.shape),
        d_frames.reshape(frames_in.shape),
        small[0],
        small[1],
        attend_owned,
        small[2].reshape(2, model),
        output_owned,
        small[3],
        small[4],
        small[5],
        up_owned,
        small[7],
        down_owned,
        small[6],
    )


def solution(mesh):
    sizes = (mesh.shape["dp"], mesh.shape["inner"])
    spread = sizes == (8, 4)
    return jax.shard_map(
        functools.partial(shards, spread, sizes),
        mesh=mesh,
        in_specs=(
            P(("dp", "inner"), None, None),
            P(("dp", "inner")),
            P(),
            P(),
            P("dp", "inner"),
            P(),
            P("dp", "inner"),
            P(),
            P(),
            P(),
            P("dp", "inner"),
            P(),
            P("dp", "inner"),
            P(),
            P(("dp", "inner"), None, None),
        ),
        out_specs=(
            P(("dp", "inner"), None, None),
            P(("dp", "inner"), None, None),
            P(),
            P(),
            P("dp", "inner"),
            P(),
            P("dp", "inner"),
            P(),
            P(),
            P(),
            P("dp", "inner"),
            P(),
            P("dp", "inner"),
            P(),
        ),
        check_vma=False,
    )
```

```python
import functools

import jax
import jax.numpy as jnp
from jax import lax
from jax.experimental import pallas as pl
from jax.experimental.pallas import tpu as pltpu
from jax.sharding import PartitionSpec as P

HEADS = 16
HEAD = 64
TILE = 1024
ROWS = 256
LOG2E = 1.4426950408889634
MASKED = -1e30
SCALE = HEAD ** (-0.5)
BF = jnp.bfloat16
F32 = jnp.float32
LIMIT = 60 * 2**20


def dot(left, right, on_left, on_right):
    return lax.dot_general(
        left, right, (((on_left,), (on_right,)), ((), ())), preferred_element_type=F32
    )


def normalise(values):
    center = values - jnp.mean(values, axis=-1, keepdims=True)
    spread = jnp.mean(center * center, axis=-1, keepdims=True)
    scale = lax.rsqrt(spread + 1e-05)
    return center * scale, scale


def params(name_limit=LIMIT):
    return pltpu.CompilerParams(vmem_limit_bytes=name_limit)


def estimate(flops, moved, exps=0):
    return pl.CostEstimate(
        flops=int(8 * flops), bytes_accessed=int(8 * moved), transcendentals=int(8 * exps)
    )


ANY = pl.BlockSpec(memory_space=pl.ANY)
SMEM = pl.BlockSpec(memory_space=pltpu.SMEM)


def whole(*shape):
    return pl.BlockSpec(shape, lambda *_: (0,) * len(shape))


def vec(size):
    return jax.ShapeDtypeStruct((1, size), F32)


PIECES = 8
SLOTS = 4
T_ROW = 0
T_COL = 8
T_SLOT_IN = 12
T_SLOT_OUT = 16
T_PAIR = 20
T_OUT = 24
T_PLACE = 32
T_CORE = 40
T_SIZE = 48


def make_table(spread, relative):
    if not spread:
        order = list(range(4))
        entries = [0] * T_SIZE
        entries[T_PAIR : T_PAIR + 4] = order
        entries[T_COL : T_COL + 4] = order
        return jnp.array(entries, jnp.int32)
    row = lax.axis_index("dp").astype(jnp.int32)
    column = lax.axis_index("inner").astype(jnp.int32)
    core = row & 1
    near = jnp.where(core == 0, 2, 4)
    far = 6 - near
    entries = [
        row,
        row ^ near,
        row ^ far,
        row ^ 6,
        row ^ 1,
        row ^ 1 ^ far,
        row ^ 1 ^ near,
        row ^ 7,
    ]
    if relative:
        entries += [(column - block) & 3 for block in range(4)] * 2
    else:
        entries += [0, 1, 2, 3] * 2
    entries += [(block - column) & 3 for block in range(4)]
    pair = row >> 1
    entries += [pair, pair ^ (near >> 1), pair ^ (far >> 1), pair ^ 3]
    for half in range(2):
        a, b = (far, near) if half == 0 else (near, far)
        own = row ^ half
        entries += [own ^ 6, own ^ a, own ^ b, own]
    for half in range(2):
        first = far if half == 0 else near
        for block in range(4):
            relative = (pair ^ block) << 1
            entries.append(
                jnp.where(
                    relative == 6,
                    0,
                    jnp.where(relative == 0, 3, jnp.where(relative == first, 1, 2)),
                )
            )
    entries += [core]
    entries += [jnp.int32(0)] * (T_SIZE - len(entries))
    return jnp.stack([jnp.asarray(entry, jnp.int32) for entry in entries])


def aligned(index, size):
    return pl.ds(pl.multiple_of(index * size, size), size)


def load_slot(pieces, tab, step, target, sems, width):
    if len(pieces) == 1:
        return load_columns(pieces, tab, tab[T_COL + step], target, sems, width)
    rows = pieces[0].shape[-2]
    copies = []
    for p in range(PIECES):
        source = pieces[p] if step == 0 else pieces[PIECES + p].at[step - 1]
        place = target.at[aligned(tab[T_ROW + p], rows), :]
        copies.append(pltpu.make_async_copy(source, place, sems.at[p]))
    return copies


def load_columns(pieces, tab, block, target, sems, width, first=0):
    if len(pieces) == 1:
        copies = [
            pltpu.make_async_copy(pieces[0].at[:, aligned(block, width)], target, sems.at[0])
        ]
        return copies
    slot = tab[T_SLOT_IN + block]
    rows = pieces[0].shape[1]
    return [
        pltpu.make_async_copy(
            pieces[p].at[slot, :, pl.ds(first, width)],
            target.at[aligned(tab[T_ROW + p], rows), :],
            sems.at[p],
        )
        for p in range(PIECES)
    ]


def load_rows(pieces, tab, step, target, sems):
    if len(pieces) == 1 and len(pieces[0].shape) == 2:
        return [
            pltpu.make_async_copy(
                pieces[0].at[aligned(tab[T_PAIR + step], TILE), :], target, sems.at[0]
            )
        ]
    rows, width = pieces[0].shape[-2:]
    if len(pieces) == 1:
        return [
            pltpu.make_async_copy(
                pieces[0].at[2 * tab[T_PAIR + step] + half, block],
                target.at[pl.ds(half * rows, rows), pl.ds(block * width, width)],
                sems.at[half * SLOTS + block],
            )
            for half in range(2)
            for block in range(4)
        ]
    partner = (4, 6, 5, 7)[step]
    copies = []
    for n, p in enumerate((step, partner)):
        half = tab[T_ROW + p] & 1
        for slot in range(SLOTS):
            copies.append(
                pltpu.make_async_copy(
                    pieces[p].at[slot],
                    target.at[aligned(half, rows), aligned(tab[T_COL + slot], width)],
                    sems.at[n * SLOTS + slot],
                )
            )
    return copies


def load_all(pieces, tab, target, sems, width, first=0):
    if len(pieces) == 1:
        return [pltpu.make_async_copy(pieces[0], target, sems.at[0])]
    rows = pieces[0].shape[1]
    return [
        pltpu.make_async_copy(
            pieces[p].at[slot, :, pl.ds(first, width)],
            target.at[aligned(tab[T_ROW + p], rows), aligned(tab[T_COL + slot], width)],
            sems.at[p * SLOTS + slot],
        )
        for p in range(PIECES)
        for slot in range(SLOTS)
    ]


def store_column_block(outs, tab, block, source, sems, width, first=0):
    if len(outs) == 1:
        return [pltpu.make_async_copy(source, outs[0].at[:, aligned(block, width)], sems.at[0])]
    rows = outs[0].shape[2]
    slot = tab[T_SLOT_OUT + block]
    return [
        pltpu.make_async_copy(
            source.at[aligned(tab[T_OUT + half * 4 + place], rows), :],
            outs[half].at[place, slot, :, pl.ds(first, width)],
            sems.at[half * 4 + place],
        )
        for half in range(2)
        for place in range(4)
    ]


def store_row_pair(outs, tab, pair, source, sems):
    if len(outs) == 1:
        return [pltpu.make_async_copy(source, outs[0].at[aligned(pair, TILE), :], sems.at[0])]
    rows, width = outs[0].shape[2:]
    copies = []
    for half in range(2):
        local = tab[T_CORE] ^ half
        for block in range(4):
            copies.append(
                pltpu.make_async_copy(
                    source.at[aligned(local, rows), pl.ds(block * width, width)],
                    outs[half].at[tab[T_PLACE + half * 4 + pair], tab[T_SLOT_OUT + block]],
                    sems.at[half * 4 + block],
                )
            )
    return copies


def chunks(extent, size, body, init=0):
    for first in range(0, extent, size):
        init = body(pl.ds(first, size), init)
    return init


def start(copies):
    for copy in copies:
        copy.start()


def wait(copies):
    for copy in copies:
        copy.wait()


def gradient_shapes(spread, rows, columns, dp, inner):
    if spread:
        return [jax.ShapeDtypeStruct((4, 4, rows // dp, columns // inner), BF)] * 2
    return [jax.ShapeDtypeStruct((rows, columns), BF)]


def project_kernel(count, tab, tokens, gain, shift, bias, *rest):
    pieces = rest[:count]
    normed, project, weight, sems = rest[count:]
    step = pl.program_id(0)
    width = project.shape[0]

    def fetch(index):
        slot = index % 2
        return load_slot(pieces, tab, index, weight.at[slot], sems.at[slot], width)

    @pl.when(step == 0)
    def _():
        start(fetch(0))

        def norm(rows, carry):
            unit, _ = normalise(tokens[rows, :].astype(F32))
            normed[rows, :] = (unit * gain[...] + shift[...]).astype(BF)
            return carry

        chunks(tokens.shape[0], ROWS, norm)

    def arrive(index):
        if index + 1 < 4:
            start(fetch(index + 1))
        wait(fetch(index))

    for index in range(4):
        pl.when(step == index)(functools.partial(arrive, index))

    column = jnp.transpose(jnp.broadcast_to(bias[...], (128, width)))[:, :1]

    project[...] = (dot(weight[lax.rem(step, 2)], normed[...], 0, 1) + column).astype(BF)


def project_call(tab, tokens, gain, shift, bias, pieces):
    extent, model = tokens.shape
    width = 3 * model // 4
    grid = pltpu.PrefetchScalarGridSpec(
        num_scalar_prefetch=1,
        grid=(4,),
        in_specs=[whole(extent, model), whole(1, model), whole(1, model)]
        + [pl.BlockSpec((1, width), lambda i, tab: (0, tab[T_COL + i]))]
        + [ANY] * len(pieces),
        out_specs=[
            whole(extent, model),
            pl.BlockSpec((width, extent), lambda i, tab: (tab[T_COL + i], 0)),
        ],
        scratch_shapes=[
            pltpu.VMEM((2, model, width), BF),
            pltpu.SemaphoreType.DMA((2, 8)),
        ],
    )
    return pl.pallas_call(
        functools.partial(project_kernel, len(pieces)),
        grid_spec=grid,
        out_shape=[
            jax.ShapeDtypeStruct((extent, model), BF),
            jax.ShapeDtypeStruct((3 * model, extent), BF),
        ],
        compiler_params=params(),
        cost_estimate=estimate(1e6, 1e4),
        name="project",
    )(tab, tokens, gain, shift, bias, *pieces)


def causal_bias(keys, queries):
    key = lax.broadcasted_iota(jnp.int32, (keys, queries), 0)
    query = lax.broadcasted_iota(jnp.int32, (keys, queries), 1)
    return jnp.where(key <= query, 0.0, MASKED)


def extend_rows(length, extent):
    first = lax.broadcasted_iota(jnp.int32, (16, extent), 0) == 0
    past = lax.broadcasted_iota(jnp.int32, (16, extent), 1) >= length
    key_rows = jnp.where(first & past, MASKED, 0.0).astype(BF)
    query_rows = jnp.where(first, 1.0, 0.0).astype(BF)
    return key_rows, query_rows


def attention_kernel(group, block, lengths, query, key, value, *rest):
    mixture, totals, keys, queries, causal = rest[-5:]
    extent = query.shape[1]

    half = block // 2

    @pl.when(pl.program_id(0) == 0)
    def _():
        causal[...] = causal_bias(half, block)

    key_rows, query_rows = extend_rows(lengths[0], extent)
    for head in range(group):
        part = pl.ds(HEAD * head, HEAD)
        keys[head, :HEAD, :] = key[part, :]
        keys[head, HEAD:, :] = key_rows
        queries[head, :HEAD, :] = query[part, :]
        queries[head, HEAD:, :] = query_rows
    for head in range(group):
        part = pl.ds(HEAD * head, HEAD)
        for tile in range(extent // block):
            first = tile * block
            place = pl.ds(first, block)
            later = pl.ds(first + half, half)
            spans = [pl.ds(other * block, block) for other in range(tile)] + [pl.ds(first, half)]
            own = queries[head, :, place]
            scores = [dot(keys[head, :, span], own, 0, 0) for span in spans]
            scores[-1] = scores[-1] + causal[...]
            corner = dot(keys[head, :, later], queries[head, :, later], 0, 0) + causal[:, :half]
            highest = scores[0].max(0, keepdims=True)
            for score in scores[1:]:
                highest = jnp.maximum(highest, score.max(0, keepdims=True))
            corner_highest = jnp.maximum(highest[:, half:], corner.max(0, keepdims=True))
            highest = jnp.concatenate([highest[:, :half], corner_highest], axis=1)
            offset = highest * (SCALE * LOG2E)
            weight = jnp.exp2(corner * (SCALE * LOG2E) - offset[:, half:])
            corner_summed = weight.sum(0, keepdims=True)
            corner_total = dot(value[part, later], weight.astype(BF), 1, 0)
            summed = jnp.zeros((1, block), F32)
            total = jnp.zeros((HEAD, block), F32)
            for span, score in zip(spans, scores):
                weight = jnp.exp2(score * (SCALE * LOG2E) - offset)
                summed = summed + weight.sum(0, keepdims=True)
                total = total + dot(value[part, span], weight.astype(BF), 1, 0)
            summed = jnp.concatenate([summed[:, :half], summed[:, half:] + corner_summed], axis=1)
            total = jnp.concatenate([total[:, :half], total[:, half:] + corner_total], axis=1)
            mixture[part, place] = (total * (1.0 / summed)).astype(BF)
            totals[0, pl.ds(head, 1), place] = offset + jnp.log2(summed)


def attention_call(lengths, project, part_of=(0, 1), earlier=(), weight=0.001):
    extent = project.shape[1]
    group, block = 2, min(512, extent)
    size, groups = HEAD * group, HEADS // group
    steps = groups // part_of[1]
    base = steps * part_of[0]

    def part(section):
        return pl.BlockSpec((size, extent), lambda i: (i + base + section * groups, 0))

    pairs = extent * extent * 5 // 8
    return pl.pallas_call(
        functools.partial(attention_kernel, group, block),
        grid=(steps,),
        in_specs=[SMEM, part(0), part(1), part(2)] + [ANY] * len(earlier),
        out_specs=[part(0), pl.BlockSpec((1, group, extent), lambda i: (i + base, 0, 0))],
        out_shape=[
            jax.ShapeDtypeStruct((HEADS * HEAD, extent), BF),
            jax.ShapeDtypeStruct((groups, group, extent), F32),
        ],
        input_output_aliases={4 + n: n for n in range(len(earlier))},
        scratch_shapes=[
            pltpu.VMEM((group, HEAD + 16, extent), BF),
            pltpu.VMEM((group, HEAD + 16, extent), BF),
            pltpu.VMEM((block // 2, block), F32),
        ],
        compiler_params=params(),
        cost_estimate=estimate(weight * 16 * HEADS * pairs * HEAD / part_of[1], weight * 8e6),
        name="attention",
    )(lengths, project, project, project, *earlier)


def gelu_parts(hidden):
    chance = 0.5 + 0.5 * lax.erf(hidden * 0.7071067811865476)
    density = jnp.exp2(hidden * hidden * (-0.5 * LOG2E)) * 0.3989422804014327
    return hidden * chance, chance + hidden * density


def out_kernel(
    count, tab, lengths, mixture, frames, cotangent, out_bias, gain, shift, *rest
):
    pieces = rest[:count]
    middle, normed, result, down_bias, out_weight, sems = rest[count:]
    step = pl.program_id(0)
    model = mixture.shape[0]

    size = frames.shape[0]

    def fetch():
        return load_all(pieces, tab, out_weight, sems, model // 4, TILE)

    @pl.when(step == 0)
    def _():
        start(fetch())
        down_bias[...] = jnp.zeros_like(down_bias)

    def mask(rows, sums):
        place = step * size + rows.start + lax.broadcasted_iota(jnp.int32, (ROWS, 1), 0)
        masked = jnp.where(place < lengths[0], cotangent[rows, :].astype(F32), 0.0)
        result[rows, :] = masked.astype(BF)
        return sums + masked.sum(0, keepdims=True)

    down_bias[...] += chunks(size, ROWS, mask, jnp.zeros((1, model), F32))

    @pl.when(step == 0)
    def _():
        wait(fetch())

    def branch(rows, carry):
        total = dot(mixture[:, rows], out_weight[...], 0, 0) + out_bias[...]
        total = frames[rows, :].astype(F32) + total
        middle[rows, :] = total
        unit, _ = normalise(total)
        normed[rows, :] = (unit * gain[...] + shift[...]).astype(BF)
        return carry

    chunks(size, ROWS, branch)


def out_call(tab, lengths, mixture, frames, cotangent, vectors, pieces):
    model, extent = mixture.shape
    size = min(512, extent)
    block = pl.BlockSpec((size, model), lambda i: (i, 0))
    return pl.pallas_call(
        functools.partial(out_kernel, len(pieces)),
        grid=(extent // size,),
        in_specs=[SMEM, SMEM]
        + [pl.BlockSpec((model, size), lambda i: (0, i)), block, block]
        + [whole(1, model)] * 3
        + [ANY] * len(pieces),
        out_specs=[block, block, block, whole(1, model)],
        out_shape=[
            jax.ShapeDtypeStruct((extent, model), F32),
            jax.ShapeDtypeStruct((extent, model), BF),
            jax.ShapeDtypeStruct((extent, model), BF),
            vec(model),
        ],
        scratch_shapes=[pltpu.VMEM((model, model), BF), pltpu.SemaphoreType.DMA((32,))],
        compiler_params=params(),
        cost_estimate=estimate(1, 1),
        name="out",
    )(tab, lengths, mixture, frames, cotangent, *vectors, *pieces)


def up_kernel(counts, base, tab, normed, result, up_bias, *rest):
    count_up, count_earlier, count_grad = counts
    up_pieces, rest = rest[:count_up], rest[count_up + count_earlier :]
    active, slope = rest[:2]
    grads, rest = rest[2 : 2 + count_grad], rest[2 + count_grad :]
    weight, staged, graded, sems_up, sems_grad, sem_in = rest
    step = pl.program_id(0)
    steps = pl.num_programs(0)
    extent = normed.shape[0]

    def late():
        return pltpu.make_async_copy(result, graded, sem_in)

    def fetch(index):
        slot = lax.rem(index, 2)
        return load_columns(
            up_pieces, tab, base + index, weight.at[slot], sems_up.at[slot], TILE
        )

    def send(index):
        slot = lax.rem(index, 2)
        return store_row_pair(grads, tab, base + index, staged.at[slot], sems_grad.at[slot])

    @pl.when(step == 0)
    def _():
        start(fetch(step))
        late().start()

    @pl.when(step + 1 < steps)
    def _():
        start(fetch(step + 1))

    wait(fetch(step))
    now = lax.rem(step, 2)

    def widen(rows, carry):
        hidden = dot(normed[rows, :], weight[now], 1, 0) + up_bias[...]
        value, grade = gelu_parts(hidden)
        active[rows, :] = value.astype(BF)
        slope[rows, :] = grade.astype(BF)
        return carry

    chunks(extent, ROWS, widen)

    @pl.when(step == 0)
    def _():
        late().wait()

    @pl.when(step >= 2)
    def _():
        wait(send(step - 2))

    def weigh(columns, carry):
        staged[now, columns, :] = dot(active[:, columns], graded[...], 0, 0).astype(BF)
        return carry

    chunks(TILE, ROWS, weigh)
    start(send(step))

    @pl.when(step == steps - 1)
    def _():
        wait(send(step - 1))
        wait(send(step))


def up_call(
    tab, normed, result, up_bias, up_pieces, spread, sizes, part_of=(0, 1), earlier=(), weight=1.0
):
    extent, model = normed.shape
    hidden = 4 * model
    grads = gradient_shapes(spread, hidden, model, *sizes)
    steps = hidden // TILE // part_of[1]
    base = steps * part_of[0]
    tile = pl.BlockSpec((extent, TILE), lambda i: (0, base + i))
    aliases = {4 + len(up_pieces) + n: n for n in range(len(earlier))}
    return pl.pallas_call(
        functools.partial(up_kernel, (len(up_pieces), len(earlier), len(grads)), base),
        grid=(steps,),
        in_specs=[SMEM, whole(extent, model), ANY]
        + [pl.BlockSpec((1, TILE), lambda i: (0, base + i))]
        + [ANY] * (len(up_pieces) + len(earlier)),
        out_specs=[tile, tile] + [ANY] * len(grads),
        out_shape=[
            jax.ShapeDtypeStruct((extent, hidden), BF),
            jax.ShapeDtypeStruct((extent, hidden), BF),
        ]
        + grads,
        input_output_aliases=aliases,
        scratch_shapes=[
            pltpu.VMEM((2, model, TILE), BF),
            pltpu.VMEM((2, TILE, model), BF),
            pltpu.VMEM((extent, model), BF),
            pltpu.SemaphoreType.DMA((2, 8)),
            pltpu.SemaphoreType.DMA((2, 8)),
            pltpu.SemaphoreType.DMA,
        ],
        compiler_params=params(),
        cost_estimate=estimate(weight * 16 * extent * model * model / part_of[1], weight * 50e6),
        name="up",
    )(tab, normed, result, up_bias, *up_pieces, *earlier)


def back_kernel(counts, tab, mixture, middle, normed, d_result, slope, *rest):
    count_out, count_up, count_down, count_grad = counts
    gain = rest[0]
    rest = rest[1:]
    out_pieces, rest = rest[:count_out], rest[count_out:]
    up_pieces, rest = rest[:count_up], rest[count_up:]
    down_pieces, rest = rest[:count_down], rest[count_down:]
    d_middle, d_mixture, up_bias, gain_grad, shift_grad, out_bias = rest[:6]
    rest = rest[6:]
    grads, rest = rest[:count_grad], rest[count_grad:]
    (
        mixed,
        out_weight,
        total,
        unit_rows,
        result,
        down,
        up,
        d_hidden,
        d_normed,
        staged,
        sems_in,
        sems_out,
        sems_down,
        sems_up,
        sems_grad,
    ) = rest
    spread = len(grads[0].shape) == 4
    if spread:
        up_grads = out_grads = grads
    else:
        up_grads, out_grads = grads[:1], grads[1:]
    step = pl.program_id(0)
    steps = pl.num_programs(0)
    extent, model = result.shape
    width = model // 4

    def fetch(index):
        slot = index % 2
        return load_rows(down_pieces, tab, index, down.at[slot], sems_down.at[slot])

    def fetch_up(index):
        slot = index % 2
        block = tab[T_PAIR + index]
        return load_columns(up_pieces, tab, block, up.at[slot], sems_up.at[slot], TILE)

    def send(index):
        slot = index % 2
        block = tab[T_PAIR + index]
        return store_column_block(
            up_grads, tab, block, staged.at[slot], sems_grad.at[slot], TILE
        )

    def send_out(block):
        return store_column_block(
            out_grads,
            tab,
            block,
            staged.at[0, :, pl.ds(block * width, width)],
            sems_out.at[pl.ds(block * 8, 8)],
            width,
            TILE if spread else 0,
        )

    def early(n):
        pair = ((d_result, result), (normed, unit_rows))[n]
        return pltpu.make_async_copy(*pair, sems_in.at[n])

    def late():
        return [
            pltpu.make_async_copy(middle, total, sems_in.at[2]),
            pltpu.make_async_copy(mixture, mixed, sems_in.at[3]),
        ] + load_all(out_pieces, tab, out_weight, sems_out, width, TILE)

    now = lax.rem(step, 2)

    @pl.when(step == 0)
    def _():
        early(0).start()
        start(fetch(0))
        early(1).start()
        start(fetch_up(0))
        early(0).wait()
        d_normed[...] = jnp.zeros_like(d_normed)

    def arrive(index):
        if index == 2:
            start(late())
        if index + 1 < 4:
            start(fetch(index + 1))
            start(fetch_up(index + 1))
        wait(fetch(index))
        if index >= 2:
            wait(send(index - 2))

    for index in range(4):
        pl.when(step == index)(functools.partial(arrive, index))

    def shrink(rows, sums):
        d_active = dot(result[rows, :], down[now], 1, 1)
        piece = (d_active * slope[rows, :].astype(F32)).astype(BF)
        d_hidden[rows, :] = piece
        return sums + piece.astype(F32).sum(0, keepdims=True)

    up_bias[...] = chunks(extent, ROWS, shrink, jnp.zeros((1, TILE), F32))

    @pl.when(step == 0)
    def _():
        early(1).wait()

    def weigh(columns, carry):
        staged[now, columns, :] = dot(unit_rows[:, columns], d_hidden[...], 0, 0).astype(BF)
        return carry

    chunks(model, ROWS, weigh)
    def leave(index):
        start(send(index))
        wait(fetch_up(index))

    for index in range(4):
        pl.when(step == index)(functools.partial(leave, index))

    def widen(rows, carry):
        d_normed[rows, :] += dot(d_hidden[rows, :], up[now], 1, 1)
        return carry

    @pl.when(step < steps - 1)
    def _():
        chunks(extent, ROWS, widen)

    @pl.when(step == steps - 1)
    def _():
        wait(late())
        none = jnp.zeros((1, model), F32)

        def norm(rows, sums):
            grade = d_normed[rows, :] + dot(d_hidden[rows, :], up[now], 1, 1)
            unit, scale = normalise(total[rows, :])
            gains = sums[0] + (grade * unit).sum(0, keepdims=True)
            shifts = sums[1] + grade.sum(0, keepdims=True)
            grade = grade * gain[...]
            level = jnp.mean(grade, axis=-1, keepdims=True)
            tilt = jnp.mean(grade * unit, axis=-1, keepdims=True)
            d_total = result[rows, :].astype(F32) + scale * (grade - level - unit * tilt)
            d_middle[rows, :] = d_total
            branch = d_total.astype(BF)
            unit_rows[rows, :] = branch
            return gains, shifts, sums[2] + branch.astype(F32).sum(0, keepdims=True)

        sums = chunks(extent, ROWS, norm, (none, none, none))
        gain_grad[...], shift_grad[...], out_bias[...] = sums
        wait(send(2))

        def weigh_out(rows, carry):
            staged[0, rows, :] = dot(mixed[rows, :], unit_rows[...], 1, 0).astype(BF)
            return carry

        chunks(model, ROWS, weigh_out)
        for block in range(4):
            start(send_out(block))

        def turn(rows, carry):
            d_mixture[rows, :] = dot(out_weight[rows, :], unit_rows[...], 1, 1).astype(BF)
            return carry

        chunks(model, ROWS, turn)
        wait(send(3))
        for block in range(4):
            wait(send_out(block))


def back_call(tab, mixture, middle, normed, d_result, slope, gain, pieces, spread, sizes):
    out_pieces, up_pieces, down_pieces = pieces
    model, extent = mixture.shape
    hidden = slope.shape[1]
    if spread:
        grads = gradient_shapes(spread, model, hidden + model, *sizes)
    else:
        grads = gradient_shapes(spread, model, hidden, *sizes)
        grads += gradient_shapes(spread, model, model, *sizes)
    steps = hidden // TILE
    grid = pltpu.PrefetchScalarGridSpec(
        num_scalar_prefetch=1,
        grid=(steps,),
        in_specs=[ANY, ANY, ANY, ANY]
        + [pl.BlockSpec((extent, TILE), lambda i, tab: (0, tab[T_PAIR + i]))]
        + [whole(1, model)]
        + [ANY] * (len(out_pieces) + len(up_pieces) + len(down_pieces)),
        out_specs=[
            whole(extent, model),
            whole(model, extent),
            pl.BlockSpec((1, TILE), lambda i, tab: (0, tab[T_PAIR + i])),
            whole(1, model),
            whole(1, model),
            whole(1, model),
        ]
        + [ANY] * len(grads),
        scratch_shapes=[
            pltpu.VMEM((model, extent), BF),
            pltpu.VMEM((model, model), BF),
            pltpu.VMEM((extent, model), F32),
            pltpu.VMEM((extent, model), BF),
            pltpu.VMEM((extent, model), BF),
            pltpu.VMEM((2, TILE, model), BF),
            pltpu.VMEM((2, model, TILE), BF),
            pltpu.VMEM((extent, TILE), BF),
            pltpu.VMEM((extent, model), F32),
            pltpu.VMEM((2, model, TILE), BF),
            pltpu.SemaphoreType.DMA((4,)),
            pltpu.SemaphoreType.DMA((32,)),
            pltpu.SemaphoreType.DMA((2, 8)),
            pltpu.SemaphoreType.DMA((2, 8)),
            pltpu.SemaphoreType.DMA((2, 8)),
        ],
    )
    return pl.pallas_call(
        functools.partial(
            back_kernel, (len(out_pieces), len(up_pieces), len(down_pieces), len(grads))
        ),
        grid_spec=grid,
        out_shape=[
            jax.ShapeDtypeStruct((extent, model), F32),
            jax.ShapeDtypeStruct((model, extent), BF),
            vec(hidden),
            vec(model),
            vec(model),
            vec(model),
        ]
        + grads,
        compiler_params=params(),
        cost_estimate=estimate(28 * extent * model * model, 60e6),
        name="back",
    )(
        tab,
        mixture,
        middle,
        normed,
        d_result,
        slope,
        gain,
        *out_pieces,
        *up_pieces,
        *down_pieces,
    )


def attention_back_kernel(
    group,
    block,
    lengths,
    query,
    key,
    value,
    mixture,
    d_mixture,
    totals,
    *rest,
):
    d_project, keys, queries, causal, d_keys, d_values = rest[-6:]
    extent = query.shape[1]

    @pl.when(pl.program_id(0) == 0)
    def _():
        causal[...] = causal_bias(block, block)

    key_rows, query_rows = extend_rows(lengths[0], extent)
    for head in range(group):
        part = pl.ds(HEAD * head, HEAD)
        keys[head, :HEAD, :] = key[part, :]
        keys[head, HEAD:, :] = key_rows
        queries[head, :HEAD, :] = query[part, :]
        queries[head, HEAD:, :] = query_rows
    for head in range(group):
        part = pl.ds(HEAD * head, HEAD)
        for tile in range(extent // block):
            place = pl.ds(tile * block, block)
            own = queries[head, :, place]
            grade = d_mixture[part, place]
            center = (grade.astype(F32) * mixture[part, place].astype(F32)).sum(0, keepdims=True)
            total = totals[0, pl.ds(head, 1), place]
            d_query = jnp.zeros((HEAD, block), F32)
            for other in range(tile + 1):
                span = pl.ds(other * block, block)
                score = dot(keys[head, :, span], own, 0, 0)
                if other == tile:
                    score = score + causal[...]
                weight = jnp.exp2(score * (SCALE * LOG2E) - total)
                d_weight = dot(value[part, span], grade, 0, 0)
                d_score = (weight * (d_weight - center)).astype(BF)
                d_value = dot(grade, weight.astype(BF), 1, 1)
                d_key = dot(query[part, place], d_score, 1, 1)
                d_query = d_query + dot(key[part, span], d_score, 1, 0)
                if other == tile:
                    d_values[:, span] = d_value
                    d_keys[:, span] = d_key
                else:
                    d_values[:, span] += d_value
                    d_keys[:, span] += d_key
            d_project[0, part, place] = (d_query * SCALE).astype(BF)
        d_project[1, part, :] = (d_keys[...] * SCALE).astype(BF)
        d_project[2, part, :] = d_values[...].astype(BF)


def attention_back_call(
    lengths, project, mixture, d_mixture, totals, base=0, ending=HEADS // 2, earlier=()
):
    extent = project.shape[1]
    group, block = 2, min(512, extent)
    size, groups = HEAD * group, HEADS // group
    steps = ending - base

    def part(section):
        return pl.BlockSpec((size, extent), lambda i: (i + base + section * groups, 0))

    pairs = extent * extent * 5 // 8
    return pl.pallas_call(
        functools.partial(attention_back_kernel, group, block),
        grid=(steps,),
        in_specs=[SMEM, part(0), part(1), part(2), part(0), part(0)]
        + [pl.BlockSpec((1, group, extent), lambda i: (i + base, 0, 0))]
        + [ANY] * len(earlier),
        out_specs=pl.BlockSpec((3, size, extent), lambda i: (0, i + base, 0)),
        out_shape=jax.ShapeDtypeStruct((3, HEADS * HEAD, extent), BF),
        input_output_aliases={7: 0} if earlier else {},
        scratch_shapes=[
            pltpu.VMEM((group, HEAD + 16, extent), BF),
            pltpu.VMEM((group, HEAD + 16, extent), BF),
            pltpu.VMEM((block, block), F32),
            pltpu.VMEM((HEAD, extent), F32),
            pltpu.VMEM((HEAD, extent), F32),
        ],
        compiler_params=params(),
        cost_estimate=estimate(4 * HEADS * pairs * HEAD * steps / groups, 1e6),
        name="attention_back",
    )(lengths, project, project, project, mixture, d_mixture, totals, *earlier)


def attend_grad_kernel(count_grad, tab, d_project, normed, *rest):
    bias_grad = rest[0]
    grads, rest = rest[1 : 1 + count_grad], rest[1 + count_grad :]
    staged, sems_grad = rest
    step = pl.program_id(0)
    steps = pl.num_programs(0)
    extent, model = normed.shape
    width = d_project.shape[0]

    def send(block):
        slot = lax.rem(block, 2)
        return store_column_block(grads, tab, block, staged.at[slot], sems_grad.at[slot], width)

    @pl.when(step >= 2)
    def _():
        wait(send(step - 2))

    now = lax.rem(step, 2)

    def weigh(columns, carry):
        staged[now, columns, :] = dot(normed[:, columns], d_project[...], 0, 1).astype(BF)
        return carry

    chunks(model, ROWS, weigh)
    start(send(step))
    sums = d_project[...].astype(F32).sum(1, keepdims=True)
    bias_grad[...] = jnp.transpose(jnp.broadcast_to(sums, (width, 128)))[:1, :]

    @pl.when(step == steps - 1)
    def _():
        wait(send(step - 1))
        wait(send(step))


def attend_grad_call(tab, d_project, normed, spread, sizes):
    extent, model = normed.shape
    width = 3 * model // 4
    grads = gradient_shapes(spread, model, 3 * model, *sizes)
    return pl.pallas_call(
        functools.partial(attend_grad_kernel, len(grads)),
        grid=(4,),
        in_specs=[SMEM, pl.BlockSpec((width, extent), lambda i: (i, 0)), whole(extent, model)],
        out_specs=[pl.BlockSpec((1, width), lambda i: (0, i))] + [ANY] * len(grads),
        out_shape=[vec(3 * model)] + grads,
        scratch_shapes=[
            pltpu.VMEM((2, model, width), BF),
            pltpu.SemaphoreType.DMA((2, 8)),
        ],
        compiler_params=params(),
        cost_estimate=estimate(6 * extent * model * model, 14e6),
        name="attend_grad",
    )(tab, d_project, normed)


def first_kernel(count_in, tab, d_project, frames, d_middle, gain, *rest):
    pieces, rest = rest[:count_in], rest[count_in:]
    bias_grad, *early = rest[:6]
    d_frames, small, weight, total, d_normed, sems, sem_total = rest[6:]
    step = pl.program_id(0)
    steps = pl.num_programs(0)
    extent, model = frames.shape
    width = d_project.shape[0]

    def fetch(index):
        slot = index % 2
        return load_slot(pieces, tab, index, weight.at[slot], sems.at[slot], width)

    def late():
        return pltpu.make_async_copy(d_middle, total, sem_total)

    @pl.when(step == 0)
    def _():
        start(fetch(0))
        late().start()
        d_normed[...] = jnp.zeros_like(d_normed)

    def arrive(index):
        if index + 1 < 4:
            start(fetch(index + 1))
        wait(fetch(index))

    for index in range(4):
        pl.when(step == index)(functools.partial(arrive, index))
    now = lax.rem(step, 2)

    def widen(rows, carry):
        d_normed[rows, :] += dot(d_project[:, rows], weight[now], 0, 1)
        return carry

    @pl.when(step < steps - 1)
    def _():
        chunks(extent, ROWS, widen)

    @pl.when(step == steps - 1)
    def _():
        late().wait()
        none = jnp.zeros((1, model), F32)

        def norm(rows, sums):
            grade = d_normed[rows, :] + dot(d_project[:, rows], weight[now], 0, 1)
            unit, scale = normalise(frames[rows, :].astype(F32))
            gains = sums[0] + (grade * unit).sum(0, keepdims=True)
            shifts = sums[1] + grade.sum(0, keepdims=True)
            grade = grade * gain[...]
            level = jnp.mean(grade, axis=-1, keepdims=True)
            tilt = jnp.mean(grade * unit, axis=-1, keepdims=True)
            d_frames[rows, :] = (total[rows, :] + scale * (grade - level - unit * tilt)).astype(BF)
            return gains, shifts

        gains, shifts = chunks(extent, ROWS, norm, (none, none))
        bias = bias_grad[...]
        vectors = [gains, shifts, bias[:, :model], bias[:, 2 * model :]]
        vectors += [vector[...] for vector in early]
        place = 0
        for vector in vectors:
            for column in range(0, vector.shape[1], 128):
                small[place : place + 1, :] = vector[:, column : column + 128]
                place += 1


def small_kernel(*refs):
    *terms, a, b, c, d, e, f, g, h = refs
    terms = [term[...] for term in terms]
    total = tree_sum(terms)
    place = 0
    for out in (a, b, c, d, e, f, g, h):
        out[...] = total[place : place + out.shape[0], :]
        place += out.shape[0]


def small_call(terms):
    unit = terms[0].shape[0] // 12
    sizes = [unit, unit, 2 * unit, unit, unit, unit, unit, 4 * unit]
    return pl.pallas_call(
        small_kernel,
        out_shape=[jax.ShapeDtypeStruct((size, 128), F32) for size in sizes],
        name="small",
    )(*terms)


def first_call(tab, d_project, frames, d_middle, gain, pieces, vectors):
    extent, model = frames.shape
    width = 3 * model // 4
    count = model + sum(vector.shape[1] for vector in vectors)
    grid = pltpu.PrefetchScalarGridSpec(
        num_scalar_prefetch=1,
        grid=(4,),
        in_specs=[pl.BlockSpec((width, extent), lambda i, tab: (tab[T_COL + i], 0))]
        + [whole(extent, model), ANY, whole(1, model)]
        + [ANY] * len(pieces)
        + [whole(*vector.shape) for vector in vectors],
        out_specs=[whole(extent, model), whole(count // 128, 128)],
        scratch_shapes=[
            pltpu.VMEM((2, model, width), BF),
            pltpu.VMEM((extent, model), F32),
            pltpu.VMEM((extent, model), F32),
            pltpu.SemaphoreType.DMA((2, 8)),
            pltpu.SemaphoreType.DMA,
        ],
    )
    return pl.pallas_call(
        functools.partial(first_kernel, len(pieces)),
        grid_spec=grid,
        out_shape=[
            jax.ShapeDtypeStruct((extent, model), BF),
            jax.ShapeDtypeStruct((count // 128, 128), F32),
        ],
        compiler_params=params(),
        cost_estimate=estimate(6 * extent * model * model, 24e6),
        name="first",
    )(tab, d_project, frames, d_middle, gain, *pieces, *vectors)


def down_kernel(count, count_earlier, row, tab, active, middle, bias, *rest):
    pieces = rest[:count]
    frames_out, weight, total, base, sems, sem_base = rest[count + count_earlier :]
    step = pl.program_id(0)
    steps = pl.num_programs(0)
    extent = total.shape[0]

    def fetch(index):
        slot = index % 2
        return load_rows(pieces, tab, index, weight.at[slot], sems.at[slot])

    def late():
        return pltpu.make_async_copy(middle.at[pl.ds(row * extent, extent), :], base, sem_base)

    def arrive(index):
        if index == 0:
            start(fetch(index))
            late().start()
        if index + 1 < 4:
            start(fetch(index + 1))
        wait(fetch(index))

    for index in range(4):
        pl.when(step == index)(functools.partial(arrive, index))
    now = lax.rem(step, 2)

    @pl.when(step < steps - 1)
    def _():
        def widen(rows, carry):
            before = jnp.where(step == 0, 0.0, total[rows, :])
            total[rows, :] = before + dot(active[rows, :], weight[now], 1, 0)
            return carry

        chunks(extent, ROWS, widen)

    @pl.when(step == steps - 1)
    def _():
        late().wait()

        def finish(rows, carry):
            result = total[rows, :] + dot(active[rows, :], weight[now], 1, 0)
            frames_out[rows, :] = (result + (base[rows, :] + bias[...])).astype(BF)
            return carry

        chunks(extent, ROWS, finish)


def down_call(tab, active, middle, bias, pieces, part_of=(0, 1), earlier=()):
    extent, hidden = active.shape
    model = middle.shape[1]
    row, size = part_of[0], extent // part_of[1]
    grid = pltpu.PrefetchScalarGridSpec(
        num_scalar_prefetch=1,
        grid=(hidden // TILE,),
        in_specs=[pl.BlockSpec((size, TILE), lambda i, tab: (row, tab[T_PAIR + i]))]
        + [ANY, whole(1, model)]
        + [ANY] * (len(pieces) + len(earlier)),
        out_specs=pl.BlockSpec((size, model), lambda i, tab: (row, 0)),
        scratch_shapes=[
            pltpu.VMEM((2, TILE, model), BF),
            pltpu.VMEM((size, model), F32),
            pltpu.VMEM((size, model), F32),
            pltpu.SemaphoreType.DMA((2, 8)),
            pltpu.SemaphoreType.DMA,
        ],
    )
    return pl.pallas_call(
        functools.partial(down_kernel, len(pieces), len(earlier), row),
        grid_spec=grid,
        out_shape=jax.ShapeDtypeStruct((extent, model), BF),
        input_output_aliases={4 + len(pieces): 0} if earlier else {},
        compiler_params=params(),
        cost_estimate=estimate(8 * size * model * model, 24e6),
        name="down",
    )(tab, active, middle, bias, *pieces, *earlier)


def gather_plain(weight):
    wide = lax.all_gather(weight, "inner", axis=1, tiled=True)
    return [lax.all_gather(wide, "dp", axis=0, tiled=True)]


def scatter_plain(grads):
    wide = lax.psum_scatter(grads[0], "dp", scatter_dimension=0, tiled=True)
    return lax.psum_scatter(wide, "inner", scatter_dimension=1, tiled=True).astype(F32)


CORE, NEAR, FAR = 0, 1, 2


def swap(value, way):
    flips = {CORE: (1, 1), NEAR: (2, 4), FAR: (4, 2)}[way]
    return lax.ppermute(value, "dp", [(d, d ^ flips[d & 1]) for d in range(8)])


def shift(value, amount):
    return lax.ppermute(value, "inner", [(i, (i + amount) & 3) for i in range(4)])


def after(value, *done):
    return lax.optimization_barrier((value, done))[0]


def stack_spread(block):
    return jnp.stack([block] + [shift(block, amount) for amount in (1, 2, 3)])


def added(*values):
    total = values[0].astype(F32)
    for value in values[1:]:
        total = total + value.astype(F32)
    return total


def add_kernel(count, *refs):
    total = added(*[ref[...] for ref in refs[:count]])
    outs = refs[count:]
    if len(outs) == 1:
        outs[0][...] = total.reshape(outs[0].shape).astype(BF)
        return
    for index, out in enumerate(outs):

        @pl.when(pl.program_id(0) == index)
        def _(out=out):
            out[...] = total.reshape(out.shape).astype(out.dtype)


def add_call(terms, outs, grid):
    rows, columns = terms[0][0].shape[-2:]
    specs = []
    for term, place in terms:
        if term.ndim == 3:
            specs.append(pl.BlockSpec((1, rows, columns), lambda *at: (at[-1], 0, 0)))
        elif place is None:
            specs.append(pl.BlockSpec((1, 1, rows, columns), lambda p, k: (p, k, 0, 0)))
        else:
            specs.append(
                pl.BlockSpec((1, 1, rows, columns), lambda k, place=place: (place, k, 0, 0))
            )
    if len(outs) == 1:
        lead = (1,) * len(grid)
        out_specs = [pl.BlockSpec(lead + (rows, columns), lambda *at: at + (0, 0))]
    else:
        out_specs = [whole(rows, columns)] * len(outs)

    def kernel(*refs):
        ins = [
            ref.at[0] if len(ref.shape) == 3 else ref.at[0, 0] for ref in refs[: len(terms)]
        ]
        add_kernel(len(terms), *ins, *refs[len(terms) :])

    return pl.pallas_call(
        kernel,
        grid=grid,
        in_specs=specs,
        out_specs=out_specs,
        out_shape=outs,
        compiler_params=params(),
        cost_estimate=estimate(1e10, 1e7),
        name="add",
    )(*[term for term, _ in terms])


def add_first(keep, core):
    return added(keep[:2], core[:2]).astype(BF)


def add_second(keep, core, link):
    return added(keep[2], core[2], link[0]).astype(BF)


def add_third(keep, core, link, last):
    blocks = [added(keep[3, k], core[3, k], link[1, k], last[k]) for k in range(4)]
    return [blocks[0]] + [block.astype(BF) for block in blocks[1:]]


def add_third_kernel(keep, core, link, last):
    shapes = [jax.ShapeDtypeStruct(keep.shape[2:], F32)]
    shapes += [jax.ShapeDtypeStruct(keep.shape[2:], BF)] * 3
    return add_call([(keep, 3), (core, 3), (link, 1), (last, None)], shapes, (4,))


def shift_parts(parts):
    return [shift(parts[k], k) for k in (1, 2, 3)]


def exchange(values, axis, size):
    return [values] + [
        lax.ppermute(values, axis, [(i, i ^ flip) for i in range(size)])
        for flip in range(1, size)
    ]


def tree_sum(terms):
    while len(terms) > 1:
        terms = [terms[i] + terms[i + 1] for i in range(0, len(terms), 2)]
    return terms[0]


def shards(
    spread,
    sizes,
    frames_in,
    lengths,
    first_gain,
    first_shift,
    attend_weight,
    attend_bias,
    output_weight,
    output_bias,
    second_gain,
    second_shift,
    up_weight,
    up_bias,
    down_weight,
    down_bias,
    cotangent,
):
    _, extent, model = frames_in.shape
    frames = frames_in.reshape(extent, model)
    upstream = cotangent.reshape(extent, model)
    tab = make_table(spread, True)
    tab_plain = make_table(spread, False)

    def row(vector):
        return vector.reshape(1, -1)

    if not spread:
        attend_pieces = gather_plain(attend_weight)
        out_pieces = gather_plain(output_weight)
        up_pieces = gather_plain(up_weight)
        down_pieces = gather_plain(down_weight)
    else:
        others = [shift(attend_weight, amount) for amount in (1, 2, 3)]
        up_block = jnp.concatenate([up_weight, output_weight], axis=1)
        near, far = swap(attend_weight, NEAR), swap(attend_weight, FAR)
        others = jnp.stack(others)
        far, near = after((far, near), near, far)
        diagonal = swap(near, FAR)
        attend_pieces = [attend_weight, near, far, diagonal]
        attend_pieces += [swap(piece, CORE) for piece in attend_pieces]
        others = after(others, diagonal)
        near, far = swap(others, NEAR), swap(others, FAR)
        up_block = after(up_block, others)
        up_own = lax.all_gather(up_block, "inner")
        near, far = after((near, far), near, far)
        diagonal = swap(near, FAR)
        others = [others, near, far, diagonal]
        attend_pieces += others + [swap(piece, CORE) for piece in others]
        up_own = after(up_own, *attend_pieces)
        up_near, up_far = swap(up_own, NEAR), swap(up_own, FAR)
        down_own = lax.all_gather(after(down_weight, up_own), "inner")
    bias_row = jnp.concatenate([attend_bias[0], jnp.zeros_like(attend_bias[0]), attend_bias[1]])
    vectors = (row(first_gain), row(first_shift), row(bias_row))
    tokens = after(frames, up_own) if spread else frames
    normed, project = project_call(tab, tokens, *vectors, attend_pieces)
    if spread:
        mixture, totals = attention_call(lengths, after(project, up_own), (0, 2))
        up_near, up_far = after((up_near, up_far), totals)
        up_diagonal = swap(up_near, FAR)
        ahead = [swap(piece, CORE) for piece in (after(up_own, totals), up_near, up_far)]
        mixture, totals = attention_call(
            lengths, after(project, up_near, up_far, down_own), (1, 2), (mixture, totals)
        )
        up_pieces = [up_own, up_near, up_far, up_diagonal]
        up_pieces += ahead + [swap(after(up_diagonal, totals), CORE)]
        out_pieces = up_pieces
    else:
        mixture, totals = attention_call(lengths, project)
    vectors = (row(output_bias), row(second_gain), row(second_shift))
    if spread:
        down_near, down_far = swap(down_own, NEAR), swap(down_own, FAR)
    middle, normed_two, d_result, grad_down_bias = out_call(
        tab_plain, lengths, mixture, frames, upstream, vectors, out_pieces
    )
    if spread:
        *halves, half_grad = up_call(
            tab_plain,
            normed_two,
            d_result,
            row(up_bias),
            up_pieces,
            False,
            sizes,
            (0, 2),
        )
        down_near, down_far = after((down_near, down_far), halves)
        down_diagonal = swap(down_near, FAR)
        ahead = [swap(piece, CORE) for piece in (after(down_own, totals), down_near, down_far)]
        active, slope, *down_grads = up_call(
            tab_plain,
            after(normed_two, down_near, down_far),
            d_result,
            row(up_bias),
            up_pieces,
            False,
            sizes,
            (1, 2),
            (*halves, half_grad),
        )
    else:
        active, slope, *down_grads = up_call(
            tab_plain, normed_two, d_result, row(up_bias), up_pieces, False, sizes
        )
    if spread:
        down_pieces = [down_own, down_near, down_far, down_diagonal]
        down_pieces += ahead + [swap(after(down_diagonal, slope), CORE)]
        down_wide = lax.psum_scatter(down_grads[0], "dp", scatter_dimension=0, tiled=True)
    else:
        down_owned = scatter_plain(down_grads)
    (
        d_middle,
        d_mixture,
        grad_up_bias,
        grad_second_gain,
        grad_second_shift,
        grad_output_bias,
        *back_grads,
    ) = back_call(
        tab_plain,
        mixture,
        middle,
        normed_two,
        d_result,
        slope,
        row(second_gain),
        (out_pieces, up_pieces, down_pieces),
        spread,
        sizes,
    )
    early = [grad_output_bias, grad_second_gain, grad_second_shift, grad_down_bias, grad_up_bias]
    if spread:
        back_keep, back_send = back_grads
        back_core = swap(back_send, CORE)
        d_project = attention_back_call(lengths, project, mixture, d_mixture, totals, 0, 2)
        back_core = after(back_core, d_project)
        back_first = add_first(back_keep, back_core)
        back_link = swap(back_first, FAR)
        d_mixture = after(d_mixture, back_first)
        d_project = attention_back_call(
            lengths, project, mixture, d_mixture, totals, 2, HEADS // 2, (d_project,)
        )
        back_link, down_wide = after((back_link, down_wide), d_project)
        down_owned = lax.psum_scatter(down_wide, "inner", scatter_dimension=1, tiled=True)
        back_second = add_second(back_keep, back_core, back_link)
        back_last = swap(back_second, NEAR)
        d_rows = after(d_project, back_second, down_wide).reshape(3 * model, extent)
        grad_bias, attend_keep, attend_send = attend_grad_call(tab, d_rows, normed, spread, sizes)
        attend_core = swap(attend_send, CORE)
        back_last = after(back_last, grad_bias)
        back_parts = add_third_kernel(back_keep, back_core, back_link, back_last)
        back_others = shift_parts(back_parts)
        attend_core = after(attend_core, back_parts)
        attend_first = add_first(attend_keep, attend_core)
        attend_link = swap(attend_first, FAR)
        d_frames, small = first_call(
            tab,
            after(d_rows, attend_first),
            frames,
            d_middle,
            row(first_gain),
            attend_pieces,
            [grad_bias] + early,
        )
        attend_link, down_owned = after((attend_link, down_owned), d_frames)
        attend_second = add_second(attend_keep, attend_core, attend_link)
        attend_last = swap(attend_second, NEAR)
        small_terms = exchange(small, "inner", 4)
        active, middle = after((active, middle), attend_second, down_owned)
        frames_out = down_call(tab_plain, active, middle, row(down_bias), down_pieces)
        attend_last, back_others, small_terms = after(
            (attend_last, back_others, small_terms), frames_out
        )
        back_owned = added(back_parts[0], *back_others)
        small = tree_sum(small_terms)
        attend_parts = add_third(attend_keep, attend_core, attend_link, attend_last)
        attend_parts, small = after((attend_parts, small), back_owned, small, attend_parts)
        others = shift_parts(attend_parts)
        small_terms = exchange(small, "dp", 8)
        attend_owned = added(attend_parts[0], *others)
        small = small_call(after(small_terms, attend_owned))
        down_owned = down_owned.astype(F32)
        up_owned, output_owned = back_owned[:, :TILE], back_owned[:, TILE:]
    else:
        d_project = attention_back_call(lengths, project, mixture, d_mixture, totals)
        d_rows = d_project.reshape(3 * model, extent)
        grad_bias, *attend_grads = attend_grad_call(tab, d_rows, normed, spread, sizes)
        d_frames, small = first_call(
            tab,
            d_rows,
            frames,
            d_middle,
            row(first_gain),
            attend_pieces,
            [grad_bias] + early,
        )
        frames_out = down_call(tab_plain, active, middle, row(down_bias), down_pieces)
        up_owned = scatter_plain(back_grads[:1])
        output_owned = scatter_plain(back_grads[1:])
        attend_owned = scatter_plain(attend_grads)
        small = small_call([lax.psum(small, ("dp", "inner"))])
    small = [vector.reshape(-1) for vector in small]

    return (
        frames_out.reshape(frames_in.shape),
        d_frames.reshape(frames_in.shape),
        small[0],
        small[1],
        attend_owned,
        small[2].reshape(2, model),
        output_owned,
        small[3],
        small[4],
        small[5],
        up_owned,
        small[7],
        down_owned,
        small[6],
    )


def solution(mesh):
    sizes = (mesh.shape["dp"], mesh.shape["inner"])
    spread = sizes == (8, 4)
    return jax.shard_map(
        functools.partial(shards, spread, sizes),
        mesh=mesh,
        in_specs=(
            P(("dp", "inner"), None, None),
            P(("dp", "inner")),
            P(),
            P(),
            P("dp", "inner"),
            P(),
            P("dp", "inner"),
            P(),
            P(),
            P(),
            P("dp", "inner"),
            P(),
            P("dp", "inner"),
            P(),
            P(("dp", "inner"), None, None),
        ),
        out_specs=(
            P(("dp", "inner"), None, None),
            P(("dp", "inner"), None, None),
            P(),
            P(),
            P("dp", "inner"),
            P(),
            P("dp", "inner"),
            P(),
            P(),
            P(),
            P("dp", "inner"),
            P(),
            P("dp", "inner"),
            P(),
        ),
        check_vma=False,
    )
```

```python
import functools

import jax
import jax.numpy as jnp
from jax import lax
from jax.experimental import pallas as pl
from jax.experimental.pallas import tpu as pltpu
from jax.sharding import PartitionSpec as P

HEADS = 16
HEAD = 64
TILE = 1024
ROWS = 512
LOG2E = 1.4426950408889634
MASKED = -1e30
SCALE = HEAD ** (-0.5)
BF = jnp.bfloat16
F32 = jnp.float32
LIMIT = 60 * 2**20


def dot(left, right, on_left, on_right):
    return lax.dot_general(
        left, right, (((on_left,), (on_right,)), ((), ())), preferred_element_type=F32
    )


def normalise(values):
    center = values - jnp.mean(values, axis=-1, keepdims=True)
    spread = jnp.mean(center * center, axis=-1, keepdims=True)
    scale = lax.rsqrt(spread + 1e-05)
    return center * scale, scale


def params(name_limit=LIMIT):
    return pltpu.CompilerParams(vmem_limit_bytes=name_limit)


def estimate(flops, moved, exps=0):
    return pl.CostEstimate(
        flops=int(8 * flops), bytes_accessed=int(8 * moved), transcendentals=int(8 * exps)
    )


ANY = pl.BlockSpec(memory_space=pl.ANY)
SMEM = pl.BlockSpec(memory_space=pltpu.SMEM)


def whole(*shape):
    return pl.BlockSpec(shape, lambda *_: (0,) * len(shape))


def vec(size):
    return jax.ShapeDtypeStruct((1, size), F32)


PIECES = 8
SLOTS = 4
T_ROW = 0
T_COL = 8
T_SLOT_IN = 12
T_SLOT_OUT = 16
T_PAIR = 20
T_OUT = 24
T_PLACE = 32
T_CORE = 40
T_SIZE = 48


def make_table(spread, relative):
    if not spread:
        order = list(range(4))
        entries = [0] * T_SIZE
        entries[T_PAIR : T_PAIR + 4] = order
        entries[T_COL : T_COL + 4] = order
        return jnp.array(entries, jnp.int32)
    row = lax.axis_index("dp").astype(jnp.int32)
    column = lax.axis_index("inner").astype(jnp.int32)
    core = row & 1
    near = jnp.where(core == 0, 2, 4)
    far = 6 - near
    entries = [
        row,
        row ^ near,
        row ^ far,
        row ^ 6,
        row ^ 1,
        row ^ 1 ^ far,
        row ^ 1 ^ near,
        row ^ 7,
    ]
    if relative:
        entries += [(column - block) & 3 for block in range(4)] * 2
    else:
        entries += [0, 1, 2, 3] * 2
    entries += [(block - column) & 3 for block in range(4)]
    pair = row >> 1
    entries += [pair, pair ^ (near >> 1), pair ^ (far >> 1), pair ^ 3]
    for half in range(2):
        a, b = (far, near) if half == 0 else (near, far)
        own = row ^ half
        entries += [own ^ 6, own ^ a, own ^ b, own]
    for half in range(2):
        first = far if half == 0 else near
        for block in range(4):
            relative = (pair ^ block) << 1
            entries.append(
                jnp.where(
                    relative == 6,
                    0,
                    jnp.where(relative == 0, 3, jnp.where(relative == first, 1, 2)),
                )
            )
    entries += [core]
    entries += [jnp.int32(0)] * (T_SIZE - len(entries))
    return jnp.stack([jnp.asarray(entry, jnp.int32) for entry in entries])


def aligned(index, size):
    return pl.ds(pl.multiple_of(index * size, size), size)


def load_slot(pieces, tab, step, target, sems, width):
    if len(pieces) == 1:
        return load_columns(pieces, tab, tab[T_COL + step], target, sems, width)
    rows = pieces[0].shape[-2]
    copies = []
    for p in range(PIECES):
        source = pieces[p] if step == 0 else pieces[PIECES + p].at[step - 1]
        place = target.at[aligned(tab[T_ROW + p], rows), :]
        copies.append(pltpu.make_async_copy(source, place, sems.at[p]))
    return copies


def load_columns(pieces, tab, block, target, sems, width, first=0):
    if len(pieces) == 1:
        copies = [
            pltpu.make_async_copy(pieces[0].at[:, aligned(block, width)], target, sems.at[0])
        ]
        return copies
    slot = tab[T_SLOT_IN + block]
    rows = pieces[0].shape[1]
    return [
        pltpu.make_async_copy(
            pieces[p].at[slot, :, pl.ds(first, width)],
            target.at[aligned(tab[T_ROW + p], rows), :],
            sems.at[p],
        )
        for p in range(PIECES)
    ]


def load_rows(pieces, tab, step, target, sems):
    if len(pieces) == 1 and len(pieces[0].shape) == 2:
        return [
            pltpu.make_async_copy(
                pieces[0].at[aligned(tab[T_PAIR + step], TILE), :], target, sems.at[0]
            )
        ]
    rows, width = pieces[0].shape[-2:]
    if len(pieces) == 1:
        return [
            pltpu.make_async_copy(
                pieces[0].at[2 * tab[T_PAIR + step] + half, block],
                target.at[pl.ds(half * rows, rows), pl.ds(block * width, width)],
                sems.at[half * SLOTS + block],
            )
            for half in range(2)
            for block in range(4)
        ]
    partner = (4, 6, 5, 7)[step]
    copies = []
    for n, p in enumerate((step, partner)):
        half = tab[T_ROW + p] & 1
        for slot in range(SLOTS):
            copies.append(
                pltpu.make_async_copy(
                    pieces[p].at[slot],
                    target.at[aligned(half, rows), aligned(tab[T_COL + slot], width)],
                    sems.at[n * SLOTS + slot],
                )
            )
    return copies


def load_all(pieces, tab, target, sems, width, first=0):
    if len(pieces) == 1:
        return [pltpu.make_async_copy(pieces[0], target, sems.at[0])]
    rows = pieces[0].shape[1]
    return [
        pltpu.make_async_copy(
            pieces[p].at[slot, :, pl.ds(first, width)],
            target.at[aligned(tab[T_ROW + p], rows), aligned(tab[T_COL + slot], width)],
            sems.at[p * SLOTS + slot],
        )
        for p in range(PIECES)
        for slot in range(SLOTS)
    ]


def store_column_block(outs, tab, block, source, sems, width, first=0):
    if len(outs) == 1:
        return [pltpu.make_async_copy(source, outs[0].at[:, aligned(block, width)], sems.at[0])]
    rows = outs[0].shape[2]
    slot = tab[T_SLOT_OUT + block]
    return [
        pltpu.make_async_copy(
            source.at[aligned(tab[T_OUT + half * 4 + place], rows), :],
            outs[half].at[place, slot, :, pl.ds(first, width)],
            sems.at[half * 4 + place],
        )
        for half in range(2)
        for place in range(4)
    ]


def store_row_pair(outs, tab, pair, source, sems):
    if len(outs) == 1:
        return [pltpu.make_async_copy(source, outs[0].at[aligned(pair, TILE), :], sems.at[0])]
    rows, width = outs[0].shape[2:]
    copies = []
    for half in range(2):
        local = tab[T_CORE] ^ half
        for block in range(4):
            copies.append(
                pltpu.make_async_copy(
                    source.at[aligned(local, rows), pl.ds(block * width, width)],
                    outs[half].at[tab[T_PLACE + half * 4 + pair], tab[T_SLOT_OUT + block]],
                    sems.at[half * 4 + block],
                )
            )
    return copies


def chunks(extent, size, body, init=0):
    for first in range(0, extent, size):
        init = body(pl.ds(first, size), init)
    return init


def start(copies):
    for copy in copies:
        copy.start()


def wait(copies):
    for copy in copies:
        copy.wait()


def gradient_shapes(spread, rows, columns, dp, inner):
    if spread:
        return [jax.ShapeDtypeStruct((4, 4, rows // dp, columns // inner), BF)] * 2
    return [jax.ShapeDtypeStruct((rows, columns), BF)]


def project_kernel(count, tab, tokens, gain, shift, bias, *rest):
    pieces = rest[:count]
    normed, project, weight, sems = rest[count:]
    step = pl.program_id(0)
    width = project.shape[0]

    def fetch(index):
        slot = index % 2
        return load_slot(pieces, tab, index, weight.at[slot], sems.at[slot], width)

    @pl.when(step == 0)
    def _():
        start(fetch(0))

        def norm(rows, carry):
            unit, _ = normalise(tokens[rows, :].astype(F32))
            normed[rows, :] = (unit * gain[...] + shift[...]).astype(BF)
            return carry

        chunks(tokens.shape[0], ROWS, norm)

    def arrive(index):
        if index + 1 < 4:
            start(fetch(index + 1))
        wait(fetch(index))

    for index in range(4):
        pl.when(step == index)(functools.partial(arrive, index))

    column = jnp.transpose(jnp.broadcast_to(bias[...], (128, width)))[:, :1]

    project[...] = (dot(weight[lax.rem(step, 2)], normed[...], 0, 1) + column).astype(BF)


def project_call(tab, tokens, gain, shift, bias, pieces):
    extent, model = tokens.shape
    width = 3 * model // 4
    grid = pltpu.PrefetchScalarGridSpec(
        num_scalar_prefetch=1,
        grid=(4,),
        in_specs=[whole(extent, model), whole(1, model), whole(1, model)]
        + [pl.BlockSpec((1, width), lambda i, tab: (0, tab[T_COL + i]))]
        + [ANY] * len(pieces),
        out_specs=[
            whole(extent, model),
            pl.BlockSpec((width, extent), lambda i, tab: (tab[T_COL + i], 0)),
        ],
        scratch_shapes=[
            pltpu.VMEM((2, model, width), BF),
            pltpu.SemaphoreType.DMA((2, 8)),
        ],
    )
    return pl.pallas_call(
        functools.partial(project_kernel, len(pieces)),
        grid_spec=grid,
        out_shape=[
            jax.ShapeDtypeStruct((extent, model), BF),
            jax.ShapeDtypeStruct((3 * model, extent), BF),
        ],
        compiler_params=params(),
        cost_estimate=estimate(1e6, 1e4),
        name="project",
    )(tab, tokens, gain, shift, bias, *pieces)


def causal_bias(keys, queries):
    key = lax.broadcasted_iota(jnp.int32, (keys, queries), 0)
    query = lax.broadcasted_iota(jnp.int32, (keys, queries), 1)
    return jnp.where(key <= query, 0.0, MASKED)


def extend_rows(length, extent):
    first = lax.broadcasted_iota(jnp.int32, (16, extent), 0) == 0
    past = lax.broadcasted_iota(jnp.int32, (16, extent), 1) >= length
    key_rows = jnp.where(first & past, MASKED, 0.0).astype(BF)
    query_rows = jnp.where(first, 1.0, 0.0).astype(BF)
    return key_rows, query_rows


def attention_kernel(group, block, lengths, query, key, value, *rest):
    mixture, totals, keys, queries, causal = rest[-5:]
    extent = query.shape[1]

    half = block // 2

    @pl.when(pl.program_id(0) == 0)
    def _():
        causal[...] = causal_bias(half, block)

    key_rows, query_rows = extend_rows(lengths[0], extent)
    for head in range(group):
        part = pl.ds(HEAD * head, HEAD)
        keys[head, :HEAD, :] = key[part, :]
        keys[head, HEAD:, :] = key_rows
        queries[head, :HEAD, :] = query[part, :]
        queries[head, HEAD:, :] = query_rows
    for head in range(group):
        part = pl.ds(HEAD * head, HEAD)
        for tile in range(extent // block):
            first = tile * block
            place = pl.ds(first, block)
            later = pl.ds(first + half, half)
            spans = [pl.ds(other * block, block) for other in range(tile)] + [pl.ds(first, half)]
            own = queries[head, :, place]
            scores = [dot(keys[head, :, span], own, 0, 0) for span in spans]
            scores[-1] = scores[-1] + causal[...]
            corner = dot(keys[head, :, later], queries[head, :, later], 0, 0) + causal[:, :half]
            highest = scores[0].max(0, keepdims=True)
            for score in scores[1:]:
                highest = jnp.maximum(highest, score.max(0, keepdims=True))
            corner_highest = jnp.maximum(highest[:, half:], corner.max(0, keepdims=True))
            highest = jnp.concatenate([highest[:, :half], corner_highest], axis=1)
            offset = highest * (SCALE * LOG2E)
            weight = jnp.exp2(corner * (SCALE * LOG2E) - offset[:, half:])
            corner_summed = weight.sum(0, keepdims=True)
            corner_total = dot(value[part, later], weight.astype(BF), 1, 0)
            summed = jnp.zeros((1, block), F32)
            total = jnp.zeros((HEAD, block), F32)
            for span, score in zip(spans, scores):
                weight = jnp.exp2(score * (SCALE * LOG2E) - offset)
                summed = summed + weight.sum(0, keepdims=True)
                total = total + dot(value[part, span], weight.astype(BF), 1, 0)
            summed = jnp.concatenate([summed[:, :half], summed[:, half:] + corner_summed], axis=1)
            total = jnp.concatenate([total[:, :half], total[:, half:] + corner_total], axis=1)
            mixture[part, place] = (total * (1.0 / summed)).astype(BF)
            totals[0, pl.ds(head, 1), place] = offset + jnp.log2(summed)


def attention_call(lengths, project, part_of=(0, 1), earlier=(), weight=0.001):
    extent = project.shape[1]
    group, block = 2, min(512, extent)
    size, groups = HEAD * group, HEADS // group
    steps = groups // part_of[1]
    base = steps * part_of[0]

    def part(section):
        return pl.BlockSpec((size, extent), lambda i: (i + base + section * groups, 0))

    pairs = extent * extent * 5 // 8
    return pl.pallas_call(
        functools.partial(attention_kernel, group, block),
        grid=(steps,),
        in_specs=[SMEM, part(0), part(1), part(2)] + [ANY] * len(earlier),
        out_specs=[part(0), pl.BlockSpec((1, group, extent), lambda i: (i + base, 0, 0))],
        out_shape=[
            jax.ShapeDtypeStruct((HEADS * HEAD, extent), BF),
            jax.ShapeDtypeStruct((groups, group, extent), F32),
        ],
        input_output_aliases={4 + n: n for n in range(len(earlier))},
        scratch_shapes=[
            pltpu.VMEM((group, HEAD + 16, extent), BF),
            pltpu.VMEM((group, HEAD + 16, extent), BF),
            pltpu.VMEM((block // 2, block), F32),
        ],
        compiler_params=params(),
        cost_estimate=estimate(weight * 16 * HEADS * pairs * HEAD / part_of[1], weight * 8e6),
        name="attention",
    )(lengths, project, project, project, *earlier)


def gelu_parts(hidden):
    chance = 0.5 + 0.5 * lax.erf(hidden * 0.7071067811865476)
    density = jnp.exp2(hidden * hidden * (-0.5 * LOG2E)) * 0.3989422804014327
    return hidden * chance, chance + hidden * density


def out_kernel(
    count, tab, lengths, mixture, frames, cotangent, out_bias, gain, shift, *rest
):
    pieces = rest[:count]
    middle, normed, result, down_bias, out_weight, sems = rest[count:]
    step = pl.program_id(0)
    model = mixture.shape[0]

    size = frames.shape[0]

    def fetch():
        return load_all(pieces, tab, out_weight, sems, model // 4, TILE)

    @pl.when(step == 0)
    def _():
        start(fetch())
        down_bias[...] = jnp.zeros_like(down_bias)

    def mask(rows, sums):
        place = step * size + rows.start + lax.broadcasted_iota(jnp.int32, (ROWS, 1), 0)
        masked = jnp.where(place < lengths[0], cotangent[rows, :].astype(F32), 0.0)
        result[rows, :] = masked.astype(BF)
        return sums + masked.sum(0, keepdims=True)

    down_bias[...] += chunks(size, ROWS, mask, jnp.zeros((1, model), F32))

    @pl.when(step == 0)
    def _():
        wait(fetch())

    def branch(rows, carry):
        total = dot(mixture[:, rows], out_weight[...], 0, 0) + out_bias[...]
        total = frames[rows, :].astype(F32) + total
        middle[rows, :] = total
        unit, _ = normalise(total)
        normed[rows, :] = (unit * gain[...] + shift[...]).astype(BF)
        return carry

    chunks(size, ROWS, branch)


def out_call(tab, lengths, mixture, frames, cotangent, vectors, pieces):
    model, extent = mixture.shape
    size = min(512, extent)
    block = pl.BlockSpec((size, model), lambda i: (i, 0))
    return pl.pallas_call(
        functools.partial(out_kernel, len(pieces)),
        grid=(extent // size,),
        in_specs=[SMEM, SMEM]
        + [pl.BlockSpec((model, size), lambda i: (0, i)), block, block]
        + [whole(1, model)] * 3
        + [ANY] * len(pieces),
        out_specs=[block, block, block, whole(1, model)],
        out_shape=[
            jax.ShapeDtypeStruct((extent, model), F32),
            jax.ShapeDtypeStruct((extent, model), BF),
            jax.ShapeDtypeStruct((extent, model), BF),
            vec(model),
        ],
        scratch_shapes=[pltpu.VMEM((model, model), BF), pltpu.SemaphoreType.DMA((32,))],
        compiler_params=params(),
        cost_estimate=estimate(1, 1),
        name="out",
    )(tab, lengths, mixture, frames, cotangent, *vectors, *pieces)


def up_kernel(counts, base, tab, normed, result, up_bias, *rest):
    count_up, count_earlier, count_grad = counts
    up_pieces, rest = rest[:count_up], rest[count_up + count_earlier :]
    active, slope = rest[:2]
    grads, rest = rest[2 : 2 + count_grad], rest[2 + count_grad :]
    weight, staged, graded, sems_up, sems_grad, sem_in = rest
    step = pl.program_id(0)
    steps = pl.num_programs(0)
    extent = normed.shape[0]

    def late():
        return pltpu.make_async_copy(result, graded, sem_in)

    def fetch(index):
        slot = lax.rem(index, 2)
        return load_columns(
            up_pieces, tab, base + index, weight.at[slot], sems_up.at[slot], TILE
        )

    def send(index):
        slot = lax.rem(index, 2)
        return store_row_pair(grads, tab, base + index, staged.at[slot], sems_grad.at[slot])

    @pl.when(step == 0)
    def _():
        start(fetch(step))
        late().start()

    @pl.when(step + 1 < steps)
    def _():
        start(fetch(step + 1))

    wait(fetch(step))
    now = lax.rem(step, 2)

    def widen(rows, carry):
        hidden = dot(normed[rows, :], weight[now], 1, 0) + up_bias[...]
        value, grade = gelu_parts(hidden)
        active[rows, :] = value.astype(BF)
        slope[rows, :] = grade.astype(BF)
        return carry

    chunks(extent, ROWS, widen)

    @pl.when(step == 0)
    def _():
        late().wait()

    @pl.when(step >= 2)
    def _():
        wait(send(step - 2))

    def weigh(columns, carry):
        staged[now, columns, :] = dot(active[:, columns], graded[...], 0, 0).astype(BF)
        return carry

    chunks(TILE, ROWS, weigh)
    start(send(step))

    @pl.when(step == steps - 1)
    def _():
        wait(send(step - 1))
        wait(send(step))


def up_call(
    tab, normed, result, up_bias, up_pieces, spread, sizes, part_of=(0, 1), earlier=(), weight=1.0
):
    extent, model = normed.shape
    hidden = 4 * model
    grads = gradient_shapes(spread, hidden, model, *sizes)
    steps = hidden // TILE // part_of[1]
    base = steps * part_of[0]
    tile = pl.BlockSpec((extent, TILE), lambda i: (0, base + i))
    aliases = {4 + len(up_pieces) + n: n for n in range(len(earlier))}
    return pl.pallas_call(
        functools.partial(up_kernel, (len(up_pieces), len(earlier), len(grads)), base),
        grid=(steps,),
        in_specs=[SMEM, whole(extent, model), ANY]
        + [pl.BlockSpec((1, TILE), lambda i: (0, base + i))]
        + [ANY] * (len(up_pieces) + len(earlier)),
        out_specs=[tile, tile] + [ANY] * len(grads),
        out_shape=[
            jax.ShapeDtypeStruct((extent, hidden), BF),
            jax.ShapeDtypeStruct((extent, hidden), BF),
        ]
        + grads,
        input_output_aliases=aliases,
        scratch_shapes=[
            pltpu.VMEM((2, model, TILE), BF),
            pltpu.VMEM((2, TILE, model), BF),
            pltpu.VMEM((extent, model), BF),
            pltpu.SemaphoreType.DMA((2, 8)),
            pltpu.SemaphoreType.DMA((2, 8)),
            pltpu.SemaphoreType.DMA,
        ],
        compiler_params=params(),
        cost_estimate=estimate(weight * 16 * extent * model * model / part_of[1], weight * 50e6),
        name="up",
    )(tab, normed, result, up_bias, *up_pieces, *earlier)


def back_kernel(counts, tab, mixture, middle, normed, d_result, slope, *rest):
    count_out, count_up, count_down, count_grad = counts
    gain = rest[0]
    rest = rest[1:]
    out_pieces, rest = rest[:count_out], rest[count_out:]
    up_pieces, rest = rest[:count_up], rest[count_up:]
    down_pieces, rest = rest[:count_down], rest[count_down:]
    d_middle, d_mixture, up_bias, gain_grad, shift_grad, out_bias = rest[:6]
    rest = rest[6:]
    grads, rest = rest[:count_grad], rest[count_grad:]
    (
        mixed,
        out_weight,
        total,
        unit_rows,
        result,
        down,
        up,
        d_hidden,
        d_normed,
        staged,
        sems_in,
        sems_out,
        sems_down,
        sems_up,
        sems_grad,
    ) = rest
    spread = len(grads[0].shape) == 4
    if spread:
        up_grads = out_grads = grads
    else:
        up_grads, out_grads = grads[:1], grads[1:]
    step = pl.program_id(0)
    steps = pl.num_programs(0)
    extent, model = result.shape
    width = model // 4

    def fetch(index):
        slot = index % 2
        return load_rows(down_pieces, tab, index, down.at[slot], sems_down.at[slot])

    def fetch_up(index):
        slot = index % 2
        block = tab[T_PAIR + index]
        return load_columns(up_pieces, tab, block, up.at[slot], sems_up.at[slot], TILE)

    def send(index):
        slot = index % 2
        block = tab[T_PAIR + index]
        return store_column_block(
            up_grads, tab, block, staged.at[slot], sems_grad.at[slot], TILE
        )

    def send_out(block):
        return store_column_block(
            out_grads,
            tab,
            block,
            staged.at[0, :, pl.ds(block * width, width)],
            sems_out.at[pl.ds(block * 8, 8)],
            width,
            TILE if spread else 0,
        )

    def early(n):
        pair = ((d_result, result), (normed, unit_rows))[n]
        return pltpu.make_async_copy(*pair, sems_in.at[n])

    def late():
        return [
            pltpu.make_async_copy(middle, total, sems_in.at[2]),
            pltpu.make_async_copy(mixture, mixed, sems_in.at[3]),
        ] + load_all(out_pieces, tab, out_weight, sems_out, width, TILE)

    now = lax.rem(step, 2)

    @pl.when(step == 0)
    def _():
        early(0).start()
        start(fetch(0))
        early(1).start()
        start(fetch_up(0))
        early(0).wait()
        d_normed[...] = jnp.zeros_like(d_normed)

    def arrive(index):
        if index == 2:
            start(late())
        if index + 1 < 4:
            start(fetch(index + 1))
            start(fetch_up(index + 1))
        wait(fetch(index))
        if index >= 2:
            wait(send(index - 2))

    for index in range(4):
        pl.when(step == index)(functools.partial(arrive, index))

    def shrink(rows, sums):
        d_active = dot(result[rows, :], down[now], 1, 1)
        piece = (d_active * slope[rows, :].astype(F32)).astype(BF)
        d_hidden[rows, :] = piece
        return sums + piece.astype(F32).sum(0, keepdims=True)

    up_bias[...] = chunks(extent, ROWS, shrink, jnp.zeros((1, TILE), F32))

    @pl.when(step == 0)
    def _():
        early(1).wait()

    def weigh(columns, carry):
        staged[now, columns, :] = dot(unit_rows[:, columns], d_hidden[...], 0, 0).astype(BF)
        return carry

    chunks(model, ROWS, weigh)
    def leave(index):
        start(send(index))
        wait(fetch_up(index))

    for index in range(4):
        pl.when(step == index)(functools.partial(leave, index))

    def widen(rows, carry):
        d_normed[rows, :] += dot(d_hidden[rows, :], up[now], 1, 1)
        return carry

    @pl.when(step < steps - 1)
    def _():
        chunks(extent, ROWS, widen)

    @pl.when(step == steps - 1)
    def _():
        wait(late())
        none = jnp.zeros((1, model), F32)

        def norm(rows, sums):
            grade = d_normed[rows, :] + dot(d_hidden[rows, :], up[now], 1, 1)
            unit, scale = normalise(total[rows, :])
            gains = sums[0] + (grade * unit).sum(0, keepdims=True)
            shifts = sums[1] + grade.sum(0, keepdims=True)
            grade = grade * gain[...]
            level = jnp.mean(grade, axis=-1, keepdims=True)
            tilt = jnp.mean(grade * unit, axis=-1, keepdims=True)
            d_total = result[rows, :].astype(F32) + scale * (grade - level - unit * tilt)
            d_middle[rows, :] = d_total
            branch = d_total.astype(BF)
            unit_rows[rows, :] = branch
            return gains, shifts, sums[2] + branch.astype(F32).sum(0, keepdims=True)

        sums = chunks(extent, ROWS, norm, (none, none, none))
        gain_grad[...], shift_grad[...], out_bias[...] = sums
        wait(send(2))

        def weigh_out(rows, carry):
            staged[0, rows, :] = dot(mixed[rows, :], unit_rows[...], 1, 0).astype(BF)
            return carry

        chunks(model, ROWS, weigh_out)
        for block in range(4):
            start(send_out(block))

        def turn(rows, carry):
            d_mixture[rows, :] = dot(out_weight[rows, :], unit_rows[...], 1, 1).astype(BF)
            return carry

        chunks(model, ROWS, turn)
        wait(send(3))
        for block in range(4):
            wait(send_out(block))


def back_call(tab, mixture, middle, normed, d_result, slope, gain, pieces, spread, sizes):
    out_pieces, up_pieces, down_pieces = pieces
    model, extent = mixture.shape
    hidden = slope.shape[1]
    if spread:
        grads = gradient_shapes(spread, model, hidden + model, *sizes)
    else:
        grads = gradient_shapes(spread, model, hidden, *sizes)
        grads += gradient_shapes(spread, model, model, *sizes)
    steps = hidden // TILE
    grid = pltpu.PrefetchScalarGridSpec(
        num_scalar_prefetch=1,
        grid=(steps,),
        in_specs=[ANY, ANY, ANY, ANY]
        + [pl.BlockSpec((extent, TILE), lambda i, tab: (0, tab[T_PAIR + i]))]
        + [whole(1, model)]
        + [ANY] * (len(out_pieces) + len(up_pieces) + len(down_pieces)),
        out_specs=[
            whole(extent, model),
            whole(model, extent),
            pl.BlockSpec((1, TILE), lambda i, tab: (0, tab[T_PAIR + i])),
            whole(1, model),
            whole(1, model),
            whole(1, model),
        ]
        + [ANY] * len(grads),
        scratch_shapes=[
            pltpu.VMEM((model, extent), BF),
            pltpu.VMEM((model, model), BF),
            pltpu.VMEM((extent, model), F32),
            pltpu.VMEM((extent, model), BF),
            pltpu.VMEM((extent, model), BF),
            pltpu.VMEM((2, TILE, model), BF),
            pltpu.VMEM((2, model, TILE), BF),
            pltpu.VMEM((extent, TILE), BF),
            pltpu.VMEM((extent, model), F32),
            pltpu.VMEM((2, model, TILE), BF),
            pltpu.SemaphoreType.DMA((4,)),
            pltpu.SemaphoreType.DMA((32,)),
            pltpu.SemaphoreType.DMA((2, 8)),
            pltpu.SemaphoreType.DMA((2, 8)),
            pltpu.SemaphoreType.DMA((2, 8)),
        ],
    )
    return pl.pallas_call(
        functools.partial(
            back_kernel, (len(out_pieces), len(up_pieces), len(down_pieces), len(grads))
        ),
        grid_spec=grid,
        out_shape=[
            jax.ShapeDtypeStruct((extent, model), F32),
            jax.ShapeDtypeStruct((model, extent), BF),
            vec(hidden),
            vec(model),
            vec(model),
            vec(model),
        ]
        + grads,
        compiler_params=params(),
        cost_estimate=estimate(28 * extent * model * model, 60e6),
        name="back",
    )(
        tab,
        mixture,
        middle,
        normed,
        d_result,
        slope,
        gain,
        *out_pieces,
        *up_pieces,
        *down_pieces,
    )


def attention_back_kernel(
    group,
    block,
    lengths,
    query,
    key,
    value,
    mixture,
    d_mixture,
    totals,
    *rest,
):
    d_project, keys, queries, causal, d_keys, d_values = rest[-6:]
    extent = query.shape[1]

    @pl.when(pl.program_id(0) == 0)
    def _():
        causal[...] = causal_bias(block, block)

    key_rows, query_rows = extend_rows(lengths[0], extent)
    for head in range(group):
        part = pl.ds(HEAD * head, HEAD)
        keys[head, :HEAD, :] = key[part, :]
        keys[head, HEAD:, :] = key_rows
        queries[head, :HEAD, :] = query[part, :]
        queries[head, HEAD:, :] = query_rows
    for head in range(group):
        part = pl.ds(HEAD * head, HEAD)
        for tile in range(extent // block):
            place = pl.ds(tile * block, block)
            own = queries[head, :, place]
            grade = d_mixture[part, place]
            center = (grade.astype(F32) * mixture[part, place].astype(F32)).sum(0, keepdims=True)
            total = totals[0, pl.ds(head, 1), place]
            d_query = jnp.zeros((HEAD, block), F32)
            for other in range(tile + 1):
                span = pl.ds(other * block, block)
                score = dot(keys[head, :, span], own, 0, 0)
                if other == tile:
                    score = score + causal[...]
                weight = jnp.exp2(score * (SCALE * LOG2E) - total)
                d_weight = dot(value[part, span], grade, 0, 0)
                d_score = (weight * (d_weight - center)).astype(BF)
                d_value = dot(grade, weight.astype(BF), 1, 1)
                d_key = dot(query[part, place], d_score, 1, 1)
                d_query = d_query + dot(key[part, span], d_score, 1, 0)
                if other == tile:
                    d_values[:, span] = d_value
                    d_keys[:, span] = d_key
                else:
                    d_values[:, span] += d_value
                    d_keys[:, span] += d_key
            d_project[0, part, place] = (d_query * SCALE).astype(BF)
        d_project[1, part, :] = (d_keys[...] * SCALE).astype(BF)
        d_project[2, part, :] = d_values[...].astype(BF)


def attention_back_call(
    lengths, project, mixture, d_mixture, totals, base=0, ending=HEADS // 2, earlier=()
):
    extent = project.shape[1]
    group, block = 2, min(512, extent)
    size, groups = HEAD * group, HEADS // group
    steps = ending - base

    def part(section):
        return pl.BlockSpec((size, extent), lambda i: (i + base + section * groups, 0))

    pairs = extent * extent * 5 // 8
    return pl.pallas_call(
        functools.partial(attention_back_kernel, group, block),
        grid=(steps,),
        in_specs=[SMEM, part(0), part(1), part(2), part(0), part(0)]
        + [pl.BlockSpec((1, group, extent), lambda i: (i + base, 0, 0))]
        + [ANY] * len(earlier),
        out_specs=pl.BlockSpec((3, size, extent), lambda i: (0, i + base, 0)),
        out_shape=jax.ShapeDtypeStruct((3, HEADS * HEAD, extent), BF),
        input_output_aliases={7: 0} if earlier else {},
        scratch_shapes=[
            pltpu.VMEM((group, HEAD + 16, extent), BF),
            pltpu.VMEM((group, HEAD + 16, extent), BF),
            pltpu.VMEM((block, block), F32),
            pltpu.VMEM((HEAD, extent), F32),
            pltpu.VMEM((HEAD, extent), F32),
        ],
        compiler_params=params(),
        cost_estimate=estimate(4 * HEADS * pairs * HEAD * steps / groups, 1e6),
        name="attention_back",
    )(lengths, project, project, project, mixture, d_mixture, totals, *earlier)


def attend_grad_kernel(count_grad, tab, d_project, normed, *rest):
    bias_grad = rest[0]
    grads, rest = rest[1 : 1 + count_grad], rest[1 + count_grad :]
    staged, sems_grad = rest
    step = pl.program_id(0)
    steps = pl.num_programs(0)
    extent, model = normed.shape
    width = d_project.shape[0]

    def send(block):
        slot = lax.rem(block, 2)
        return store_column_block(grads, tab, block, staged.at[slot], sems_grad.at[slot], width)

    @pl.when(step >= 2)
    def _():
        wait(send(step - 2))

    now = lax.rem(step, 2)

    def weigh(columns, carry):
        staged[now, columns, :] = dot(normed[:, columns], d_project[...], 0, 1).astype(BF)
        return carry

    chunks(model, ROWS, weigh)
    start(send(step))
    sums = d_project[...].astype(F32).sum(1, keepdims=True)
    bias_grad[...] = jnp.transpose(jnp.broadcast_to(sums, (width, 128)))[:1, :]

    @pl.when(step == steps - 1)
    def _():
        wait(send(step - 1))
        wait(send(step))


def attend_grad_call(tab, d_project, normed, spread, sizes):
    extent, model = normed.shape
    width = 3 * model // 4
    grads = gradient_shapes(spread, model, 3 * model, *sizes)
    return pl.pallas_call(
        functools.partial(attend_grad_kernel, len(grads)),
        grid=(4,),
        in_specs=[SMEM, pl.BlockSpec((width, extent), lambda i: (i, 0)), whole(extent, model)],
        out_specs=[pl.BlockSpec((1, width), lambda i: (0, i))] + [ANY] * len(grads),
        out_shape=[vec(3 * model)] + grads,
        scratch_shapes=[
            pltpu.VMEM((2, model, width), BF),
            pltpu.SemaphoreType.DMA((2, 8)),
        ],
        compiler_params=params(),
        cost_estimate=estimate(6 * extent * model * model, 14e6),
        name="attend_grad",
    )(tab, d_project, normed)


def first_kernel(count_in, tab, d_project, frames, d_middle, gain, *rest):
    pieces, rest = rest[:count_in], rest[count_in:]
    bias_grad, *early = rest[:6]
    d_frames, small, weight, total, d_normed, sems, sem_total = rest[6:]
    step = pl.program_id(0)
    steps = pl.num_programs(0)
    extent, model = frames.shape
    width = d_project.shape[0]

    def fetch(index):
        slot = index % 2
        return load_slot(pieces, tab, index, weight.at[slot], sems.at[slot], width)

    def late():
        return pltpu.make_async_copy(d_middle, total, sem_total)

    @pl.when(step == 0)
    def _():
        start(fetch(0))
        late().start()
        d_normed[...] = jnp.zeros_like(d_normed)

    def arrive(index):
        if index + 1 < 4:
            start(fetch(index + 1))
        wait(fetch(index))

    for index in range(4):
        pl.when(step == index)(functools.partial(arrive, index))
    now = lax.rem(step, 2)

    def widen(rows, carry):
        d_normed[rows, :] += dot(d_project[:, rows], weight[now], 0, 1)
        return carry

    @pl.when(step < steps - 1)
    def _():
        chunks(extent, ROWS, widen)

    @pl.when(step == steps - 1)
    def _():
        late().wait()
        none = jnp.zeros((1, model), F32)

        def norm(rows, sums):
            grade = d_normed[rows, :] + dot(d_project[:, rows], weight[now], 0, 1)
            unit, scale = normalise(frames[rows, :].astype(F32))
            gains = sums[0] + (grade * unit).sum(0, keepdims=True)
            shifts = sums[1] + grade.sum(0, keepdims=True)
            grade = grade * gain[...]
            level = jnp.mean(grade, axis=-1, keepdims=True)
            tilt = jnp.mean(grade * unit, axis=-1, keepdims=True)
            d_frames[rows, :] = (total[rows, :] + scale * (grade - level - unit * tilt)).astype(BF)
            return gains, shifts

        gains, shifts = chunks(extent, ROWS, norm, (none, none))
        bias = bias_grad[...]
        vectors = [gains, shifts, bias[:, :model], bias[:, 2 * model :]]
        vectors += [vector[...] for vector in early]
        place = 0
        for vector in vectors:
            for column in range(0, vector.shape[1], 128):
                small[place : place + 1, :] = vector[:, column : column + 128]
                place += 1


def small_kernel(*refs):
    *terms, a, b, c, d, e, f, g, h = refs
    terms = [term[...] for term in terms]
    total = tree_sum(terms)
    place = 0
    for out in (a, b, c, d, e, f, g, h):
        if out.shape[1] == 128:
            out[...] = total[place : place + out.shape[0], :]
            place += out.shape[0]
            continue
        for row in range(out.shape[0]):
            for column in range(0, out.shape[1], 128):
                out[row : row + 1, column : column + 128] = total[place : place + 1, :]
                place += 1


def small_call(terms):
    unit = terms[0].shape[0] // 12
    sizes = [unit, unit, 2 * unit, unit, unit, unit, unit, 4 * unit]
    return pl.pallas_call(
        small_kernel,
        out_shape=[
            jax.ShapeDtypeStruct((size, 128) if n != 2 else (2, size * 64), F32)
            for n, size in enumerate(sizes)
        ],
        name="small",
    )(*terms)


def first_call(tab, d_project, frames, d_middle, gain, pieces, vectors):
    extent, model = frames.shape
    width = 3 * model // 4
    count = model + sum(vector.shape[1] for vector in vectors)
    grid = pltpu.PrefetchScalarGridSpec(
        num_scalar_prefetch=1,
        grid=(4,),
        in_specs=[pl.BlockSpec((width, extent), lambda i, tab: (tab[T_COL + i], 0))]
        + [whole(extent, model), ANY, whole(1, model)]
        + [ANY] * len(pieces)
        + [whole(*vector.shape) for vector in vectors],
        out_specs=[whole(extent, model), whole(count // 128, 128)],
        scratch_shapes=[
            pltpu.VMEM((2, model, width), BF),
            pltpu.VMEM((extent, model), F32),
            pltpu.VMEM((extent, model), F32),
            pltpu.SemaphoreType.DMA((2, 8)),
            pltpu.SemaphoreType.DMA,
        ],
    )
    return pl.pallas_call(
        functools.partial(first_kernel, len(pieces)),
        grid_spec=grid,
        out_shape=[
            jax.ShapeDtypeStruct((extent, model), BF),
            jax.ShapeDtypeStruct((count // 128, 128), F32),
        ],
        compiler_params=params(),
        cost_estimate=estimate(6 * extent * model * model, 24e6),
        name="first",
    )(tab, d_project, frames, d_middle, gain, *pieces, *vectors)


def down_kernel(count, count_earlier, row, tab, active, middle, bias, *rest):
    pieces = rest[:count]
    frames_out, weight, total, base, sems, sem_base = rest[count + count_earlier :]
    step = pl.program_id(0)
    steps = pl.num_programs(0)
    extent = total.shape[0]

    def fetch(index):
        slot = index % 2
        return load_rows(pieces, tab, index, weight.at[slot], sems.at[slot])

    def late():
        return pltpu.make_async_copy(middle.at[pl.ds(row * extent, extent), :], base, sem_base)

    def arrive(index):
        if index == 0:
            start(fetch(index))
            late().start()
        if index + 1 < 4:
            start(fetch(index + 1))
        wait(fetch(index))

    for index in range(4):
        pl.when(step == index)(functools.partial(arrive, index))
    now = lax.rem(step, 2)

    @pl.when(step < steps - 1)
    def _():
        def widen(rows, carry):
            before = jnp.where(step == 0, 0.0, total[rows, :])
            total[rows, :] = before + dot(active[rows, :], weight[now], 1, 0)
            return carry

        chunks(extent, ROWS, widen)

    @pl.when(step == steps - 1)
    def _():
        late().wait()

        def finish(rows, carry):
            result = total[rows, :] + dot(active[rows, :], weight[now], 1, 0)
            frames_out[rows, :] = (result + (base[rows, :] + bias[...])).astype(BF)
            return carry

        chunks(extent, ROWS, finish)


def down_call(tab, active, middle, bias, pieces, part_of=(0, 1), earlier=()):
    extent, hidden = active.shape
    model = middle.shape[1]
    row, size = part_of[0], extent // part_of[1]
    grid = pltpu.PrefetchScalarGridSpec(
        num_scalar_prefetch=1,
        grid=(hidden // TILE,),
        in_specs=[pl.BlockSpec((size, TILE), lambda i, tab: (row, tab[T_PAIR + i]))]
        + [ANY, whole(1, model)]
        + [ANY] * (len(pieces) + len(earlier)),
        out_specs=pl.BlockSpec((size, model), lambda i, tab: (row, 0)),
        scratch_shapes=[
            pltpu.VMEM((2, TILE, model), BF),
            pltpu.VMEM((size, model), F32),
            pltpu.VMEM((size, model), F32),
            pltpu.SemaphoreType.DMA((2, 8)),
            pltpu.SemaphoreType.DMA,
        ],
    )
    return pl.pallas_call(
        functools.partial(down_kernel, len(pieces), len(earlier), row),
        grid_spec=grid,
        out_shape=jax.ShapeDtypeStruct((extent, model), BF),
        input_output_aliases={4 + len(pieces): 0} if earlier else {},
        compiler_params=params(),
        cost_estimate=estimate(8 * size * model * model, 24e6),
        name="down",
    )(tab, active, middle, bias, *pieces, *earlier)


def gather_plain(weight):
    wide = lax.all_gather(weight, "inner", axis=1, tiled=True)
    return [lax.all_gather(wide, "dp", axis=0, tiled=True)]


def scatter_plain(grads):
    wide = lax.psum_scatter(grads[0], "dp", scatter_dimension=0, tiled=True)
    return lax.psum_scatter(wide, "inner", scatter_dimension=1, tiled=True).astype(F32)


CORE, NEAR, FAR = 0, 1, 2


def swap(value, way):
    flips = {CORE: (1, 1), NEAR: (2, 4), FAR: (4, 2)}[way]
    return lax.ppermute(value, "dp", [(d, d ^ flips[d & 1]) for d in range(8)])


def shift(value, amount):
    return lax.ppermute(value, "inner", [(i, (i + amount) & 3) for i in range(4)])


def after(value, *done):
    return lax.optimization_barrier((value, done))[0]


def stack_spread(block):
    return jnp.stack([block] + [shift(block, amount) for amount in (1, 2, 3)])


def added(*values):
    total = values[0].astype(F32)
    for value in values[1:]:
        total = total + value.astype(F32)
    return total


def add_kernel(count, *refs):
    total = added(*[ref[...] for ref in refs[:count]])
    outs = refs[count:]
    if len(outs) == 1:
        outs[0][...] = total.reshape(outs[0].shape).astype(BF)
        return
    for index, out in enumerate(outs):

        @pl.when(pl.program_id(0) == index)
        def _(out=out):
            out[...] = total.reshape(out.shape).astype(out.dtype)


def add_call(terms, outs, grid):
    rows, columns = terms[0][0].shape[-2:]
    specs = []
    for term, place in terms:
        if term.ndim == 3:
            specs.append(pl.BlockSpec((1, rows, columns), lambda *at: (at[-1], 0, 0)))
        elif place is None:
            specs.append(pl.BlockSpec((1, 1, rows, columns), lambda p, k: (p, k, 0, 0)))
        else:
            specs.append(
                pl.BlockSpec((1, 1, rows, columns), lambda k, place=place: (place, k, 0, 0))
            )
    if len(outs) == 1:
        lead = (1,) * len(grid)
        out_specs = [pl.BlockSpec(lead + (rows, columns), lambda *at: at + (0, 0))]
    else:
        out_specs = [whole(rows, columns)] * len(outs)

    def kernel(*refs):
        ins = [
            ref.at[0] if len(ref.shape) == 3 else ref.at[0, 0] for ref in refs[: len(terms)]
        ]
        add_kernel(len(terms), *ins, *refs[len(terms) :])

    return pl.pallas_call(
        kernel,
        grid=grid,
        in_specs=specs,
        out_specs=out_specs,
        out_shape=outs,
        compiler_params=params(),
        cost_estimate=estimate(1e10, 1e7),
        name="add",
    )(*[term for term, _ in terms])


def add_first(keep, core):
    return added(keep[:2], core[:2]).astype(BF)


def add_second(keep, core, link):
    return added(keep[2], core[2], link[0]).astype(BF)


def add_third(keep, core, link, last):
    blocks = [added(keep[3, k], core[3, k], link[1, k], last[k]) for k in range(4)]
    return [blocks[0]] + [block.astype(BF) for block in blocks[1:]]


def add_third_kernel(keep, core, link, last):
    shapes = [jax.ShapeDtypeStruct(keep.shape[2:], F32)]
    shapes += [jax.ShapeDtypeStruct(keep.shape[2:], BF)] * 3
    return add_call([(keep, 3), (core, 3), (link, 1), (last, None)], shapes, (4,))


def shift_parts(parts):
    return [shift(parts[k], k) for k in (1, 2, 3)]


def exchange(values, axis, size):
    return [values] + [
        lax.ppermute(values, axis, [(i, i ^ flip) for i in range(size)])
        for flip in range(1, size)
    ]


def tree_sum(terms):
    while len(terms) > 1:
        terms = [terms[i] + terms[i + 1] for i in range(0, len(terms), 2)]
    return terms[0]


def shards(
    spread,
    sizes,
    frames_in,
    lengths,
    first_gain,
    first_shift,
    attend_weight,
    attend_bias,
    output_weight,
    output_bias,
    second_gain,
    second_shift,
    up_weight,
    up_bias,
    down_weight,
    down_bias,
    cotangent,
):
    _, extent, model = frames_in.shape
    frames = frames_in.reshape(extent, model)
    upstream = cotangent.reshape(extent, model)
    tab = make_table(spread, True)
    tab_plain = make_table(spread, False)

    def row(vector):
        return vector.reshape(1, -1)

    if not spread:
        attend_pieces = gather_plain(attend_weight)
        out_pieces = gather_plain(output_weight)
        up_pieces = gather_plain(up_weight)
        down_pieces = gather_plain(down_weight)
    else:
        others = [shift(attend_weight, amount) for amount in (1, 2, 3)]
        up_block = jnp.concatenate([up_weight, output_weight], axis=1)
        near, far = swap(attend_weight, NEAR), swap(attend_weight, FAR)
        others = jnp.stack(others)
        far, near = after((far, near), near, far)
        diagonal = swap(near, FAR)
        attend_pieces = [attend_weight, near, far, diagonal]
        attend_pieces += [swap(piece, CORE) for piece in attend_pieces]
        others = after(others, diagonal)
        near, far = swap(others, NEAR), swap(others, FAR)
        up_block = after(up_block, others)
        up_own = lax.all_gather(up_block, "inner")
        near, far = after((near, far), near, far)
        diagonal = swap(near, FAR)
        others = [others, near, far, diagonal]
        attend_pieces += others + [swap(piece, CORE) for piece in others]
        up_own = after(up_own, *attend_pieces)
        up_near, up_far = swap(up_own, NEAR), swap(up_own, FAR)
        down_own = lax.all_gather(after(down_weight, up_own), "inner")
    bias_row = jnp.concatenate([attend_bias[0], jnp.zeros_like(attend_bias[0]), attend_bias[1]])
    vectors = (row(first_gain), row(first_shift), row(bias_row))
    tokens = after(frames, up_own) if spread else frames
    normed, project = project_call(tab, tokens, *vectors, attend_pieces)
    if spread:
        mixture, totals = attention_call(lengths, after(project, up_own), (0, 2))
        up_near, up_far = after((up_near, up_far), totals)
        up_diagonal = swap(up_near, FAR)
        ahead = [swap(piece, CORE) for piece in (after(up_own, totals), up_near, up_far)]
        mixture, totals = attention_call(
            lengths, after(project, up_near, up_far, down_own), (1, 2), (mixture, totals)
        )
        up_pieces = [up_own, up_near, up_far, up_diagonal]
        up_pieces += ahead + [swap(after(up_diagonal, totals), CORE)]
        out_pieces = up_pieces
    else:
        mixture, totals = attention_call(lengths, project)
    vectors = (row(output_bias), row(second_gain), row(second_shift))
    if spread:
        down_near, down_far = swap(down_own, NEAR), swap(down_own, FAR)
    middle, normed_two, d_result, grad_down_bias = out_call(
        tab_plain, lengths, mixture, frames, upstream, vectors, out_pieces
    )
    if spread:
        *halves, half_grad = up_call(
            tab_plain,
            normed_two,
            d_result,
            row(up_bias),
            up_pieces,
            False,
            sizes,
            (0, 2),
        )
        down_near, down_far = after((down_near, down_far), halves)
        down_diagonal = swap(down_near, FAR)
        ahead = [swap(piece, CORE) for piece in (after(down_own, totals), down_near, down_far)]
        active, slope, *down_grads = up_call(
            tab_plain,
            after(normed_two, down_near, down_far),
            d_result,
            row(up_bias),
            up_pieces,
            False,
            sizes,
            (1, 2),
            (*halves, half_grad),
        )
    else:
        active, slope, *down_grads = up_call(
            tab_plain, normed_two, d_result, row(up_bias), up_pieces, False, sizes
        )
    if spread:
        down_pieces = [down_own, down_near, down_far, down_diagonal]
        down_pieces += ahead + [swap(after(down_diagonal, slope), CORE)]
        down_wide = lax.psum_scatter(down_grads[0], "dp", scatter_dimension=0, tiled=True)
    else:
        down_owned = scatter_plain(down_grads)
    (
        d_middle,
        d_mixture,
        grad_up_bias,
        grad_second_gain,
        grad_second_shift,
        grad_output_bias,
        *back_grads,
    ) = back_call(
        tab_plain,
        mixture,
        middle,
        normed_two,
        d_result,
        slope,
        row(second_gain),
        (out_pieces, up_pieces, down_pieces),
        spread,
        sizes,
    )
    early = [grad_output_bias, grad_second_gain, grad_second_shift, grad_down_bias, grad_up_bias]
    if spread:
        back_keep, back_send = back_grads
        back_core = swap(back_send, CORE)
        d_project = attention_back_call(lengths, project, mixture, d_mixture, totals, 0, 2)
        back_core = after(back_core, d_project)
        back_first = add_first(back_keep, back_core)
        back_link = swap(back_first, FAR)
        d_mixture = after(d_mixture, back_first)
        d_project = attention_back_call(
            lengths, project, mixture, d_mixture, totals, 2, HEADS // 2, (d_project,)
        )
        back_link, down_wide = after((back_link, down_wide), d_project)
        down_owned = lax.psum_scatter(down_wide, "inner", scatter_dimension=1, tiled=True)
        back_second = add_second(back_keep, back_core, back_link)
        back_last = swap(back_second, NEAR)
        d_rows = after(d_project, back_second, down_wide).reshape(3 * model, extent)
        grad_bias, attend_keep, attend_send = attend_grad_call(tab, d_rows, normed, spread, sizes)
        attend_core = swap(attend_send, CORE)
        back_last = after(back_last, grad_bias)
        back_parts = add_third_kernel(back_keep, back_core, back_link, back_last)
        back_others = shift_parts(back_parts)
        attend_core = after(attend_core, back_parts)
        attend_first = add_first(attend_keep, attend_core)
        attend_link = swap(attend_first, FAR)
        d_frames, small = first_call(
            tab,
            after(d_rows, attend_first),
            frames,
            d_middle,
            row(first_gain),
            attend_pieces,
            [grad_bias] + early,
        )
        attend_link, down_owned = after((attend_link, down_owned), d_frames)
        attend_second = add_second(attend_keep, attend_core, attend_link)
        attend_last = swap(attend_second, NEAR)
        small_terms = exchange(small, "inner", 4)
        active, middle = after((active, middle), attend_second, down_owned)
        frames_out = down_call(tab_plain, active, middle, row(down_bias), down_pieces)
        attend_last, back_others, small_terms = after(
            (attend_last, back_others, small_terms), frames_out
        )
        back_owned = added(back_parts[0], *back_others)
        small = tree_sum(small_terms)
        attend_parts = add_third(attend_keep, attend_core, attend_link, attend_last)
        attend_parts, small = after((attend_parts, small), back_owned, small, attend_parts)
        others = shift_parts(attend_parts)
        small = small + lax.ppermute(small, "dp", [(i, i ^ 1) for i in range(8)])
        small_terms = [small] + [
            lax.ppermute(small, "dp", [(i, i ^ flip) for i in range(8)]) for flip in (2, 4, 6)
        ]
        attend_owned = added(attend_parts[0], *others)
        small = small_call(after(small_terms, attend_owned))
        down_owned = down_owned.astype(F32)
        up_owned, output_owned = back_owned[:, :TILE], back_owned[:, TILE:]
    else:
        d_project = attention_back_call(lengths, project, mixture, d_mixture, totals)
        d_rows = d_project.reshape(3 * model, extent)
        grad_bias, *attend_grads = attend_grad_call(tab, d_rows, normed, spread, sizes)
        d_frames, small = first_call(
            tab,
            d_rows,
            frames,
            d_middle,
            row(first_gain),
            attend_pieces,
            [grad_bias] + early,
        )
        frames_out = down_call(tab_plain, active, middle, row(down_bias), down_pieces)
        up_owned = scatter_plain(back_grads[:1])
        output_owned = scatter_plain(back_grads[1:])
        attend_owned = scatter_plain(attend_grads)
        small = small_call([lax.psum(small, ("dp", "inner"))])
    small = [vector if n == 2 else vector.reshape(-1) for n, vector in enumerate(small)]

    return (
        frames_out.reshape(frames_in.shape),
        d_frames.reshape(frames_in.shape),
        small[0],
        small[1],
        attend_owned,
        small[2],
        output_owned,
        small[3],
        small[4],
        small[5],
        up_owned,
        small[7],
        down_owned,
        small[6],
    )


def solution(mesh):
    sizes = (mesh.shape["dp"], mesh.shape["inner"])
    spread = sizes == (8, 4)
    return jax.shard_map(
        functools.partial(shards, spread, sizes),
        mesh=mesh,
        in_specs=(
            P(("dp", "inner"), None, None),
            P(("dp", "inner")),
            P(),
            P(),
            P("dp", "inner"),
            P(),
            P("dp", "inner"),
            P(),
            P(),
            P(),
            P("dp", "inner"),
            P(),
            P("dp", "inner"),
            P(),
            P(("dp", "inner"), None, None),
        ),
        out_specs=(
            P(("dp", "inner"), None, None),
            P(("dp", "inner"), None, None),
            P(),
            P(),
            P("dp", "inner"),
            P(),
            P("dp", "inner"),
            P(),
            P(),
            P(),
            P("dp", "inner"),
            P(),
            P("dp", "inner"),
            P(),
        ),
        check_vma=False,
    )
```

```python
import functools

import jax
import jax.numpy as jnp
from jax import lax
from jax.experimental import pallas as pl
from jax.experimental.pallas import tpu as pltpu
from jax.sharding import PartitionSpec as P

HEADS = 16
HEAD = 64
TILE = 1024
ROWS = 512
LOG2E = 1.4426950408889634
MASKED = -1e30
SCALE = HEAD ** (-0.5)
BF = jnp.bfloat16
F32 = jnp.float32
LIMIT = 60 * 2**20


def dot(left, right, on_left, on_right):
    return lax.dot_general(
        left, right, (((on_left,), (on_right,)), ((), ())), preferred_element_type=F32
    )


def normalise(values):
    center = values - jnp.mean(values, axis=-1, keepdims=True)
    spread = jnp.mean(center * center, axis=-1, keepdims=True)
    scale = lax.rsqrt(spread + 1e-05)
    return center * scale, scale


def params(name_limit=LIMIT):
    return pltpu.CompilerParams(vmem_limit_bytes=name_limit)


def estimate(flops, moved, exps=0):
    return pl.CostEstimate(
        flops=int(8 * flops), bytes_accessed=int(8 * moved), transcendentals=int(8 * exps)
    )


ANY = pl.BlockSpec(memory_space=pl.ANY)
SMEM = pl.BlockSpec(memory_space=pltpu.SMEM)


def whole(*shape):
    return pl.BlockSpec(shape, lambda *_: (0,) * len(shape))


def vec(size):
    return jax.ShapeDtypeStruct((1, size), F32)


PIECES = 8
SLOTS = 4
T_ROW = 0
T_COL = 8
T_SLOT_IN = 12
T_SLOT_OUT = 16
T_PAIR = 20
T_OUT = 24
T_PLACE = 32
T_CORE = 40
T_SIZE = 48


def make_table(spread, relative):
    if not spread:
        order = list(range(4))
        entries = [0] * T_SIZE
        entries[T_PAIR : T_PAIR + 4] = order
        entries[T_COL : T_COL + 4] = order
        return jnp.array(entries, jnp.int32)
    row = lax.axis_index("dp").astype(jnp.int32)
    column = lax.axis_index("inner").astype(jnp.int32)
    core = row & 1
    near = jnp.where(core == 0, 2, 4)
    far = 6 - near
    entries = [
        row,
        row ^ near,
        row ^ far,
        row ^ 6,
        row ^ 1,
        row ^ 1 ^ far,
        row ^ 1 ^ near,
        row ^ 7,
    ]
    if relative:
        entries += [(column - block) & 3 for block in range(4)] * 2
    else:
        entries += [0, 1, 2, 3] * 2
    entries += [(block - column) & 3 for block in range(4)]
    pair = row >> 1
    entries += [pair, pair ^ (near >> 1), pair ^ (far >> 1), pair ^ 3]
    for half in range(2):
        a, b = (far, near) if half == 0 else (near, far)
        own = row ^ half
        entries += [own ^ 6, own ^ a, own ^ b, own]
    for half in range(2):
        first = far if half == 0 else near
        for block in range(4):
            relative = (pair ^ block) << 1
            entries.append(
                jnp.where(
                    relative == 6,
                    0,
                    jnp.where(relative == 0, 3, jnp.where(relative == first, 1, 2)),
                )
            )
    entries += [core]
    entries += [jnp.int32(0)] * (T_SIZE - len(entries))
    return jnp.stack([jnp.asarray(entry, jnp.int32) for entry in entries])


def aligned(index, size):
    return pl.ds(pl.multiple_of(index * size, size), size)


def load_slot(pieces, tab, step, target, sems, width):
    if len(pieces) == 1:
        return load_columns(pieces, tab, tab[T_COL + step], target, sems, width)
    rows = pieces[0].shape[-2]
    copies = []
    for p in range(PIECES):
        source = pieces[p] if step == 0 else pieces[PIECES + p].at[step - 1]
        place = target.at[aligned(tab[T_ROW + p], rows), :]
        copies.append(pltpu.make_async_copy(source, place, sems.at[p]))
    return copies


def load_columns(pieces, tab, block, target, sems, width, first=0):
    if len(pieces) == 1:
        copies = [
            pltpu.make_async_copy(pieces[0].at[:, aligned(block, width)], target, sems.at[0])
        ]
        return copies
    slot = tab[T_SLOT_IN + block]
    rows = pieces[0].shape[1]
    return [
        pltpu.make_async_copy(
            pieces[p].at[slot, :, pl.ds(first, width)],
            target.at[aligned(tab[T_ROW + p], rows), :],
            sems.at[p],
        )
        for p in range(PIECES)
    ]


def load_rows(pieces, tab, step, target, sems):
    if len(pieces) == 1 and len(pieces[0].shape) == 2:
        return [
            pltpu.make_async_copy(
                pieces[0].at[aligned(tab[T_PAIR + step], TILE), :], target, sems.at[0]
            )
        ]
    rows, width = pieces[0].shape[-2:]
    if len(pieces) == 1:
        return [
            pltpu.make_async_copy(
                pieces[0].at[2 * tab[T_PAIR + step] + half, block],
                target.at[pl.ds(half * rows, rows), pl.ds(block * width, width)],
                sems.at[half * SLOTS + block],
            )
            for half in range(2)
            for block in range(4)
        ]
    partner = (4, 6, 5, 7)[step]
    copies = []
    for n, p in enumerate((step, partner)):
        half = tab[T_ROW + p] & 1
        for slot in range(SLOTS):
            copies.append(
                pltpu.make_async_copy(
                    pieces[p].at[slot],
                    target.at[aligned(half, rows), aligned(tab[T_COL + slot], width)],
                    sems.at[n * SLOTS + slot],
                )
            )
    return copies


def load_all(pieces, tab, target, sems, width, first=0):
    if len(pieces) == 1:
        return [pltpu.make_async_copy(pieces[0], target, sems.at[0])]
    rows = pieces[0].shape[1]
    return [
        pltpu.make_async_copy(
            pieces[p].at[slot, :, pl.ds(first, width)],
            target.at[aligned(tab[T_ROW + p], rows), aligned(tab[T_COL + slot], width)],
            sems.at[p * SLOTS + slot],
        )
        for p in range(PIECES)
        for slot in range(SLOTS)
    ]


def store_column_block(outs, tab, block, source, sems, width, first=0):
    if len(outs) == 1:
        return [pltpu.make_async_copy(source, outs[0].at[:, aligned(block, width)], sems.at[0])]
    rows = outs[0].shape[2]
    slot = tab[T_SLOT_OUT + block]
    return [
        pltpu.make_async_copy(
            source.at[aligned(tab[T_OUT + half * 4 + place], rows), :],
            outs[half].at[place, slot, :, pl.ds(first, width)],
            sems.at[half * 4 + place],
        )
        for half in range(2)
        for place in range(4)
    ]


def store_row_pair(outs, tab, pair, source, sems):
    if len(outs) == 1:
        return [pltpu.make_async_copy(source, outs[0].at[aligned(pair, TILE), :], sems.at[0])]
    rows, width = outs[0].shape[2:]
    copies = []
    for half in range(2):
        local = tab[T_CORE] ^ half
        for block in range(4):
            copies.append(
                pltpu.make_async_copy(
                    source.at[aligned(local, rows), pl.ds(block * width, width)],
                    outs[half].at[tab[T_PLACE + half * 4 + pair], tab[T_SLOT_OUT + block]],
                    sems.at[half * 4 + block],
                )
            )
    return copies


def chunks(extent, size, body, init=0):
    for first in range(0, extent, size):
        init = body(pl.ds(first, size), init)
    return init


def start(copies):
    for copy in copies:
        copy.start()


def wait(copies):
    for copy in copies:
        copy.wait()


def gradient_shapes(spread, rows, columns, dp, inner):
    if spread:
        return [jax.ShapeDtypeStruct((4, 4, rows // dp, columns // inner), BF)] * 2
    return [jax.ShapeDtypeStruct((rows, columns), BF)]


def project_kernel(count, tab, tokens, gain, shift, bias, *rest):
    pieces = rest[:count]
    normed, project, weight, sems = rest[count:]
    step = pl.program_id(0)
    width = project.shape[0]

    def fetch(index):
        slot = index % 2
        return load_slot(pieces, tab, index, weight.at[slot], sems.at[slot], width)

    @pl.when(step == 0)
    def _():
        start(fetch(0))

        def norm(rows, carry):
            unit, _ = normalise(tokens[rows, :].astype(F32))
            normed[rows, :] = (unit * gain[...] + shift[...]).astype(BF)
            return carry

        chunks(tokens.shape[0], ROWS, norm)

    def arrive(index):
        if index + 1 < 4:
            start(fetch(index + 1))
        wait(fetch(index))

    for index in range(4):
        pl.when(step == index)(functools.partial(arrive, index))

    column = jnp.transpose(jnp.broadcast_to(bias[...], (128, width)))[:, :1]

    project[...] = (dot(weight[lax.rem(step, 2)], normed[...], 0, 1) + column).astype(BF)


def project_call(tab, tokens, gain, shift, bias, pieces):
    extent, model = tokens.shape
    width = 3 * model // 4
    grid = pltpu.PrefetchScalarGridSpec(
        num_scalar_prefetch=1,
        grid=(4,),
        in_specs=[whole(extent, model), whole(1, model), whole(1, model)]
        + [pl.BlockSpec((1, width), lambda i, tab: (0, tab[T_COL + i]))]
        + [ANY] * len(pieces),
        out_specs=[
            whole(extent, model),
            pl.BlockSpec((width, extent), lambda i, tab: (tab[T_COL + i], 0)),
        ],
        scratch_shapes=[
            pltpu.VMEM((2, model, width), BF),
            pltpu.SemaphoreType.DMA((2, 8)),
        ],
    )
    return pl.pallas_call(
        functools.partial(project_kernel, len(pieces)),
        grid_spec=grid,
        out_shape=[
            jax.ShapeDtypeStruct((extent, model), BF),
            jax.ShapeDtypeStruct((3 * model, extent), BF),
        ],
        compiler_params=params(),
        cost_estimate=estimate(1e6, 1e4),
        name="project",
    )(tab, tokens, gain, shift, bias, *pieces)


def causal_bias(keys, queries):
    key = lax.broadcasted_iota(jnp.int32, (keys, queries), 0)
    query = lax.broadcasted_iota(jnp.int32, (keys, queries), 1)
    return jnp.where(key <= query, 0.0, MASKED)


def extend_rows(length, extent):
    first = lax.broadcasted_iota(jnp.int32, (16, extent), 0) == 0
    past = lax.broadcasted_iota(jnp.int32, (16, extent), 1) >= length
    key_rows = jnp.where(first & past, MASKED, 0.0).astype(BF)
    query_rows = jnp.where(first, 1.0, 0.0).astype(BF)
    return key_rows, query_rows


def attention_kernel(group, block, lengths, query, key, value, *rest):
    mixture, totals, keys, queries, causal = rest[-5:]
    extent = query.shape[1]

    half = block // 2

    @pl.when(pl.program_id(0) == 0)
    def _():
        causal[...] = causal_bias(half, block)

    key_rows, query_rows = extend_rows(lengths[0], extent)
    for head in range(group):
        part = pl.ds(HEAD * head, HEAD)
        keys[head, :HEAD, :] = key[part, :]
        keys[head, HEAD:, :] = key_rows
        queries[head, :HEAD, :] = query[part, :]
        queries[head, HEAD:, :] = query_rows
    for head in range(group):
        part = pl.ds(HEAD * head, HEAD)
        for tile in range(extent // block):
            first = tile * block
            place = pl.ds(first, block)
            later = pl.ds(first + half, half)
            spans = [pl.ds(other * block, block) for other in range(tile)] + [pl.ds(first, half)]
            own = queries[head, :, place]
            scores = [dot(keys[head, :, span], own, 0, 0) for span in spans]
            scores[-1] = scores[-1] + causal[...]
            corner = dot(keys[head, :, later], queries[head, :, later], 0, 0) + causal[:, :half]
            highest = scores[0].max(0, keepdims=True)
            for score in scores[1:]:
                highest = jnp.maximum(highest, score.max(0, keepdims=True))
            corner_highest = jnp.maximum(highest[:, half:], corner.max(0, keepdims=True))
            highest = jnp.concatenate([highest[:, :half], corner_highest], axis=1)
            offset = highest * (SCALE * LOG2E)
            weight = jnp.exp2(corner * (SCALE * LOG2E) - offset[:, half:])
            corner_summed = weight.sum(0, keepdims=True)
            corner_total = dot(value[part, later], weight.astype(BF), 1, 0)
            summed = jnp.zeros((1, block), F32)
            total = jnp.zeros((HEAD, block), F32)
            for span, score in zip(spans, scores):
                weight = jnp.exp2(score * (SCALE * LOG2E) - offset)
                summed = summed + weight.sum(0, keepdims=True)
                total = total + dot(value[part, span], weight.astype(BF), 1, 0)
            summed = jnp.concatenate([summed[:, :half], summed[:, half:] + corner_summed], axis=1)
            total = jnp.concatenate([total[:, :half], total[:, half:] + corner_total], axis=1)
            mixture[part, place] = (total * (1.0 / summed)).astype(BF)
            totals[0, pl.ds(head, 1), place] = offset + jnp.log2(summed)


def attention_call(lengths, project, part_of=(0, 1), earlier=(), weight=0.001):
    extent = project.shape[1]
    group, block = 2, min(512, extent)
    size, groups = HEAD * group, HEADS // group
    steps = groups // part_of[1]
    base = steps * part_of[0]

    def part(section):
        return pl.BlockSpec((size, extent), lambda i: (i + base + section * groups, 0))

    pairs = extent * extent * 5 // 8
    return pl.pallas_call(
        functools.partial(attention_kernel, group, block),
        grid=(steps,),
        in_specs=[SMEM, part(0), part(1), part(2)] + [ANY] * len(earlier),
        out_specs=[part(0), pl.BlockSpec((1, group, extent), lambda i: (i + base, 0, 0))],
        out_shape=[
            jax.ShapeDtypeStruct((HEADS * HEAD, extent), BF),
            jax.ShapeDtypeStruct((groups, group, extent), F32),
        ],
        input_output_aliases={4 + n: n for n in range(len(earlier))},
        scratch_shapes=[
            pltpu.VMEM((group, HEAD + 16, extent), BF),
            pltpu.VMEM((group, HEAD + 16, extent), BF),
            pltpu.VMEM((block // 2, block), F32),
        ],
        compiler_params=params(),
        cost_estimate=estimate(weight * 16 * HEADS * pairs * HEAD / part_of[1], weight * 8e6),
        name="attention",
    )(lengths, project, project, project, *earlier)


def gelu_parts(hidden):
    chance = 0.5 + 0.5 * lax.erf(hidden * 0.7071067811865476)
    density = jnp.exp2(hidden * hidden * (-0.5 * LOG2E)) * 0.3989422804014327
    return hidden * chance, chance + hidden * density


def out_kernel(
    count, tab, lengths, mixture, frames, cotangent, out_bias, gain, shift, *rest
):
    pieces = rest[:count]
    middle, normed, result, down_bias, out_weight, sems = rest[count:]
    step = pl.program_id(0)
    model = mixture.shape[0]

    size = frames.shape[0]

    def fetch():
        return load_all(pieces, tab, out_weight, sems, model // 4, TILE)

    @pl.when(step == 0)
    def _():
        start(fetch())
        down_bias[...] = jnp.zeros_like(down_bias)

    def mask(rows, sums):
        place = step * size + rows.start + lax.broadcasted_iota(jnp.int32, (ROWS, 1), 0)
        masked = jnp.where(place < lengths[0], cotangent[rows, :].astype(F32), 0.0)
        result[rows, :] = masked.astype(BF)
        return sums + masked.sum(0, keepdims=True)

    down_bias[...] += chunks(size, ROWS, mask, jnp.zeros((1, model), F32))

    @pl.when(step == 0)
    def _():
        wait(fetch())

    def branch(rows, carry):
        total = dot(mixture[:, rows], out_weight[...], 0, 0) + out_bias[...]
        total = frames[rows, :].astype(F32) + total
        middle[rows, :] = total
        unit, _ = normalise(total)
        normed[rows, :] = (unit * gain[...] + shift[...]).astype(BF)
        return carry

    chunks(size, ROWS, branch)


def out_call(tab, lengths, mixture, frames, cotangent, vectors, pieces):
    model, extent = mixture.shape
    size = min(512, extent)
    block = pl.BlockSpec((size, model), lambda i: (i, 0))
    return pl.pallas_call(
        functools.partial(out_kernel, len(pieces)),
        grid=(extent // size,),
        in_specs=[SMEM, SMEM]
        + [pl.BlockSpec((model, size), lambda i: (0, i)), block, block]
        + [whole(1, model)] * 3
        + [ANY] * len(pieces),
        out_specs=[block, block, block, whole(1, model)],
        out_shape=[
            jax.ShapeDtypeStruct((extent, model), F32),
            jax.ShapeDtypeStruct((extent, model), BF),
            jax.ShapeDtypeStruct((extent, model), BF),
            vec(model),
        ],
        scratch_shapes=[pltpu.VMEM((model, model), BF), pltpu.SemaphoreType.DMA((32,))],
        compiler_params=params(),
        cost_estimate=estimate(1, 1),
        name="out",
    )(tab, lengths, mixture, frames, cotangent, *vectors, *pieces)


def up_kernel(counts, base, tab, normed, result, up_bias, *rest):
    count_up, count_earlier, count_grad = counts
    up_pieces, rest = rest[:count_up], rest[count_up + count_earlier :]
    active, slope = rest[:2]
    grads, rest = rest[2 : 2 + count_grad], rest[2 + count_grad :]
    weight, staged, graded, sems_up, sems_grad, sem_in = rest
    step = pl.program_id(0)
    steps = pl.num_programs(0)
    extent = normed.shape[0]

    def late():
        return pltpu.make_async_copy(result, graded, sem_in)

    def fetch(index):
        slot = lax.rem(index, 2)
        return load_columns(
            up_pieces, tab, base + index, weight.at[slot], sems_up.at[slot], TILE
        )

    def send(index):
        slot = lax.rem(index, 2)
        return store_row_pair(grads, tab, base + index, staged.at[slot], sems_grad.at[slot])

    @pl.when(step == 0)
    def _():
        start(fetch(step))
        late().start()

    @pl.when(step + 1 < steps)
    def _():
        start(fetch(step + 1))

    wait(fetch(step))
    now = lax.rem(step, 2)

    def widen(rows, carry):
        hidden = dot(normed[rows, :], weight[now], 1, 0) + up_bias[...]
        value, grade = gelu_parts(hidden)
        active[rows, :] = value.astype(BF)
        slope[rows, :] = grade.astype(BF)
        return carry

    chunks(extent, ROWS, widen)

    @pl.when(step == 0)
    def _():
        late().wait()

    @pl.when(step >= 2)
    def _():
        wait(send(step - 2))

    def weigh(columns, carry):
        staged[now, columns, :] = dot(active[:, columns], graded[...], 0, 0).astype(BF)
        return carry

    chunks(TILE, ROWS, weigh)
    start(send(step))

    @pl.when(step == steps - 1)
    def _():
        wait(send(step - 1))
        wait(send(step))


def up_call(
    tab, normed, result, up_bias, up_pieces, spread, sizes, part_of=(0, 1), earlier=(), weight=1.0
):
    extent, model = normed.shape
    hidden = 4 * model
    grads = gradient_shapes(spread, hidden, model, *sizes)
    steps = hidden // TILE // part_of[1]
    base = steps * part_of[0]
    tile = pl.BlockSpec((extent, TILE), lambda i: (0, base + i))
    aliases = {4 + len(up_pieces) + n: n for n in range(len(earlier))}
    return pl.pallas_call(
        functools.partial(up_kernel, (len(up_pieces), len(earlier), len(grads)), base),
        grid=(steps,),
        in_specs=[SMEM, whole(extent, model), ANY]
        + [pl.BlockSpec((1, TILE), lambda i: (0, base + i))]
        + [ANY] * (len(up_pieces) + len(earlier)),
        out_specs=[tile, tile] + [ANY] * len(grads),
        out_shape=[
            jax.ShapeDtypeStruct((extent, hidden), BF),
            jax.ShapeDtypeStruct((extent, hidden), BF),
        ]
        + grads,
        input_output_aliases=aliases,
        scratch_shapes=[
            pltpu.VMEM((2, model, TILE), BF),
            pltpu.VMEM((2, TILE, model), BF),
            pltpu.VMEM((extent, model), BF),
            pltpu.SemaphoreType.DMA((2, 8)),
            pltpu.SemaphoreType.DMA((2, 8)),
            pltpu.SemaphoreType.DMA,
        ],
        compiler_params=params(),
        cost_estimate=estimate(weight * 16 * extent * model * model / part_of[1], weight * 50e6),
        name="up",
    )(tab, normed, result, up_bias, *up_pieces, *earlier)


def back_kernel(counts, tab, mixture, middle, normed, d_result, slope, *rest):
    count_out, count_up, count_down, count_grad = counts
    gain = rest[0]
    rest = rest[1:]
    out_pieces, rest = rest[:count_out], rest[count_out:]
    up_pieces, rest = rest[:count_up], rest[count_up:]
    down_pieces, rest = rest[:count_down], rest[count_down:]
    d_middle, d_mixture, up_bias, gain_grad, shift_grad, out_bias = rest[:6]
    rest = rest[6:]
    grads, rest = rest[:count_grad], rest[count_grad:]
    (
        mixed,
        out_weight,
        total,
        unit_rows,
        result,
        down,
        up,
        d_hidden,
        d_normed,
        staged,
        sems_in,
        sems_out,
        sems_down,
        sems_up,
        sems_grad,
    ) = rest
    spread = len(grads[0].shape) == 4
    if spread:
        up_grads = out_grads = grads
    else:
        up_grads, out_grads = grads[:1], grads[1:]
    step = pl.program_id(0)
    steps = pl.num_programs(0)
    extent, model = result.shape
    width = model // 4

    def fetch(index):
        slot = index % 2
        return load_rows(down_pieces, tab, index, down.at[slot], sems_down.at[slot])

    def fetch_up(index):
        slot = index % 2
        block = tab[T_PAIR + index]
        return load_columns(up_pieces, tab, block, up.at[slot], sems_up.at[slot], TILE)

    def send(index):
        slot = index % 2
        block = tab[T_PAIR + index]
        return store_column_block(
            up_grads, tab, block, staged.at[slot], sems_grad.at[slot], TILE
        )

    def send_out(block):
        return store_column_block(
            out_grads,
            tab,
            block,
            staged.at[0, :, pl.ds(block * width, width)],
            sems_out.at[pl.ds(block * 8, 8)],
            width,
            TILE if spread else 0,
        )

    def early(n):
        pair = ((d_result, result), (normed, unit_rows))[n]
        return pltpu.make_async_copy(*pair, sems_in.at[n])

    def late():
        return [
            pltpu.make_async_copy(middle, total, sems_in.at[2]),
            pltpu.make_async_copy(mixture, mixed, sems_in.at[3]),
        ] + load_all(out_pieces, tab, out_weight, sems_out, width, TILE)

    now = lax.rem(step, 2)

    @pl.when(step == 0)
    def _():
        early(0).start()
        start(fetch(0))
        early(1).start()
        start(fetch_up(0))
        early(0).wait()
        d_normed[...] = jnp.zeros_like(d_normed)

    def arrive(index):
        if index == 2:
            start(late())
        if index + 1 < 4:
            start(fetch(index + 1))
            start(fetch_up(index + 1))
        wait(fetch(index))
        if index >= 2:
            wait(send(index - 2))

    for index in range(4):
        pl.when(step == index)(functools.partial(arrive, index))

    def shrink(rows, sums):
        d_active = dot(result[rows, :], down[now], 1, 1)
        piece = (d_active * slope[rows, :].astype(F32)).astype(BF)
        d_hidden[rows, :] = piece
        return sums + piece.astype(F32).sum(0, keepdims=True)

    up_bias[...] = chunks(extent, ROWS, shrink, jnp.zeros((1, TILE), F32))

    @pl.when(step == 0)
    def _():
        early(1).wait()

    def weigh(columns, carry):
        staged[now, columns, :] = dot(unit_rows[:, columns], d_hidden[...], 0, 0).astype(BF)
        return carry

    chunks(model, ROWS, weigh)
    def leave(index):
        start(send(index))
        wait(fetch_up(index))

    for index in range(4):
        pl.when(step == index)(functools.partial(leave, index))

    def widen(rows, carry):
        d_normed[rows, :] += dot(d_hidden[rows, :], up[now], 1, 1)
        return carry

    @pl.when(step < steps - 1)
    def _():
        chunks(extent, ROWS, widen)

    @pl.when(step == steps - 1)
    def _():
        wait(late())
        none = jnp.zeros((1, model), F32)

        def norm(rows, sums):
            grade = d_normed[rows, :] + dot(d_hidden[rows, :], up[now], 1, 1)
            unit, scale = normalise(total[rows, :])
            gains = sums[0] + (grade * unit).sum(0, keepdims=True)
            shifts = sums[1] + grade.sum(0, keepdims=True)
            grade = grade * gain[...]
            level = jnp.mean(grade, axis=-1, keepdims=True)
            tilt = jnp.mean(grade * unit, axis=-1, keepdims=True)
            d_total = result[rows, :].astype(F32) + scale * (grade - level - unit * tilt)
            d_middle[rows, :] = d_total
            branch = d_total.astype(BF)
            unit_rows[rows, :] = branch
            return gains, shifts, sums[2] + branch.astype(F32).sum(0, keepdims=True)

        sums = chunks(extent, ROWS, norm, (none, none, none))
        gain_grad[...], shift_grad[...], out_bias[...] = sums
        wait(send(2))

        def weigh_out(rows, carry):
            staged[0, rows, :] = dot(mixed[rows, :], unit_rows[...], 1, 0).astype(BF)
            return carry

        chunks(model, ROWS, weigh_out)
        for block in range(4):
            start(send_out(block))

        def turn(rows, carry):
            d_mixture[rows, :] = dot(out_weight[rows, :], unit_rows[...], 1, 1).astype(BF)
            return carry

        chunks(model, ROWS, turn)
        wait(send(3))
        for block in range(4):
            wait(send_out(block))


def back_call(tab, mixture, middle, normed, d_result, slope, gain, pieces, spread, sizes):
    out_pieces, up_pieces, down_pieces = pieces
    model, extent = mixture.shape
    hidden = slope.shape[1]
    if spread:
        grads = gradient_shapes(spread, model, hidden + model, *sizes)
    else:
        grads = gradient_shapes(spread, model, hidden, *sizes)
        grads += gradient_shapes(spread, model, model, *sizes)
    steps = hidden // TILE
    grid = pltpu.PrefetchScalarGridSpec(
        num_scalar_prefetch=1,
        grid=(steps,),
        in_specs=[ANY, ANY, ANY, ANY]
        + [pl.BlockSpec((extent, TILE), lambda i, tab: (0, tab[T_PAIR + i]))]
        + [whole(1, model)]
        + [ANY] * (len(out_pieces) + len(up_pieces) + len(down_pieces)),
        out_specs=[
            whole(extent, model),
            whole(model, extent),
            pl.BlockSpec((1, TILE), lambda i, tab: (0, tab[T_PAIR + i])),
            whole(1, model),
            whole(1, model),
            whole(1, model),
        ]
        + [ANY] * len(grads),
        scratch_shapes=[
            pltpu.VMEM((model, extent), BF),
            pltpu.VMEM((model, model), BF),
            pltpu.VMEM((extent, model), F32),
            pltpu.VMEM((extent, model), BF),
            pltpu.VMEM((extent, model), BF),
            pltpu.VMEM((2, TILE, model), BF),
            pltpu.VMEM((2, model, TILE), BF),
            pltpu.VMEM((extent, TILE), BF),
            pltpu.VMEM((extent, model), F32),
            pltpu.VMEM((2, model, TILE), BF),
            pltpu.SemaphoreType.DMA((4,)),
            pltpu.SemaphoreType.DMA((32,)),
            pltpu.SemaphoreType.DMA((2, 8)),
            pltpu.SemaphoreType.DMA((2, 8)),
            pltpu.SemaphoreType.DMA((2, 8)),
        ],
    )
    return pl.pallas_call(
        functools.partial(
            back_kernel, (len(out_pieces), len(up_pieces), len(down_pieces), len(grads))
        ),
        grid_spec=grid,
        out_shape=[
            jax.ShapeDtypeStruct((extent, model), F32),
            jax.ShapeDtypeStruct((model, extent), BF),
            vec(hidden),
            vec(model),
            vec(model),
            vec(model),
        ]
        + grads,
        compiler_params=params(),
        cost_estimate=estimate(28 * extent * model * model, 60e6),
        name="back",
    )(
        tab,
        mixture,
        middle,
        normed,
        d_result,
        slope,
        gain,
        *out_pieces,
        *up_pieces,
        *down_pieces,
    )


def attention_back_kernel(
    group,
    block,
    lengths,
    query,
    key,
    value,
    mixture,
    d_mixture,
    totals,
    *rest,
):
    d_project, keys, queries, causal, d_keys, d_values = rest[-6:]
    extent = query.shape[1]

    @pl.when(pl.program_id(0) == 0)
    def _():
        causal[...] = causal_bias(block, block)

    key_rows, query_rows = extend_rows(lengths[0], extent)
    for head in range(group):
        part = pl.ds(HEAD * head, HEAD)
        keys[head, :HEAD, :] = key[part, :]
        keys[head, HEAD:, :] = key_rows
        queries[head, :HEAD, :] = query[part, :]
        queries[head, HEAD:, :] = query_rows
    for head in range(group):
        part = pl.ds(HEAD * head, HEAD)
        for tile in range(extent // block):
            place = pl.ds(tile * block, block)
            own = queries[head, :, place]
            grade = d_mixture[part, place]
            center = (grade.astype(F32) * mixture[part, place].astype(F32)).sum(0, keepdims=True)
            total = totals[0, pl.ds(head, 1), place]
            d_query = jnp.zeros((HEAD, block), F32)
            for other in range(tile + 1):
                span = pl.ds(other * block, block)
                score = dot(keys[head, :, span], own, 0, 0)
                if other == tile:
                    score = score + causal[...]
                weight = jnp.exp2(score * (SCALE * LOG2E) - total)
                d_weight = dot(value[part, span], grade, 0, 0)
                d_score = (weight * (d_weight - center)).astype(BF)
                d_value = dot(grade, weight.astype(BF), 1, 1)
                d_key = dot(query[part, place], d_score, 1, 1)
                d_query = d_query + dot(key[part, span], d_score, 1, 0)
                if other == tile:
                    d_values[:, span] = d_value
                    d_keys[:, span] = d_key
                else:
                    d_values[:, span] += d_value
                    d_keys[:, span] += d_key
            d_project[0, part, place] = (d_query * SCALE).astype(BF)
        d_project[1, part, :] = (d_keys[...] * SCALE).astype(BF)
        d_project[2, part, :] = d_values[...].astype(BF)


def attention_back_call(
    lengths, project, mixture, d_mixture, totals, base=0, ending=HEADS // 2, earlier=()
):
    extent = project.shape[1]
    group, block = 2, min(512, extent)
    size, groups = HEAD * group, HEADS // group
    steps = ending - base

    def part(section):
        return pl.BlockSpec((size, extent), lambda i: (i + base + section * groups, 0))

    pairs = extent * extent * 5 // 8
    return pl.pallas_call(
        functools.partial(attention_back_kernel, group, block),
        grid=(steps,),
        in_specs=[SMEM, part(0), part(1), part(2), part(0), part(0)]
        + [pl.BlockSpec((1, group, extent), lambda i: (i + base, 0, 0))]
        + [ANY] * len(earlier),
        out_specs=pl.BlockSpec((3, size, extent), lambda i: (0, i + base, 0)),
        out_shape=jax.ShapeDtypeStruct((3, HEADS * HEAD, extent), BF),
        input_output_aliases={7: 0} if earlier else {},
        scratch_shapes=[
            pltpu.VMEM((group, HEAD + 16, extent), BF),
            pltpu.VMEM((group, HEAD + 16, extent), BF),
            pltpu.VMEM((block, block), F32),
            pltpu.VMEM((HEAD, extent), F32),
            pltpu.VMEM((HEAD, extent), F32),
        ],
        compiler_params=params(),
        cost_estimate=estimate(4 * HEADS * pairs * HEAD * steps / groups, 1e6),
        name="attention_back",
    )(lengths, project, project, project, mixture, d_mixture, totals, *earlier)


def attend_grad_kernel(count_grad, tab, d_project, normed, *rest):
    bias_grad = rest[0]
    grads, rest = rest[1 : 1 + count_grad], rest[1 + count_grad :]
    staged, sems_grad = rest
    step = pl.program_id(0)
    steps = pl.num_programs(0)
    extent, model = normed.shape
    width = d_project.shape[0]

    def send(block):
        slot = lax.rem(block, 2)
        return store_column_block(grads, tab, block, staged.at[slot], sems_grad.at[slot], width)

    @pl.when(step >= 2)
    def _():
        wait(send(step - 2))

    now = lax.rem(step, 2)

    def weigh(columns, carry):
        staged[now, columns, :] = dot(normed[:, columns], d_project[...], 0, 1).astype(BF)
        return carry

    chunks(model, ROWS, weigh)
    start(send(step))
    sums = d_project[...].astype(F32).sum(1, keepdims=True)
    bias_grad[...] = jnp.transpose(jnp.broadcast_to(sums, (width, 128)))[:1, :]

    @pl.when(step == steps - 1)
    def _():
        wait(send(step - 1))
        wait(send(step))


def attend_grad_call(tab, d_project, normed, spread, sizes):
    extent, model = normed.shape
    width = 3 * model // 4
    grads = gradient_shapes(spread, model, 3 * model, *sizes)
    return pl.pallas_call(
        functools.partial(attend_grad_kernel, len(grads)),
        grid=(4,),
        in_specs=[SMEM, pl.BlockSpec((width, extent), lambda i: (i, 0)), whole(extent, model)],
        out_specs=[pl.BlockSpec((1, width), lambda i: (0, i))] + [ANY] * len(grads),
        out_shape=[vec(3 * model)] + grads,
        scratch_shapes=[
            pltpu.VMEM((2, model, width), BF),
            pltpu.SemaphoreType.DMA((2, 8)),
        ],
        compiler_params=params(),
        cost_estimate=estimate(6 * extent * model * model, 14e6),
        name="attend_grad",
    )(tab, d_project, normed)


def first_kernel(count_in, tab, d_project, frames, d_middle, gain, *rest):
    pieces, rest = rest[:count_in], rest[count_in:]
    bias_grad, *early = rest[:6]
    d_frames, small, weight, total, d_normed, sems, sem_total = rest[6:]
    step = pl.program_id(0)
    steps = pl.num_programs(0)
    extent, model = frames.shape
    width = d_project.shape[0]

    def fetch(index):
        slot = index % 2
        return load_slot(pieces, tab, index, weight.at[slot], sems.at[slot], width)

    def late():
        return pltpu.make_async_copy(d_middle, total, sem_total)

    @pl.when(step == 0)
    def _():
        start(fetch(0))
        late().start()
        d_normed[...] = jnp.zeros_like(d_normed)

    def arrive(index):
        if index + 1 < 4:
            start(fetch(index + 1))
        wait(fetch(index))

    for index in range(4):
        pl.when(step == index)(functools.partial(arrive, index))
    now = lax.rem(step, 2)

    def widen(rows, carry):
        d_normed[rows, :] += dot(d_project[:, rows], weight[now], 0, 1)
        return carry

    @pl.when(step < steps - 1)
    def _():
        chunks(extent, ROWS, widen)

    @pl.when(step == steps - 1)
    def _():
        late().wait()
        none = jnp.zeros((1, model), F32)

        def norm(rows, sums):
            grade = d_normed[rows, :] + dot(d_project[:, rows], weight[now], 0, 1)
            unit, scale = normalise(frames[rows, :].astype(F32))
            gains = sums[0] + (grade * unit).sum(0, keepdims=True)
            shifts = sums[1] + grade.sum(0, keepdims=True)
            grade = grade * gain[...]
            level = jnp.mean(grade, axis=-1, keepdims=True)
            tilt = jnp.mean(grade * unit, axis=-1, keepdims=True)
            d_frames[rows, :] = (total[rows, :] + scale * (grade - level - unit * tilt)).astype(BF)
            return gains, shifts

        gains, shifts = chunks(extent, ROWS, norm, (none, none))
        bias = bias_grad[...]
        vectors = [gains, shifts, bias[:, :model], bias[:, 2 * model :]]
        vectors += [vector[...] for vector in early]
        place = 0
        for vector in vectors:
            for column in range(0, vector.shape[1], 128):
                small[place : place + 1, :] = vector[:, column : column + 128]
                place += 1


def small_kernel(*refs):
    *terms, a, b, c, d, e, f, g, h = refs
    terms = [term[...] for term in terms]
    total = tree_sum(terms)
    place = 0
    for out in (a, b, c, d, e, f, g, h):
        if out.shape[1] == 128:
            out[...] = total[place : place + out.shape[0], :]
            place += out.shape[0]
            continue
        for row in range(out.shape[0]):
            for column in range(0, out.shape[1], 128):
                out[row : row + 1, column : column + 128] = total[place : place + 1, :]
                place += 1


def small_call(terms):
    unit = terms[0].shape[0] // 12
    sizes = [unit, unit, 2 * unit, unit, unit, unit, unit, 4 * unit]
    return pl.pallas_call(
        small_kernel,
        out_shape=[
            jax.ShapeDtypeStruct((size, 128) if n != 2 else (2, size * 64), F32)
            for n, size in enumerate(sizes)
        ],
        name="small",
    )(*terms)


def first_call(tab, d_project, frames, d_middle, gain, pieces, vectors):
    extent, model = frames.shape
    width = 3 * model // 4
    count = model + sum(vector.shape[1] for vector in vectors)
    grid = pltpu.PrefetchScalarGridSpec(
        num_scalar_prefetch=1,
        grid=(4,),
        in_specs=[pl.BlockSpec((width, extent), lambda i, tab: (tab[T_COL + i], 0))]
        + [whole(extent, model), ANY, whole(1, model)]
        + [ANY] * len(pieces)
        + [whole(*vector.shape) for vector in vectors],
        out_specs=[whole(extent, model), whole(count // 128, 128)],
        scratch_shapes=[
            pltpu.VMEM((2, model, width), BF),
            pltpu.VMEM((extent, model), F32),
            pltpu.VMEM((extent, model), F32),
            pltpu.SemaphoreType.DMA((2, 8)),
            pltpu.SemaphoreType.DMA,
        ],
    )
    return pl.pallas_call(
        functools.partial(first_kernel, len(pieces)),
        grid_spec=grid,
        out_shape=[
            jax.ShapeDtypeStruct((extent, model), BF),
            jax.ShapeDtypeStruct((count // 128, 128), F32),
        ],
        compiler_params=params(),
        cost_estimate=estimate(6 * extent * model * model, 24e6),
        name="first",
    )(tab, d_project, frames, d_middle, gain, *pieces, *vectors)


def down_kernel(count, count_earlier, row, tab, active, middle, bias, *rest):
    pieces = rest[:count]
    frames_out, weight, total, base, sems, sem_base = rest[count + count_earlier :]
    step = pl.program_id(0)
    steps = pl.num_programs(0)
    extent = total.shape[0]

    def fetch(index):
        slot = index % 2
        return load_rows(pieces, tab, index, weight.at[slot], sems.at[slot])

    def late():
        return pltpu.make_async_copy(middle.at[pl.ds(row * extent, extent), :], base, sem_base)

    def arrive(index):
        if index == 0:
            start(fetch(index))
            late().start()
        if index + 1 < 4:
            start(fetch(index + 1))
        wait(fetch(index))

    for index in range(4):
        pl.when(step == index)(functools.partial(arrive, index))
    now = lax.rem(step, 2)

    @pl.when(step < steps - 1)
    def _():
        def widen(rows, carry):
            before = jnp.where(step == 0, 0.0, total[rows, :])
            total[rows, :] = before + dot(active[rows, :], weight[now], 1, 0)
            return carry

        chunks(extent, ROWS, widen)

    @pl.when(step == steps - 1)
    def _():
        late().wait()

        def finish(rows, carry):
            result = total[rows, :] + dot(active[rows, :], weight[now], 1, 0)
            frames_out[rows, :] = (result + (base[rows, :] + bias[...])).astype(BF)
            return carry

        chunks(extent, ROWS, finish)


def down_call(tab, active, middle, bias, pieces, part_of=(0, 1), earlier=()):
    extent, hidden = active.shape
    model = middle.shape[1]
    row, size = part_of[0], extent // part_of[1]
    grid = pltpu.PrefetchScalarGridSpec(
        num_scalar_prefetch=1,
        grid=(hidden // TILE,),
        in_specs=[pl.BlockSpec((size, TILE), lambda i, tab: (row, tab[T_PAIR + i]))]
        + [ANY, whole(1, model)]
        + [ANY] * (len(pieces) + len(earlier)),
        out_specs=pl.BlockSpec((size, model), lambda i, tab: (row, 0)),
        scratch_shapes=[
            pltpu.VMEM((2, TILE, model), BF),
            pltpu.VMEM((size, model), F32),
            pltpu.VMEM((size, model), F32),
            pltpu.SemaphoreType.DMA((2, 8)),
            pltpu.SemaphoreType.DMA,
        ],
    )
    return pl.pallas_call(
        functools.partial(down_kernel, len(pieces), len(earlier), row),
        grid_spec=grid,
        out_shape=jax.ShapeDtypeStruct((extent, model), BF),
        input_output_aliases={4 + len(pieces): 0} if earlier else {},
        compiler_params=params(),
        cost_estimate=estimate(8 * size * model * model, 24e6),
        name="down",
    )(tab, active, middle, bias, *pieces, *earlier)


def gather_plain(weight):
    wide = lax.all_gather(weight, "inner", axis=1, tiled=True)
    return [lax.all_gather(wide, "dp", axis=0, tiled=True)]


def scatter_plain(grads):
    wide = lax.psum_scatter(grads[0], "dp", scatter_dimension=0, tiled=True)
    return lax.psum_scatter(wide, "inner", scatter_dimension=1, tiled=True).astype(F32)


CORE, NEAR, FAR = 0, 1, 2


def swap(value, way):
    flips = {CORE: (1, 1), NEAR: (2, 4), FAR: (4, 2)}[way]
    return lax.ppermute(value, "dp", [(d, d ^ flips[d & 1]) for d in range(8)])


def shift(value, amount):
    return lax.ppermute(value, "inner", [(i, (i + amount) & 3) for i in range(4)])


def after(value, *done):
    return lax.optimization_barrier((value, done))[0]


def stack_spread(block):
    return jnp.stack([block] + [shift(block, amount) for amount in (1, 2, 3)])


def added(*values):
    total = values[0].astype(F32)
    for value in values[1:]:
        total = total + value.astype(F32)
    return total


def add_kernel(count, *refs):
    total = added(*[ref[...] for ref in refs[:count]])
    outs = refs[count:]
    if len(outs) == 1:
        outs[0][...] = total.reshape(outs[0].shape).astype(BF)
        return
    for index, out in enumerate(outs):

        @pl.when(pl.program_id(0) == index)
        def _(out=out):
            out[...] = total.reshape(out.shape).astype(out.dtype)


def add_call(terms, outs, grid):
    rows, columns = terms[0][0].shape[-2:]
    specs = []
    for term, place in terms:
        if term.ndim == 3:
            specs.append(pl.BlockSpec((1, rows, columns), lambda *at: (at[-1], 0, 0)))
        elif place is None:
            specs.append(pl.BlockSpec((1, 1, rows, columns), lambda p, k: (p, k, 0, 0)))
        else:
            specs.append(
                pl.BlockSpec((1, 1, rows, columns), lambda k, place=place: (place, k, 0, 0))
            )
    if len(outs) == 1:
        lead = (1,) * len(grid)
        out_specs = [pl.BlockSpec(lead + (rows, columns), lambda *at: at + (0, 0))]
    else:
        out_specs = [whole(rows, columns)] * len(outs)

    def kernel(*refs):
        ins = [
            ref.at[0] if len(ref.shape) == 3 else ref.at[0, 0] for ref in refs[: len(terms)]
        ]
        add_kernel(len(terms), *ins, *refs[len(terms) :])

    return pl.pallas_call(
        kernel,
        grid=grid,
        in_specs=specs,
        out_specs=out_specs,
        out_shape=outs,
        compiler_params=params(),
        cost_estimate=estimate(1e10, 1e7),
        name="add",
    )(*[term for term, _ in terms])


def add_first(keep, core):
    return added(keep[:2], core[:2]).astype(BF)


def add_second(keep, core, link):
    return added(keep[2], core[2], link[0]).astype(BF)


def add_third(keep, core, link, last):
    blocks = [added(keep[3, k], core[3, k], link[1, k], last[k]) for k in range(4)]
    return [blocks[0]] + [block.astype(BF) for block in blocks[1:]]


def add_third_kernel(keep, core, link, last):
    shapes = [jax.ShapeDtypeStruct(keep.shape[2:], F32)]
    shapes += [jax.ShapeDtypeStruct(keep.shape[2:], BF)] * 3
    return add_call([(keep, 3), (core, 3), (link, 1), (last, None)], shapes, (4,))


def shift_parts(parts):
    return [shift(parts[k], k) for k in (1, 2, 3)]


def exchange(values, axis, size):
    return [values] + [
        lax.ppermute(values, axis, [(i, i ^ flip) for i in range(size)])
        for flip in range(1, size)
    ]


def tree_sum(terms):
    while len(terms) > 1:
        terms = [terms[i] + terms[i + 1] for i in range(0, len(terms), 2)]
    return terms[0]


def shards(
    spread,
    sizes,
    frames_in,
    lengths,
    first_gain,
    first_shift,
    attend_weight,
    attend_bias,
    output_weight,
    output_bias,
    second_gain,
    second_shift,
    up_weight,
    up_bias,
    down_weight,
    down_bias,
    cotangent,
):
    _, extent, model = frames_in.shape
    frames = frames_in.reshape(extent, model)
    upstream = cotangent.reshape(extent, model)
    tab = make_table(spread, True)
    tab_plain = make_table(spread, False)

    def row(vector):
        return vector.reshape(1, -1)

    if not spread:
        attend_pieces = gather_plain(attend_weight)
        out_pieces = gather_plain(output_weight)
        up_pieces = gather_plain(up_weight)
        down_pieces = gather_plain(down_weight)
    else:
        others = [shift(attend_weight, amount) for amount in (1, 2, 3)]
        up_block = jnp.concatenate([up_weight, output_weight], axis=1)
        near, far = swap(attend_weight, NEAR), swap(attend_weight, FAR)
        others = jnp.stack(others)
        far, near = after((far, near), near, far)
        diagonal = swap(near, FAR)
        attend_pieces = [attend_weight, near, far, diagonal]
        attend_pieces += [swap(piece, CORE) for piece in attend_pieces]
        others = after(others, diagonal)
        near, far = swap(others, NEAR), swap(others, FAR)
        up_block = after(up_block, others)
        up_own = lax.all_gather(up_block, "inner")
        near, far = after((near, far), near, far)
        diagonal = swap(near, FAR)
        others = [others, near, far, diagonal]
        attend_pieces += others + [swap(piece, CORE) for piece in others]
        up_own = after(up_own, *attend_pieces)
        up_near, up_far = swap(up_own, NEAR), swap(up_own, FAR)
        down_own = lax.all_gather(after(down_weight, up_own), "inner")
    bias_row = jnp.concatenate([attend_bias[0], jnp.zeros_like(attend_bias[0]), attend_bias[1]])
    vectors = (row(first_gain), row(first_shift), row(bias_row))
    tokens = after(frames, up_own) if spread else frames
    normed, project = project_call(tab, tokens, *vectors, attend_pieces)
    if spread:
        mixture, totals = attention_call(lengths, after(project, up_own), (0, 2))
        up_near, up_far = after((up_near, up_far), totals)
        up_diagonal = swap(up_near, FAR)
        ahead = [swap(piece, CORE) for piece in (after(up_own, totals), up_near, up_far)]
        mixture, totals = attention_call(
            lengths, after(project, up_near, up_far, down_own), (1, 2), (mixture, totals)
        )
        up_pieces = [up_own, up_near, up_far, up_diagonal]
        up_pieces += ahead + [swap(after(up_diagonal, totals), CORE)]
        out_pieces = up_pieces
    else:
        mixture, totals = attention_call(lengths, project)
    vectors = (row(output_bias), row(second_gain), row(second_shift))
    if spread:
        down_near, down_far = swap(down_own, NEAR), swap(down_own, FAR)
    middle, normed_two, d_result, grad_down_bias = out_call(
        tab_plain, lengths, mixture, frames, upstream, vectors, out_pieces
    )
    if spread:
        *halves, half_grad = up_call(
            tab_plain,
            normed_two,
            d_result,
            row(up_bias),
            up_pieces,
            False,
            sizes,
            (0, 2),
        )
        down_near, down_far = after((down_near, down_far), halves)
        down_diagonal = swap(down_near, FAR)
        ahead = [swap(piece, CORE) for piece in (after(down_own, totals), down_near, down_far)]
        active, slope, *down_grads = up_call(
            tab_plain,
            after(normed_two, down_near, down_far),
            d_result,
            row(up_bias),
            up_pieces,
            False,
            sizes,
            (1, 2),
            (*halves, half_grad),
        )
    else:
        active, slope, *down_grads = up_call(
            tab_plain, normed_two, d_result, row(up_bias), up_pieces, False, sizes
        )
    if spread:
        down_pieces = [down_own, down_near, down_far, down_diagonal]
        down_pieces += ahead + [swap(after(down_diagonal, slope), CORE)]
        down_wide = lax.psum_scatter(down_grads[0], "dp", scatter_dimension=0, tiled=True)
    else:
        down_owned = scatter_plain(down_grads)
    (
        d_middle,
        d_mixture,
        grad_up_bias,
        grad_second_gain,
        grad_second_shift,
        grad_output_bias,
        *back_grads,
    ) = back_call(
        tab_plain,
        mixture,
        middle,
        normed_two,
        d_result,
        slope,
        row(second_gain),
        (out_pieces, up_pieces, down_pieces),
        spread,
        sizes,
    )
    early = [grad_output_bias, grad_second_gain, grad_second_shift, grad_down_bias, grad_up_bias]
    if spread:
        back_keep, back_send = back_grads
        back_core = swap(back_send, CORE)
        d_project = attention_back_call(lengths, project, mixture, d_mixture, totals, 0, 2)
        back_core = after(back_core, d_project)
        back_first = add_first(back_keep, back_core)
        back_link = swap(back_first, FAR)
        d_mixture = after(d_mixture, back_first)
        d_project = attention_back_call(
            lengths, project, mixture, d_mixture, totals, 2, HEADS // 2, (d_project,)
        )
        back_link, down_wide = after((back_link, down_wide), d_project)
        down_owned = lax.psum_scatter(down_wide, "inner", scatter_dimension=1, tiled=True)
        back_second = add_second(back_keep, back_core, back_link)
        back_last = swap(back_second, NEAR)
        d_rows = after(d_project, back_second, down_wide).reshape(3 * model, extent)
        grad_bias, attend_keep, attend_send = attend_grad_call(tab, d_rows, normed, spread, sizes)
        attend_core = swap(attend_send, CORE)
        attend_first = add_first(attend_keep, attend_core)
        attend_link = swap(attend_first, FAR)
        back_last = after(back_last, grad_bias, attend_first)
        back_parts = add_third_kernel(back_keep, back_core, back_link, back_last)
        back_others = shift_parts(back_parts)
        d_frames, small = first_call(
            tab,
            after(d_rows, attend_first, back_parts),
            frames,
            d_middle,
            row(first_gain),
            attend_pieces,
            [grad_bias] + early,
        )
        attend_link, down_owned = after((attend_link, down_owned), d_frames)
        attend_second = add_second(attend_keep, attend_core, attend_link)
        attend_last = swap(attend_second, NEAR)
        small_terms = exchange(small, "inner", 4)
        active, middle = after((active, middle), attend_second, down_owned)
        frames_out = down_call(tab_plain, active, middle, row(down_bias), down_pieces)
        attend_last, back_others, small_terms = after(
            (attend_last, back_others, small_terms), frames_out
        )
        back_owned = added(back_parts[0], *back_others)
        small = tree_sum(small_terms)
        attend_parts = add_third(attend_keep, attend_core, attend_link, attend_last)
        attend_parts, small = after((attend_parts, small), back_owned, small, attend_parts)
        others = shift_parts(attend_parts)
        small = small + lax.ppermute(small, "dp", [(i, i ^ 1) for i in range(8)])
        small_terms = [small] + [
            lax.ppermute(small, "dp", [(i, i ^ flip) for i in range(8)]) for flip in (2, 4, 6)
        ]
        attend_owned = added(attend_parts[0], *others)
        small = small_call(after(small_terms, attend_owned))
        down_owned = down_owned.astype(F32)
        up_owned, output_owned = back_owned[:, :TILE], back_owned[:, TILE:]
    else:
        d_project = attention_back_call(lengths, project, mixture, d_mixture, totals)
        d_rows = d_project.reshape(3 * model, extent)
        grad_bias, *attend_grads = attend_grad_call(tab, d_rows, normed, spread, sizes)
        d_frames, small = first_call(
            tab,
            d_rows,
            frames,
            d_middle,
            row(first_gain),
            attend_pieces,
            [grad_bias] + early,
        )
        frames_out = down_call(tab_plain, active, middle, row(down_bias), down_pieces)
        up_owned = scatter_plain(back_grads[:1])
        output_owned = scatter_plain(back_grads[1:])
        attend_owned = scatter_plain(attend_grads)
        small = small_call([lax.psum(small, ("dp", "inner"))])
    small = [vector if n == 2 else vector.reshape(-1) for n, vector in enumerate(small)]

    return (
        frames_out.reshape(frames_in.shape),
        d_frames.reshape(frames_in.shape),
        small[0],
        small[1],
        attend_owned,
        small[2],
        output_owned,
        small[3],
        small[4],
        small[5],
        up_owned,
        small[7],
        down_owned,
        small[6],
    )


def solution(mesh):
    sizes = (mesh.shape["dp"], mesh.shape["inner"])
    spread = sizes == (8, 4)
    return jax.shard_map(
        functools.partial(shards, spread, sizes),
        mesh=mesh,
        in_specs=(
            P(("dp", "inner"), None, None),
            P(("dp", "inner")),
            P(),
            P(),
            P("dp", "inner"),
            P(),
            P("dp", "inner"),
            P(),
            P(),
            P(),
            P("dp", "inner"),
            P(),
            P("dp", "inner"),
            P(),
            P(("dp", "inner"), None, None),
        ),
        out_specs=(
            P(("dp", "inner"), None, None),
            P(("dp", "inner"), None, None),
            P(),
            P(),
            P("dp", "inner"),
            P(),
            P("dp", "inner"),
            P(),
            P(),
            P(),
            P("dp", "inner"),
            P(),
            P("dp", "inner"),
            P(),
        ),
        check_vma=False,
    )
```
